32 devices in a mesh: section: 2 (over core), shard: 4 (over z), replica: 4 (over y, x).
Axes of the slice: x: 2, y: 2, z: 4, core: 2. Of those that a mesh axis runs over, the one named last changes fastest.
Arguments:
- patches: bfloat16 [32, 197, 384], P(('shard', 'replica')), may hold values from -6 to 6
- live_slots: int32 [32], P(('shard', 'replica')), may hold values from 0 to 1, as said below
- cotangent: bfloat16 [32, 197, 384], P(('shard', 'replica')), may hold values from -6 to 6
- w_qkv: bfloat16 [2, 384, 1152], P('section', 'shard'), may hold values from -0.3125 to 0.3125
- w_out: bfloat16 [2, 384, 384], P('section', 'shard'), may hold values from -0.625 to 0.625
- w_up: bfloat16 [2, 384, 1536], P('section', 'shard'), may hold values from -0.3125 to 0.3125
- w_down: bfloat16 [2, 1536, 384], P('section', 'shard'), may hold values from -0.15625 to 0.15625
- bias_q: float32 [2, 384], P('section', 'shard'), may hold values from -1.5 to 1.5
- bias_v: float32 [2, 384], P('section', 'shard'), may hold values from -1.5 to 1.5
- bias_out: float32 [2, 384], P('section', 'shard'), may hold values from -1.5 to 1.5
- bias_up: float32 [2, 1536], P('section', 'shard'), may hold values from -1.5 to 1.5
- bias_down: float32 [2, 384], P('section', 'shard'), may hold values from -1.5 to 1.5
- gain_one: float32 [2, 384], P('section', 'shard'), may hold values from 0.5 to 1.5
- offset_one: float32 [2, 384], P('section', 'shard'), may hold values from -1.5 to 1.5
- gain_two: float32 [2, 384], P('section', 'shard'), may hold values from 0.5 to 1.5
- offset_two: float32 [2, 384], P('section', 'shard'), may hold values from -1.5 to 1.5
Outputs:
- layer_outputs: bfloat16 [2, 32, 197, 384], P('section', ('shard', 'replica'))
- input_grads: float32 [2, 32, 197, 384], P('section', ('shard', 'replica'))
- grad_w_qkv: float32 [2, 384, 1152], P('section', 'shard')
- grad_w_out: float32 [2, 384, 384], P('section', 'shard')
- grad_w_up: float32 [2, 384, 1536], P('section', 'shard')
- grad_w_down: float32 [2, 1536, 384], P('section', 'shard')
- grad_bias_q: float32 [2, 384], P('section', 'shard')
- grad_bias_v: float32 [2, 384], P('section', 'shard')
- grad_bias_out: float32 [2, 384], P('section', 'shard')
- grad_bias_up: float32 [2, 1536], P('section', 'shard')
- grad_bias_down: float32 [2, 384], P('section', 'shard')
- grad_gain_one: float32 [2, 384], P('section', 'shard')
- grad_offset_one: float32 [2, 384], P('section', 'shard')
- grad_gain_two: float32 [2, 384], P('section', 'shard')
- grad_offset_two: float32 [2, 384], P('section', 'shard')
The draws below stay inside these ranges and needn't reach their ends.
Inputs may be any that keep to these rules, and one draw needn't show every extreme that they name: `live_slots`: exactly 25 of the 32 slots hold an image.
All inputs are finite; a program needn't handle non-finite values.
Results may differ from the reference program's by a relative error of at most 0.04.
Values may be sent and summed in bfloat16 or wider, within the bound.
No kernel may reach another device: no remote copies, remote signals or barrier semaphores. Data moves between devices by JAX's collectives and lax.ppermute only.
A program may use at most 128 MiB of HBM per device.

```python
import jax
import jax.numpy as jnp
from jax import lax

D = 384
HEAD_DIM = 64
FF = 1536
SEQ = 197
SLOTS = 32
LIVE = 25


def draw_live_slots(key, part):
    key = jax.random.fold_in(key, 11)
    order = jax.random.permutation(key, SLOTS)
    return (order < LIVE).astype(jnp.int32)


def shard_levels(stream_key, shape, cuts, least, high):
    level, own = 1.0, jax.random.fold_in(stream_key, 6)
    for position, shards_of in cuts:
        draws = jnp.exp(jax.random.uniform(jax.random.fold_in(own, position), (shards_of,), jnp.float32, least / len(cuts), high / len(cuts)))
        level = level * jnp.repeat(draws, shape[position] // shards_of).reshape([-1 if axis == position else 1 for axis in range(len(shape))])
    return level


def scatter_about(own_key, shape, spread, limit, pieces=(), dtype=jnp.bfloat16):
    gain = shard_levels(own_key, shape, pieces, -0.22, 0.18) if pieces else 1.0
    drawn = jax.random.normal(own_key, shape, jnp.float32) * spread * gain
    return jnp.minimum(jnp.maximum(drawn, -limit), limit).astype(dtype)


def setup_inputs(seed: int = 0) -> dict:
    key_of = jax.random.split(jax.random.key(seed), 17)
    return {
        "patches": scatter_about(key_of[0], (SLOTS, SEQ, D), 1.0, 6.0, ((0, 16),)),
        "live_slots": draw_live_slots(jax.random.fold_in(key_of[16], 71), 0),
        "cotangent": scatter_about(key_of[2], (SLOTS, SEQ, D), 1.0, 6.0, ((0, 16),)),
        "w_qkv": scatter_about(key_of[3], (2, D, 3 * D), D ** -0.5, 0.3125, ((0, 2), (1, 4))),
        "w_out": scatter_about(key_of[4], (2, D, D), (D // 4) ** -0.5, 0.625, ((0, 2), (1, 4))),
        "w_up": scatter_about(key_of[5], (2, D, FF), D ** -0.5, 0.3125, ((0, 2), (1, 4))),
        "w_down": scatter_about(key_of[6], (2, FF, D), FF ** -0.5, 0.15625, ((0, 2), (1, 4))),
        "bias_q": scatter_about(key_of[7], (2, D), 0.3, 1.5, ((0, 2), (1, 4)), jnp.float32),
        "bias_v": scatter_about(key_of[8], (2, D), 0.3, 1.5, ((0, 2), (1, 4)), jnp.float32),
        "bias_out": scatter_about(key_of[9], (2, D), 0.3, 1.5, ((0, 2), (1, 4)), jnp.float32),
        "bias_up": scatter_about(key_of[10], (2, FF), 0.3, 1.5, ((0, 2), (1, 4)), jnp.float32),
        "bias_down": scatter_about(key_of[11], (2, D), 0.3, 1.5, ((0, 2), (1, 4)), jnp.float32),
        "gain_one": jnp.clip(1.0 + 0.1 * jax.random.normal(key_of[12], (2, D), jnp.float32), 0.5, 1.5),
        "offset_one": scatter_about(key_of[13], (2, D), 0.3, 1.5, ((0, 2), (1, 4)), jnp.float32),
        "gain_two": jnp.clip(1.0 + 0.1 * jax.random.normal(key_of[14], (2, D), jnp.float32), 0.5, 1.5),
        "offset_two": scatter_about(key_of[15], (2, D), 0.3, 1.5, ((0, 2), (1, 4)), jnp.float32),
    }


@jax.custom_vjp
def low(v):
    return lax.optimization_barrier(v.astype(jnp.bfloat16)).astype(jnp.float32)

@jax.custom_vjp
def low_back(v):
    return v

def low_keep(v):
    return (low(v), None)

def low_pass(kept, grad):
    return (grad,)

def back_keep(v):
    return (v, None)

def back_low(kept, grad):
    return (low(grad),)
low.defvjp(low_keep, low_pass)
low_back.defvjp(back_keep, back_low)
epsilon = 1e-06
highest = lax.Precision.HIGHEST

def matmul_high(former, latter):
    return jnp.matmul(former, latter, precision=highest)

def normalize(values):
    row_mean = lax.optimization_barrier(jnp.mean(values, -1, keepdims=True))
    centred = values - row_mean
    return centred * lax.rsqrt(lax.optimization_barrier(jnp.mean(centred * centred, -1, keepdims=True)) + epsilon)

def encoder_layer(inputs, params):
    w_qkv, w_out, w_up, w_down, bias_q, bias_v, bias_out, bias_up, bias_down, gain_one, offset_one, gain_two, offset_two = params
    model_width = inputs.shape[-1]
    head_shape = inputs.shape[:-1] + (model_width // HEAD_DIM, HEAD_DIM)
    score_scale = HEAD_DIM ** (-0.5)
    normed = low(normalize(inputs) * gain_one + offset_one)
    qkv_out = matmul_high(normed, w_qkv)
    queries = low(low_back(qkv_out[..., :model_width] + bias_q))
    key_rows = low(low_back(qkv_out[..., model_width:2 * model_width]))
    value_rows = low(low_back(qkv_out[..., 2 * model_width:] + bias_v))
    scores = jnp.einsum('bqhe,bkhe->bhqk', queries.reshape(head_shape), key_rows.reshape(head_shape), precision=highest)
    scores = low_back(scores * score_scale)
    attention = low(jax.nn.softmax(scores, axis=-1))
    attended = jnp.einsum('bhqk,bkhe->bqhe', attention, value_rows.reshape(head_shape), precision=highest)
    attended = low(low_back(attended.reshape(inputs.shape)))
    hidden = inputs + low_back(matmul_high(attended, w_out)) + bias_out
    normed_two = low(normalize(hidden) * gain_two + offset_two)
    up_branch = low_back(matmul_high(normed_two, w_up) + bias_up)
    activated = low(jax.nn.gelu(up_branch, approximate=False))
    return hidden + low_back(matmul_high(activated, w_down)) + bias_down

def reference(patches, live_slots, cotangent, w_qkv, w_out, w_up, w_down, bias_q, bias_v, bias_out, bias_up, bias_down, gain_one, offset_one, gain_two, offset_two):
    arrays = (w_qkv, w_out, w_up, w_down, bias_q, bias_v, bias_out, bias_up, bias_down, gain_one, offset_one, gain_two, offset_two)
    params = tuple((member.astype(jnp.float32) for member in arrays))
    start = patches.astype(jnp.float32)
    probe = jnp.zeros_like(start)

    def forward(params, start, probe):
        first = tuple((member[0] for member in params))
        second = tuple((member[1] for member in params))
        out_one = encoder_layer(start, first)
        passed = low_back(low(out_one)) + low_back(probe)
        out_two = encoder_layer(passed, second)
        return (out_two, out_one)
    (out_two, out_one), pullback = jax.vjp(forward, params, start, probe)
    seed_rows = cotangent.astype(jnp.float32) * live_slots.astype(jnp.float32)[:, None, None]
    grads, grad_start, grad_probe = pullback((seed_rows, jnp.zeros_like(out_one)))
    layer_outputs = jnp.stack([out_one, out_two]).astype(jnp.bfloat16)
    input_grads = jnp.stack([grad_start, grad_probe])
    return (layer_outputs, input_grads, grads[0], grads[1], grads[2], grads[3], grads[4], grads[5], grads[6], grads[7], grads[8], grads[9], grads[10], grads[11], grads[12])
```

```python
import functools

import jax
import jax.numpy as jnp
from jax import lax
from jax.experimental import pallas as pl
from jax.experimental.pallas import tpu as pltpu
from jax.sharding import PartitionSpec as P

HEAD_DIM = 64
EPSILON = 1e-06
ROOT_HALF = 0.7071067811865476
INVERSE_ROOT_TWO_PI = 0.3989422804014327
F32 = jnp.float32
BF16 = jnp.bfloat16
LANES = 128
VMEM_LIMIT = 48 * 1024 * 1024

BIAS_Q, BIAS_V, BIAS_OUT, BIAS_DOWN, GAIN_ONE, OFFSET_ONE, GAIN_TWO, OFFSET_TWO = range(8)


def dot(a, b):
    return lax.dot_general(a, b, (((1,), (0,)), ((), ())), preferred_element_type=F32)


def dot_back(a, b):
    return lax.dot_general(a, b, (((1,), (1,)), ((), ())), preferred_element_type=F32)


def dot_rows(a, b):
    return lax.dot_general(a, b, (((0,), (0,)), ((), ())), preferred_element_type=F32)


def normalize(values):
    row_mean = jnp.mean(values, -1, keepdims=True)
    centred = values - row_mean
    inverse = lax.rsqrt(jnp.mean(centred * centred, -1, keepdims=True) + EPSILON)
    return centred * inverse, inverse


def norm_backward(grad, unit, inverse):
    centre = jnp.mean(grad, -1, keepdims=True)
    slope = jnp.mean(grad * unit, -1, keepdims=True)
    return inverse * (grad - centre - unit * slope)


def total(values):
    return jnp.sum(values, axis=0, keepdims=True)


def head_masks(rows):
    lane = lax.broadcasted_iota(jnp.int32, (rows, LANES), 1)
    return (lane < HEAD_DIM, lane >= HEAD_DIM)


def pick(mask, value):
    return jnp.where(mask, value.astype(F32), 0.0).astype(BF16)


def layer_forward(x, seq, weights, vec, bias_up, acts):
    rows, width = x.shape
    w_qkv, w_out, w_up, w_down = weights
    qkv_ref, p_ref, attended_ref, hidden_ref, act_ref, slope_ref = acts
    unit, _ = normalize(x)
    normed = (unit * vec(GAIN_ONE) + vec(OFFSET_ONE)).astype(BF16)
    qkv = dot(normed, w_qkv())
    queries = (qkv[:, :width] + vec(BIAS_Q)).astype(BF16).astype(F32) * HEAD_DIM ** (-0.5)
    qkv_ref[:, :width] = queries.astype(BF16)
    qkv_ref[:, width : 2 * width] = qkv[:, width : 2 * width].astype(BF16)
    qkv_ref[:, 2 * width :] = (qkv[:, 2 * width :] + vec(BIAS_V)).astype(BF16)
    masks = head_masks(rows)
    key_live = lax.broadcasted_iota(jnp.int32, (rows, rows), 1) < seq
    for pair in range(width // LANES):
        lo = pair * LANES
        q = qkv_ref[:, lo : lo + LANES]
        k = qkv_ref[:, width + lo : width + lo + LANES]
        v = qkv_ref[:, 2 * width + lo : 2 * width + lo + LANES]
        gathered = None
        for half in range(2):
            scores = dot_back(pick(masks[half], q), k)
            scores = jnp.where(key_live, scores, -1e30)
            scores = jnp.exp(scores - jnp.max(scores, -1, keepdims=True))
            prob = (scores * (1.0 / jnp.sum(scores, -1, keepdims=True))).astype(BF16)
            p_ref[2 * pair + half] = prob
            part = dot(prob, pick(masks[half], v))
            gathered = part if gathered is None else gathered + part
        attended_ref[:, lo : lo + LANES] = gathered.astype(BF16)
    hidden = x + dot(attended_ref[...], w_out()) + vec(BIAS_OUT)
    hidden_ref[...] = hidden
    unit_two, _ = normalize(hidden)
    normed_two = (unit_two * vec(GAIN_TWO) + vec(OFFSET_TWO)).astype(BF16)
    output = hidden + vec(BIAS_DOWN)
    wide = act_ref.shape[1]
    step = 512
    for lo in range(0, wide, step):
        up = dot(normed_two, w_up(lo, step)) + bias_up(lo, step)
        cdf = 0.5 * (1.0 + lax.erf(up * ROOT_HALF))
        density = jnp.exp(-0.5 * up * up) * INVERSE_ROOT_TWO_PI
        act = (up * cdf).astype(BF16)
        act_ref[:, lo : lo + step] = act
        slope_ref[:, lo : lo + step] = (cdf + up * density).astype(BF16)
        output = output + dot(act, w_down(lo, step))
    return output


def layer_backward(grad, x, weights, vec, acts, up_grad_ref, qkv_grad_ref, put):
    rows, width = grad.shape
    w_qkv, w_out, w_up, w_down = weights
    qkv_ref, p_ref, attended_ref, hidden_ref, act_ref, slope_ref = acts
    wide = act_ref.shape[1]
    step = 512
    down_grad = grad.astype(BF16)
    unit_two, inverse_two = normalize(hidden_ref[...])
    normed_two = (unit_two * vec(GAIN_TWO) + vec(OFFSET_TWO)).astype(BF16)
    grad_normed_two = None
    sums_up = []
    for lo in range(0, wide, step):
        put.w_down(lo, dot_rows(act_ref[:, lo : lo + step], down_grad))
        up_grad = dot_back(down_grad, w_down(lo, step)) * slope_ref[:, lo : lo + step].astype(F32)
        up_grad = up_grad.astype(BF16)
        sums_up.append(total(up_grad.astype(F32)))
        put.w_up(lo, dot_rows(normed_two, up_grad))
        part = dot_back(up_grad, w_up(lo, step))
        grad_normed_two = part if grad_normed_two is None else grad_normed_two + part
    grad_hidden = grad + norm_backward(grad_normed_two * vec(GAIN_TWO), unit_two, inverse_two)
    out_grad = grad_hidden.astype(BF16)
    put.w_out(dot_rows(attended_ref[...], out_grad))
    attended_grad = dot_back(out_grad, w_out()).astype(BF16)
    masks = head_masks(rows)
    for pair in range(width // LANES):
        lo = pair * LANES
        q = qkv_ref[:, lo : lo + LANES]
        k = qkv_ref[:, width + lo : width + lo + LANES]
        v = qkv_ref[:, 2 * width + lo : 2 * width + lo + LANES]
        ag = attended_grad[:, lo : lo + LANES]
        q_grad = k_grad = v_grad = None
        for half in range(2):
            mine = pick(masks[half], ag)
            prob = p_ref[2 * pair + half]
            prob32 = prob.astype(F32)
            grad_prob = dot_back(mine, v)
            dv = dot_rows(prob, mine)
            row_term = jnp.sum(grad_prob * prob32, -1, keepdims=True)
            score_grad = (prob32 * (grad_prob - row_term)).astype(BF16)
            dq = dot(score_grad, pick(masks[half], k))
            dk = dot_rows(score_grad, pick(masks[half], q))
            q_grad = dq if q_grad is None else q_grad + dq
            k_grad = dk if k_grad is None else k_grad + dk
            v_grad = dv if v_grad is None else v_grad + dv
        qkv_grad_ref[:, lo : lo + LANES] = (q_grad * HEAD_DIM ** (-0.5)).astype(BF16)
        qkv_grad_ref[:, width + lo : width + lo + LANES] = k_grad.astype(BF16)
        qkv_grad_ref[:, 2 * width + lo : 2 * width + lo + LANES] = v_grad.astype(BF16)
    unit, inverse = normalize(x)
    normed = (unit * vec(GAIN_ONE) + vec(OFFSET_ONE)).astype(BF16)
    put.w_qkv(dot_rows(normed, qkv_grad_ref[...]))
    grad_normed = dot_back(qkv_grad_ref[...], w_qkv())
    grad_x = grad_hidden + norm_backward(grad_normed * vec(GAIN_ONE), unit, inverse)
    sums = jnp.concatenate(
        [
            total(qkv_grad_ref[:, :width].astype(F32)),
            total(qkv_grad_ref[:, 2 * width :].astype(F32)),
            total(grad_hidden),
            total(grad),
            total(grad_normed * unit),
            total(grad_normed),
            total(grad_normed_two * unit_two),
            total(grad_normed_two),
        ],
        0,
    )
    put.vectors(sums, jnp.concatenate(sums_up, 1))
    return grad_x


ROWS = 96
HALF = 48
UP0, QKV0, OUT0, DOWN0, VEC0, PACKED = 0, 1536, 2688, 3072, 4608, 4736
QUARTER = 896
TAIL0, TAIL = 3584, 1152
PIECE = 1280
SEQ_ROWS = 208


def positions():
    return lax.axis_index("section"), lax.axis_index("shard"), lax.axis_index("replica")


class PackedPut:
    def __init__(self, grads, shard, replica):
        self.grads, self.shard, self.replica = grads, shard, replica

    def store(self, owner, column, value, row=0):
        place = lax.rem(owner - self.shard + 4, 4)
        rows, columns = value.shape
        value = value.astype(BF16)
        while columns:
            piece, inside = column // PIECE, column % PIECE
            count = min(columns, PIECE - inside)
            where = lax.bitwise_xor(self.replica, piece)
            for half in range(2):
                lo, hi = max(row, half * HALF), min(row + rows, half * HALF + HALF)
                if lo < hi:
                    self.grads[half, where, place, lo - half * HALF : hi - half * HALF, inside : inside + count] = (
                        value[lo - row : hi - row, :count]
                    )
            value, column, columns = value[:, count:], column + count, columns - count

    def by_rows(self, column, value):
        for owner in range(4):
            self.store(owner, column, value[owner * ROWS : (owner + 1) * ROWS])

    def w_up(self, lo, value):
        self.by_rows(UP0 + lo, value)

    def w_qkv(self, value):
        self.by_rows(QKV0, value)

    def w_out(self, value):
        self.by_rows(OUT0, value)

    def w_down(self, lo, value):
        rows, at = value.shape[0], 0
        while at < rows:
            owner, inside = divmod(lo + at, 4 * ROWS)
            fold, row = divmod(inside, ROWS)
            count = min(rows - at, ROWS - row)
            self.store(owner, DOWN0 + fold * value.shape[1], value[at : at + count], row)
            at += count

    def vectors(self, sums, bias_up):
        place3 = lax.bitwise_xor(self.replica, 3)
        first = VEC0 - 3 * PIECE
        self.grads[:, place3, :, :, first:] = jnp.zeros((2, 4, HALF, PIECE - first), BF16)
        blank = jnp.zeros((8, LANES - ROWS), F32)
        rest = jnp.zeros((5, LANES), F32)
        for owner in range(4):
            up = [
                bias_up[:, owner * 384 + k * LANES : owner * 384 + (k + 1) * LANES] for k in range(3)
            ]
            top = jnp.concatenate([sums[:, owner * ROWS : (owner + 1) * ROWS], blank], 1)
            tile = jnp.concatenate([top] + up + [rest], 0)
            self.store(owner, VEC0, tile)


def packed_weights(packed, down, layer):
    def w_qkv():
        return packed[layer, :, :, QKV0:OUT0].reshape(4 * ROWS, OUT0 - QKV0)

    def w_out():
        return packed[layer, :, :, OUT0:DOWN0].reshape(4 * ROWS, DOWN0 - OUT0)

    def w_up(lo, step):
        return packed[layer, :, :, UP0 + lo : UP0 + lo + step].reshape(4 * ROWS, step)

    def w_down(lo, step):
        return down[layer, lo : lo + step]

    return w_qkv, w_out, w_up, w_down


def unfold(packed, down, vectors, biases, layer):
    width = down.shape[2]
    for owner in range(4):
        for fold in range(4):
            at = (owner * 4 + fold) * ROWS
            down[layer, at : at + ROWS] = packed[
                layer, owner, :, DOWN0 + fold * width : DOWN0 + (fold + 1) * width
            ]
    tiles = [
        packed[layer, owner, 0:16, VEC0:PACKED].astype(F32)
        + packed[layer, owner, 16:32, VEC0:PACKED].astype(F32)
        for owner in range(4)
    ]
    vectors[layer] = jnp.concatenate([tile[0:8, 0:ROWS] for tile in tiles], 1)
    biases[layer] = jnp.concatenate([tile[8 + k : 9 + k] for tile in tiles for k in range(3)], 1)


def start_copies(pieces, packed, layer, sems, shard, replica):
    own, tail1, tail2, tail3, same, across_x, across_y, across_d = pieces
    copies = [(own, packed.at[layer, shard])]
    for step, tail in ((1, tail1), (2, tail2), (3, tail3)):
        copies.append((tail, packed.at[layer, lax.rem(shard + 4 - step, 4), :, pl.ds(TAIL0, TAIL)]))
    for flip, group in ((0, same), (1, across_x), (2, across_y), (3, across_d)):
        column = pl.multiple_of(lax.bitwise_xor(replica, flip) * QUARTER, LANES)
        for step in (1, 2, 3):
            copies.append(
                (
                    group.at[step - 1],
                    packed.at[layer, lax.rem(shard + 4 - step, 4), :, pl.ds(column, QUARTER)],
                )
            )
    return [
        pltpu.make_async_copy(source, target, sems.at[layer, index])
        for index, (source, target) in enumerate(copies)
    ]


def main_kernel(seq, *refs):
    mine, other = refs[0:8], refs[8:16]
    patches, cotangent, live = refs[16:19]
    (
        out_one,
        out_two,
        grad_one,
        keep,
        send,
        kept_weights,
        kept_vectors,
        qkv0,
        p0,
        attended0,
        hidden0,
        act0,
        slope0,
    ) = refs[19:32]
    (
        packed,
        down,
        vectors,
        biases,
        rows_in,
        rows_mid,
        qkv1,
        p1,
        attended1,
        hidden1,
        act1,
        slope1,
        up_grad,
        qkv_grad,
        grads,
        sems,
        out_sems,
    ) = refs[32:]
    section, shard, replica = positions()
    for copy in start_copies(mine, packed, section, sems, shard, replica):
        copy.start()
    for copy in start_copies(other, packed, 1 - section, sems, shard, replica):
        copy.start()
    width = rows_in.shape[1]
    rows_in[seq - seq % 8 :] = jnp.zeros((SEQ_ROWS - seq + seq % 8, width), F32)
    rows_in[:seq] = patches[section].astype(F32)

    def ready(layer):
        for copy in start_copies(mine, packed, layer, sems, shard, replica):
            copy.wait()
        unfold(packed, down, vectors, biases, layer)
        vec = lambda index: vectors[layer, index : index + 1]
        bias_up = lambda lo, step: biases[layer, :, lo : lo + step]
        return packed_weights(packed, down, layer), vec, bias_up

    weights0, vec0, bias_up0 = ready(0)
    save = [
        pltpu.make_async_copy(packed.at[0], kept_weights.at[0], out_sems.at[0]),
    ]
    for copy in save:
        copy.start()
    kept_vectors[...] = vectors[0]
    x0 = rows_in[...]
    acts0 = (qkv0, p0, attended0, hidden0, act0, slope0)
    result = layer_forward(x0, seq, weights0, vec0, bias_up0, acts0)
    out_one[...] = result[:seq].astype(BF16)
    live_rows = lax.broadcasted_iota(jnp.int32, (SEQ_ROWS, width), 0) < seq
    rows_mid[...] = jnp.where(live_rows, result.astype(BF16).astype(F32), 0.0)

    weights1, vec1, bias_up1 = ready(1)
    acts1 = (qkv1, p1, attended1, hidden1, act1, slope1)
    result = layer_forward(rows_mid[...], seq, weights1, vec1, bias_up1, acts1)
    out_two[...] = result[:seq].astype(BF16)

    rows_in[:seq] = cotangent[section].astype(F32) * live[section].astype(F32)
    put = PackedPut(grads, shard, replica)
    grad_x = layer_backward(
        rows_in[...], rows_mid[...], weights1, vec1, acts1, up_grad, qkv_grad, put
    )
    grad_one[...] = grad_x[:seq].astype(BF16)
    copies = [
        pltpu.make_async_copy(grads.at[section], keep, out_sems.at[1]),
        pltpu.make_async_copy(grads.at[1 - section], send, out_sems.at[2]),
    ]
    for copy in copies:
        copy.start()
    for copy in save + copies:
        copy.wait()


def last_kernel(seq, *refs):
    weights, vectors_in, grad_one, patches = refs[0:4]
    acts = refs[4:10]
    grad_out, keep, send = refs[10:13]
    packed, down, rows_in, rows_grad, up_grad, qkv_grad, grads, sems, out_sems = refs[13:]
    section, shard, replica = positions()
    load = pltpu.make_async_copy(weights, packed, sems.at[0])
    load.start()
    width = rows_in.shape[1]
    for buffer, source in ((rows_in, patches[section]), (rows_grad, grad_one[...])):
        buffer[seq - seq % 8 :] = jnp.zeros((SEQ_ROWS - seq + seq % 8, width), F32)
        buffer[:seq] = source.astype(F32)
    load.wait()
    for owner in range(4):
        for fold in range(4):
            at = (owner * 4 + fold) * ROWS
            down[0, at : at + ROWS] = packed[
                0, owner, :, DOWN0 + fold * width : DOWN0 + (fold + 1) * width
            ]
    vec = lambda index: vectors_in[index : index + 1]
    put = PackedPut(grads, shard, replica)
    grad_x = layer_backward(
        rows_grad[...],
        rows_in[...],
        packed_weights(packed, down, 0),
        vec,
        acts,
        up_grad,
        qkv_grad,
        put,
    )
    grad_out[...] = grad_x[:seq]
    copies = [
        pltpu.make_async_copy(grads.at[section], keep, out_sems.at[0]),
        pltpu.make_async_copy(grads.at[1 - section], send, out_sems.at[1]),
    ]
    for copy in copies:
        copy.start()
    for copy in copies:
        copy.wait()


def vmem(count):
    return [pl.BlockSpec(memory_space=pltpu.VMEM)] * count


def anywhere(count):
    return [pl.BlockSpec(memory_space=pl.ANY)] * count


def shape(dims, dtype):
    return jax.ShapeDtypeStruct(dims, dtype)


def act_shapes(width, wide):
    heads = width // HEAD_DIM
    return [
        ((SEQ_ROWS, 3 * width), BF16),
        ((heads, SEQ_ROWS, SEQ_ROWS), BF16),
        ((SEQ_ROWS, width), BF16),
        ((SEQ_ROWS, width), F32),
        ((SEQ_ROWS, wide), BF16),
        ((SEQ_ROWS, wide), BF16),
    ]


PARAMS = pltpu.CompilerParams(vmem_limit_bytes=VMEM_LIMIT)


def run_main(mine, other, patches, cotangent, live, wide):
    seq, width = patches.shape[1:]
    acts = act_shapes(width, wide)
    return pl.pallas_call(
        functools.partial(main_kernel, seq),
        out_shape=[
            shape((seq, width), BF16),
            shape((seq, width), BF16),
            shape((seq, width), BF16),
            shape((4, 4, HALF, PIECE), BF16),
            shape((4, 4, HALF, PIECE), BF16),
            shape((1, 4, ROWS, PACKED), BF16),
            shape((8, width), F32),
        ]
        + [shape(*a) for a in acts],
        in_specs=anywhere(16) + vmem(2) + [pl.BlockSpec(memory_space=pltpu.SMEM)],
        out_specs=vmem(3) + anywhere(3) + vmem(7),
        scratch_shapes=[
            pltpu.VMEM((2, 4, ROWS, PACKED), BF16),
            pltpu.VMEM((2, wide, width), BF16),
            pltpu.VMEM((2, 8, width), F32),
            pltpu.VMEM((2, 1, wide), F32),
            pltpu.VMEM((SEQ_ROWS, width), F32),
            pltpu.VMEM((SEQ_ROWS, width), F32),
        ]
        + [pltpu.VMEM(*a) for a in acts]
        + [
            pltpu.VMEM((SEQ_ROWS, wide), BF16),
            pltpu.VMEM((SEQ_ROWS, 3 * width), BF16),
            pltpu.VMEM((2, 4, 4, HALF, PIECE), BF16),
            pltpu.SemaphoreType.DMA((2, 16)),
            pltpu.SemaphoreType.DMA((3,)),
        ],
        compiler_params=PARAMS,
        name="forward_and_layer_one",
    )(*mine, *other, patches, cotangent, live)


def run_last(weights, vectors, grad_one, patches, acts, wide):
    seq, width = patches.shape[1:]
    return pl.pallas_call(
        functools.partial(last_kernel, seq),
        out_shape=[
            shape((seq, width), F32),
            shape((4, 4, HALF, PIECE), BF16),
            shape((4, 4, HALF, PIECE), BF16),
        ],
        in_specs=anywhere(1) + vmem(9),
        out_specs=vmem(1) + anywhere(2),
        scratch_shapes=[
            pltpu.VMEM((1, 4, ROWS, PACKED), BF16),
            pltpu.VMEM((1, wide, width), BF16),
            pltpu.VMEM((SEQ_ROWS, width), F32),
            pltpu.VMEM((SEQ_ROWS, width), F32),
            pltpu.VMEM((SEQ_ROWS, wide), BF16),
            pltpu.VMEM((SEQ_ROWS, 3 * width), BF16),
            pltpu.VMEM((2, 4, 4, HALF, PIECE), BF16),
            pltpu.SemaphoreType.DMA((1,)),
            pltpu.SemaphoreType.DMA((2,)),
        ],
        compiler_params=PARAMS,
        name="layer_zero_backward",
    )(weights, vectors, grad_one, patches, *acts)


def pair_sum_kernel(keep, recv, *outs):
    for place in range(4):
        outs[place][...] = (keep[place].astype(F32) + recv[place].astype(F32)).astype(BF16)


def pair_sum(keep, recv):
    return pl.pallas_call(
        pair_sum_kernel,
        out_shape=[shape(keep.shape[1:], BF16)] * 4,
        in_specs=vmem(2),
        out_specs=vmem(4),
        compiler_params=PARAMS,
        name="sum_of_cores",
    )(keep, recv)


def plane_sum_kernel(a, b, c, d, *outs):
    for place in range(4):
        outs[place][...] = (
            a[place].astype(F32) + b[place].astype(F32) + (c[place].astype(F32) + d[place].astype(F32))
        ).astype(BF16)


def plane_sum(parts):
    return pl.pallas_call(
        plane_sum_kernel,
        out_shape=[shape(parts[0].shape[1:], BF16)] * 4,
        in_specs=vmem(4),
        out_specs=vmem(4),
        compiler_params=PARAMS,
        name="sum_of_plane",
    )(*parts)


def column_sum_kernel(*refs):
    ins, (mine, other) = refs[:8], refs[8:]
    section = lax.axis_index("section")
    sums = []
    for group in (ins[:4], ins[4:]):
        a, b, c, d = (member[...].astype(F32) for member in group)
        sums.append((a + b + (c + d)).astype(BF16))

    @pl.when(section == 0)
    def _():
        mine[...] = sums[0]
        other[...] = sums[1]

    @pl.when(section == 1)
    def _():
        mine[...] = sums[1]
        other[...] = sums[0]


def column_sum(zero, one):
    return pl.pallas_call(
        column_sum_kernel,
        out_shape=[shape(zero[0].shape, BF16)] * 2,
        in_specs=vmem(8),
        out_specs=vmem(2),
        compiler_params=PARAMS,
        name="sum_of_column",
    )(*zero, *one)


def unpack_kernel(*refs):
    pieces, (qkv, out, up, down), rest = refs[:8], refs[8:12], refs[12:21]
    table, sems = refs[21:]
    section, _, replica = positions()
    copies = []
    for flip in range(4):
        place = lax.bitwise_xor(replica, flip)
        for half in range(2):
            where = section if half == 0 else 1 - section
            copies.append(
                pltpu.make_async_copy(
                    pieces[2 * flip + half], table.at[place, where], sems.at[2 * flip + half]
                )
            )
    for copy in copies:
        copy.start()
    for copy in copies:
        copy.wait()

    def put(target, row, column, start, count, at):
        while count:
            piece, inside = start // PIECE, start % PIECE
            some = min(count, PIECE - inside)
            for half in range(2):
                target[0, row + half * HALF : row + half * HALF + HALF, at : at + some] = table[
                    piece, half, :, inside : inside + some
                ].astype(F32)
            start, at, count = start + some, at + some, count - some

    put(up, 0, 0, UP0, QKV0 - UP0, 0)
    put(qkv, 0, 0, QKV0, OUT0 - QKV0, 0)
    put(out, 0, 0, OUT0, DOWN0 - OUT0, 0)
    width = out.shape[2]
    for fold in range(4):
        put(down, fold * ROWS, 0, DOWN0 + fold * width, width, 0)
    inside = VEC0 - 3 * PIECE
    tile = table[3, 0, 0:16, inside : inside + LANES].astype(F32)
    for index in range(8):
        rest[index][...] = tile[index : index + 1, :ROWS]
    rest[8][...] = jnp.concatenate([tile[8 + k : 9 + k] for k in range(3)], 1)


def unpack(pieces, width, wide):
    return pl.pallas_call(
        unpack_kernel,
        out_shape=[
            shape((1, ROWS, 3 * width), F32),
            shape((1, ROWS, width), F32),
            shape((1, ROWS, wide), F32),
            shape((1, 4 * ROWS, width), F32),
        ]
        + [shape((1, ROWS), F32)] * 8
        + [shape((1, 4 * ROWS), F32)],
        in_specs=anywhere(8),
        out_specs=vmem(13),
        scratch_shapes=[
            pltpu.VMEM((4, 2, HALF, PIECE), BF16),
            pltpu.SemaphoreType.DMA((8,)),
        ],
        compiler_params=PARAMS,
        name="unpack",
    )(*pieces)


def swap(value):
    return lax.ppermute(value, "section", [(0, 1), (1, 0)])


def flip(value, bits):
    return lax.ppermute(value, "replica", [(place, place ^ bits) for place in range(4)])


def shift(value, steps):
    return lax.ppermute(value, "shard", [(place, (place + steps) % 4) for place in range(4)])


def packed_local(patches, live_slots, cotangent, w_qkv, w_out, w_up, w_down, *small):
    bias_q, bias_v, bias_out, bias_up, bias_down, gain_one, offset_one, gain_two, offset_two = small
    section, _, replica = positions()
    width, wide = w_out.shape[2], w_up.shape[2]
    folded = [w_down[0, fold * ROWS : (fold + 1) * ROWS] for fold in range(4)]
    eight = jnp.concatenate(
        [bias_q, bias_v, bias_out, bias_down, gain_one, offset_one, gain_two, offset_two], 0
    )
    eight = jnp.pad(eight, ((0, 0), (0, LANES - ROWS)))
    tile = jnp.concatenate([eight, bias_up.reshape(3, LANES), jnp.zeros((5, LANES), F32)], 0)
    high = tile.astype(BF16)
    low = (tile - high.astype(F32)).astype(BF16)
    tile = jnp.concatenate([high, low, jnp.zeros((ROWS - 32, LANES), BF16)], 0)
    own = jnp.concatenate([w_up[0], w_qkv[0], w_out[0]] + folded + [tile], 1)
    tail = own[:, TAIL0:]
    quarter = lax.dynamic_slice(own, (0, replica * QUARTER), (ROWS, QUARTER))

    same = jnp.stack([shift(quarter, step) for step in (1, 2, 3)])
    across = [flip(same, bits) for bits in (1, 2, 3)]
    tails = [shift(tail, step) for step in (1, 2, 3)]
    mine = [own] + tails + [same] + across
    other = [swap(member) for member in mine]

    (out_one, out_two, grad_one, keep1, send1, kept, vectors, *acts) = run_main(
        mine, other, patches, cotangent, live_slots, wide
    )

    def reduce_plane(keep, send):
        same, x, y, d = pair_sum(keep, swap(send))
        parts = [same, flip(x, 1), flip(y, 2), flip(d, 3)]
        chunks = plane_sum(parts)
        return [chunks[0]] + [shift(chunks[step], step) for step in (1, 2, 3)]

    one = reduce_plane(keep1, send1)
    grad_zero, keep0, send0 = run_last(kept, vectors, grad_one, patches, acts, wide)
    zero = reduce_plane(keep0, send0)
    half_mine, half_other = column_sum(zero, one)
    halves = [half_mine, swap(half_other)]
    pieces = list(halves)
    for bits in (1, 2, 3):
        pieces += [flip(member, bits) for member in halves]
    grad_qkv, grad_out, grad_up, grad_down, *rest = unpack(pieces, width, wide)

    first = section == 0
    out_send = jnp.where(first, out_two, out_one)
    out_recv = swap(out_send)
    layer_outputs = jnp.stack(
        [jnp.where(first, out_one, out_recv), jnp.where(first, out_recv, out_two)]
    )[None]
    grad_one32 = grad_one.astype(F32)
    grad_recv = swap(jnp.where(first, grad_one32, grad_zero))
    input_grads = jnp.stack(
        [jnp.where(first, grad_zero, grad_recv), jnp.where(first, grad_recv, grad_one32)]
    )[None]
    (g_q, g_v, g_o, g_d, g_g1, g_o1, g_g2, g_o2, g_up) = rest
    return (
        layer_outputs,
        input_grads,
        grad_qkv,
        grad_out,
        grad_up,
        grad_down,
        g_q,
        g_v,
        g_o,
        g_up,
        g_d,
        g_g1,
        g_o1,
        g_g2,
        g_o2,
    )


class PlainPut:
    def __init__(self, outs, layer):
        self.outs, self.layer = outs, layer

    def w_qkv(self, value):
        self.outs[0][self.layer] = value

    def w_out(self, value):
        self.outs[1][self.layer] = value

    def w_up(self, lo, value):
        self.outs[2][self.layer, :, lo : lo + value.shape[1]] = value

    def w_down(self, lo, value):
        self.outs[3][self.layer, lo : lo + value.shape[0]] = value

    def vectors(self, sums, bias_up):
        self.outs[4][self.layer] = sums
        self.outs[5][self.layer] = bias_up


def plain_kernel(seq, *refs):
    patches, cotangent, live, w_qkv, w_out, w_up, w_down, vectors, biases = refs[:9]
    out_rows, grad_rows = refs[9:11]
    grads = refs[11:17]
    rows_in, rows_mid, up_grad, qkv_grad = refs[17:21]
    acts = (refs[21:27], refs[27:33])
    section = lax.axis_index("section")
    width = rows_in.shape[1]

    def weights_of(layer):
        return (
            lambda: w_qkv[layer],
            lambda: w_out[layer],
            lambda lo, step: w_up[layer, :, lo : lo + step],
            lambda lo, step: w_down[layer, lo : lo + step],
        )

    vec_of = lambda layer: lambda index: vectors[layer, index : index + 1]
    bias_of = lambda layer: lambda lo, step: biases[layer, :, lo : lo + step]
    live_rows = lax.broadcasted_iota(jnp.int32, (SEQ_ROWS, width), 0) < seq
    rows_in[seq - seq % 8 :] = jnp.zeros((SEQ_ROWS - seq + seq % 8, width), F32)
    rows_in[:seq] = patches[section].astype(F32)
    result = layer_forward(rows_in[...], seq, weights_of(0), vec_of(0), bias_of(0), acts[0])
    out_rows[0] = result[:seq].astype(BF16)
    rows_mid[...] = jnp.where(live_rows, result.astype(BF16).astype(F32), 0.0)
    result = layer_forward(rows_mid[...], seq, weights_of(1), vec_of(1), bias_of(1), acts[1])
    out_rows[1] = result[:seq].astype(BF16)
    seed = cotangent[section].astype(F32) * live[section].astype(F32)
    blank = jnp.zeros((SEQ_ROWS - seq, width), F32)
    grad_x = layer_backward(
        jnp.concatenate([seed, blank], 0),
        rows_mid[...],
        weights_of(1),
        vec_of(1),
        acts[1],
        up_grad,
        qkv_grad,
        PlainPut(grads, 1),
    )
    grad_x = grad_x.astype(BF16).astype(F32)
    grad_rows[1] = grad_x[:seq]
    grad_x = layer_backward(
        grad_x,
        rows_in[...],
        weights_of(0),
        vec_of(0),
        acts[0],
        up_grad,
        qkv_grad,
        PlainPut(grads, 0),
    )
    grad_rows[0] = grad_x[:seq]


def plain_local(patches, live_slots, cotangent, w_qkv, w_out, w_up, w_down, *small):
    bias_q, bias_v, bias_out, bias_up, bias_down, gain_one, offset_one, gain_two, offset_two = small
    seq, width = patches.shape[1:]
    wide = w_up.shape[2]

    def whole(value):
        along = lax.all_gather(value, "shard", axis=1, tiled=True)
        return lax.all_gather(along, "section", axis=0, tiled=True)

    small = (bias_q, bias_v, bias_out, bias_down, gain_one, offset_one, gain_two, offset_two)
    vectors = whole(jnp.stack(small, 2)).transpose(0, 2, 1)
    biases = whole(bias_up)[:, None]
    acts = act_shapes(width, wide)
    out_rows, grad_rows, *grads = pl.pallas_call(
        functools.partial(plain_kernel, seq),
        out_shape=[
            shape((2, seq, width), BF16),
            shape((2, seq, width), F32),
            shape((2, width, 3 * width), F32),
            shape((2, width, width), F32),
            shape((2, width, wide), F32),
            shape((2, wide, width), F32),
            shape((2, 8, width), F32),
            shape((2, 1, wide), F32),
        ],
        in_specs=vmem(2) + [pl.BlockSpec(memory_space=pltpu.SMEM)] + vmem(6),
        out_specs=vmem(8),
        scratch_shapes=[
            pltpu.VMEM((SEQ_ROWS, width), F32),
            pltpu.VMEM((SEQ_ROWS, width), F32),
            pltpu.VMEM((SEQ_ROWS, wide), BF16),
            pltpu.VMEM((SEQ_ROWS, 3 * width), BF16),
        ]
        + [pltpu.VMEM(*a) for a in acts + acts],
        compiler_params=PARAMS,
        name="both_layers",
    )(patches, cotangent, live_slots, *(whole(w) for w in (w_qkv, w_out, w_up, w_down)), vectors, biases)

    def owned(value):
        mine = lax.psum_scatter(value, "section", scatter_dimension=0, tiled=True)
        mine = lax.psum_scatter(mine.astype(BF16), "shard", scatter_dimension=1, tiled=True)
        return lax.psum(mine, "replica").astype(F32)

    grads = [owned(value) for value in grads[:4]] + [
        owned(grads[4].transpose(0, 2, 1)),
        owned(grads[5][:, 0]),
    ]
    q, v, out, down, g1, o1, g2, o2 = (grads[4][..., index] for index in range(8))

    def by_section(value):
        section = lax.axis_index("section")
        recv = swap(jnp.where(section == 0, value[1], value[0]))
        first = jnp.where(section == 0, value[0], recv)
        return jnp.stack([first, jnp.where(section == 0, recv, value[1])])[None]

    return (
        by_section(out_rows),
        by_section(grad_rows),
        *grads[:4],
        q,
        v,
        out,
        grads[5],
        down,
        g1,
        o1,
        g2,
        o2,
    )


def solution(mesh):
    slots = P(("shard", "replica"), None, None)
    matrix, vector = P("section", "shard", None), P("section", "shard")
    outs = P("section", ("shard", "replica"), None, None)
    packed = mesh.shape["shard"] == 4 and mesh.shape["replica"] == 4
    return jax.shard_map(
        packed_local if packed else plain_local,
        mesh=mesh,
        in_specs=(slots, P(("shard", "replica")), slots) + (matrix,) * 4 + (vector,) * 9,
        out_specs=(outs, outs) + (matrix,) * 4 + (vector,) * 9,
        check_vma=False,
    )
```

```python
import functools

import jax
import jax.numpy as jnp
from jax import lax
from jax.experimental import pallas as pl
from jax.experimental.pallas import tpu as pltpu
from jax.sharding import PartitionSpec as P

HEAD_DIM = 64
EPSILON = 1e-06
ROOT_HALF = 0.7071067811865476
INVERSE_ROOT_TWO_PI = 0.3989422804014327
F32 = jnp.float32
BF16 = jnp.bfloat16
LANES = 128
MIB = 1024 * 1024

BIAS_Q, BIAS_V, BIAS_OUT, BIAS_DOWN, GAIN_ONE, OFFSET_ONE, GAIN_TWO, OFFSET_TWO = range(8)


def dot(a, b):
    return lax.dot_general(a, b, (((1,), (0,)), ((), ())), preferred_element_type=F32)


def dot_back(a, b):
    return lax.dot_general(a, b, (((1,), (1,)), ((), ())), preferred_element_type=F32)


def dot_rows(a, b):
    return lax.dot_general(a, b, (((0,), (0,)), ((), ())), preferred_element_type=F32)


def normalize(values):
    row_mean = jnp.mean(values, -1, keepdims=True)
    centred = values - row_mean
    inverse = lax.rsqrt(jnp.mean(centred * centred, -1, keepdims=True) + EPSILON)
    return centred * inverse, inverse


def norm_backward(grad, unit, inverse):
    centre = jnp.mean(grad, -1, keepdims=True)
    slope = jnp.mean(grad * unit, -1, keepdims=True)
    return inverse * (grad - centre - unit * slope)


def total(values):
    return jnp.sum(values, axis=0, keepdims=True)


def head_masks(rows):
    lane = lax.broadcasted_iota(jnp.int32, (rows, LANES), 1)
    return (lane < HEAD_DIM, lane >= HEAD_DIM)


def pick(mask, value):
    return jnp.where(mask, value.astype(F32), 0.0).astype(BF16)


def layer_forward(x, seq, weights, vec, bias_up, acts):
    rows, width = x.shape
    w_qkv, w_out, w_up, w_down = weights
    qkv_ref, p_ref, attended_ref, hidden_ref, act_ref, slope_ref = acts
    unit, _ = normalize(x)
    normed = (unit * vec(GAIN_ONE) + vec(OFFSET_ONE)).astype(BF16)
    qkv = dot(normed, w_qkv())
    queries = (qkv[:, :width] + vec(BIAS_Q)).astype(BF16).astype(F32) * HEAD_DIM ** (-0.5)
    qkv_ref[:, :width] = queries.astype(BF16)
    qkv_ref[:, width : 2 * width] = qkv[:, width : 2 * width].astype(BF16)
    qkv_ref[:, 2 * width :] = (qkv[:, 2 * width :] + vec(BIAS_V)).astype(BF16)
    masks = head_masks(rows)
    key_live = lax.broadcasted_iota(jnp.int32, (rows, rows), 1) < seq
    for pair in range(width // LANES):
        lo = pair * LANES
        q = qkv_ref[:, lo : lo + LANES]
        k = qkv_ref[:, width + lo : width + lo + LANES]
        v = qkv_ref[:, 2 * width + lo : 2 * width + lo + LANES]
        gathered = None
        for half in range(2):
            scores = dot_back(pick(masks[half], q), k)
            scores = jnp.where(key_live, scores, -1e30)
            scores = jnp.exp(scores - jnp.max(scores, -1, keepdims=True))
            prob = (scores * (1.0 / jnp.sum(scores, -1, keepdims=True))).astype(BF16)
            p_ref[2 * pair + half] = prob
            part = dot(prob, pick(masks[half], v))
            gathered = part if gathered is None else gathered + part
        attended_ref[:, lo : lo + LANES] = gathered.astype(BF16)
    hidden = x + dot(attended_ref[...], w_out()) + vec(BIAS_OUT)
    hidden_ref[...] = hidden
    unit_two, _ = normalize(hidden)
    normed_two = (unit_two * vec(GAIN_TWO) + vec(OFFSET_TWO)).astype(BF16)
    output = hidden + vec(BIAS_DOWN)
    wide = act_ref.shape[1]
    step = 512
    for lo in range(0, wide, step):
        up = dot(normed_two, w_up(lo, step)) + bias_up(lo, step)
        cdf = 0.5 * (1.0 + lax.erf(up * ROOT_HALF))
        density = jnp.exp(-0.5 * up * up) * INVERSE_ROOT_TWO_PI
        act = (up * cdf).astype(BF16)
        act_ref[:, lo : lo + step] = act
        slope_ref[:, lo : lo + step] = (cdf + up * density).astype(BF16)
        output = output + dot(act, w_down(lo, step))
    return output


def layer_backward(grad, x, weights, vec, acts, up_grad_ref, qkv_grad_ref, put):
    rows, width = grad.shape
    w_qkv, w_out, w_up, w_down = weights
    qkv_ref, p_ref, attended_ref, hidden_ref, act_ref, slope_ref = acts
    wide = act_ref.shape[1]
    step = 512
    down_grad = grad.astype(BF16)
    unit_two, inverse_two = normalize(hidden_ref[...])
    normed_two = (unit_two * vec(GAIN_TWO) + vec(OFFSET_TWO)).astype(BF16)
    grad_normed_two = None
    sums_up = []
    for lo in range(0, wide, step):
        put.w_down(lo, dot_rows(act_ref[:, lo : lo + step], down_grad))
        up_grad = dot_back(down_grad, w_down(lo, step)) * slope_ref[:, lo : lo + step].astype(F32)
        up_grad = up_grad.astype(BF16)
        sums_up.append(total(up_grad.astype(F32)))
        put.w_up(lo, dot_rows(normed_two, up_grad))
        part = dot_back(up_grad, w_up(lo, step))
        grad_normed_two = part if grad_normed_two is None else grad_normed_two + part
    grad_hidden = grad + norm_backward(grad_normed_two * vec(GAIN_TWO), unit_two, inverse_two)
    out_grad = grad_hidden.astype(BF16)
    put.w_out(dot_rows(attended_ref[...], out_grad))
    attended_grad = dot_back(out_grad, w_out()).astype(BF16)
    masks = head_masks(rows)
    for pair in range(width // LANES):
        lo = pair * LANES
        q = qkv_ref[:, lo : lo + LANES]
        k = qkv_ref[:, width + lo : width + lo + LANES]
        v = qkv_ref[:, 2 * width + lo : 2 * width + lo + LANES]
        ag = attended_grad[:, lo : lo + LANES]
        q_grad = k_grad = v_grad = None
        for half in range(2):
            mine = pick(masks[half], ag)
            prob = p_ref[2 * pair + half]
            prob32 = prob.astype(F32)
            grad_prob = dot_back(mine, v)
            dv = dot_rows(prob, mine)
            row_term = jnp.sum(grad_prob * prob32, -1, keepdims=True)
            score_grad = (prob32 * (grad_prob - row_term)).astype(BF16)
            dq = dot(score_grad, pick(masks[half], k))
            dk = dot_rows(score_grad, pick(masks[half], q))
            q_grad = dq if q_grad is None else q_grad + dq
            k_grad = dk if k_grad is None else k_grad + dk
            v_grad = dv if v_grad is None else v_grad + dv
        qkv_grad_ref[:, lo : lo + LANES] = (q_grad * HEAD_DIM ** (-0.5)).astype(BF16)
        qkv_grad_ref[:, width + lo : width + lo + LANES] = k_grad.astype(BF16)
        qkv_grad_ref[:, 2 * width + lo : 2 * width + lo + LANES] = v_grad.astype(BF16)
    unit, inverse = normalize(x)
    normed = (unit * vec(GAIN_ONE) + vec(OFFSET_ONE)).astype(BF16)
    put.w_qkv(dot_rows(normed, qkv_grad_ref[...]))
    grad_normed = dot_back(qkv_grad_ref[...], w_qkv())
    grad_x = grad_hidden + norm_backward(grad_normed * vec(GAIN_ONE), unit, inverse)
    sums = jnp.concatenate(
        [
            total(qkv_grad_ref[:, :width].astype(F32)),
            total(qkv_grad_ref[:, 2 * width :].astype(F32)),
            total(grad_hidden),
            total(grad),
            total(grad_normed * unit),
            total(grad_normed),
            total(grad_normed_two * unit_two),
            total(grad_normed_two),
        ],
        0,
    )
    put.vectors(sums, jnp.concatenate(sums_up, 1))
    return grad_x


ROWS = 96
HALF = 48
UP0, QKV0, OUT0, DOWN0, VEC0, PACKED = 0, 1536, 2688, 3072, 4608, 4736
QUARTER = 1152
PIECE_IN = QUARTER + LANES
PIECE = 1280
SEQ_ROWS = 208


def positions():
    return lax.axis_index("section"), lax.axis_index("shard"), lax.axis_index("replica")


class PackedPut:
    def __init__(self, grads, shard, replica):
        self.grads, self.shard, self.replica = grads, shard, replica

    def store(self, owner, column, value, row=0):
        place = lax.rem(owner - self.shard + 4, 4)
        rows, columns = value.shape
        value = value.astype(BF16)
        while columns:
            piece, inside = column // PIECE, column % PIECE
            count = min(columns, PIECE - inside)
            where = lax.bitwise_xor(self.replica, piece)
            for half in range(2):
                lo, hi = max(row, half * HALF), min(row + rows, half * HALF + HALF)
                if lo < hi:
                    self.grads[half, where, place, lo - half * HALF : hi - half * HALF, inside : inside + count] = (
                        value[lo - row : hi - row, :count]
                    )
            value, column, columns = value[:, count:], column + count, columns - count

    def by_rows(self, column, value):
        for owner in range(4):
            self.store(owner, column, value[owner * ROWS : (owner + 1) * ROWS])

    def w_up(self, lo, value):
        self.by_rows(UP0 + lo, value)

    def w_qkv(self, value):
        self.by_rows(QKV0, value)

    def w_out(self, value):
        self.by_rows(OUT0, value)

    def w_down(self, lo, value):
        rows, at = value.shape[0], 0
        while at < rows:
            owner, inside = divmod(lo + at, 4 * ROWS)
            fold, row = divmod(inside, ROWS)
            count = min(rows - at, ROWS - row)
            self.store(owner, DOWN0 + fold * value.shape[1], value[at : at + count], row)
            at += count

    def vectors(self, sums, bias_up):
        place3 = lax.bitwise_xor(self.replica, 3)
        first = VEC0 - 3 * PIECE
        self.grads[:, place3, :, :, first:] = jnp.zeros((2, 4, HALF, PIECE - first), BF16)
        blank = jnp.zeros((8, LANES - ROWS), F32)
        rest = jnp.zeros((5, LANES), F32)
        for owner in range(4):
            up = [
                bias_up[:, owner * 384 + k * LANES : owner * 384 + (k + 1) * LANES] for k in range(3)
            ]
            top = jnp.concatenate([sums[:, owner * ROWS : (owner + 1) * ROWS], blank], 1)
            tile = jnp.concatenate([top] + up + [rest], 0)
            self.store(owner, VEC0, tile)


def packed_weights(packed, down, layer):
    def w_qkv():
        return packed[layer, :, :, QKV0:OUT0].reshape(4 * ROWS, OUT0 - QKV0)

    def w_out():
        return packed[layer, :, :, OUT0:DOWN0].reshape(4 * ROWS, DOWN0 - OUT0)

    def w_up(lo, step):
        return packed[layer, :, :, UP0 + lo : UP0 + lo + step].reshape(4 * ROWS, step)

    def w_down(lo, step):
        return down[layer, lo : lo + step]

    return w_qkv, w_out, w_up, w_down


def unfold(packed, down, vectors, biases, layer):
    width = down.shape[2]
    for owner in range(4):
        for fold in range(4):
            at = (owner * 4 + fold) * ROWS
            down[layer, at : at + ROWS] = packed[
                layer, owner, :, DOWN0 + fold * width : DOWN0 + (fold + 1) * width
            ]
    tiles = [
        packed[layer, owner, 0:16, VEC0:PACKED].astype(F32)
        + packed[layer, owner, 16:32, VEC0:PACKED].astype(F32)
        for owner in range(4)
    ]
    vectors[layer] = jnp.concatenate([tile[0:8, 0:ROWS] for tile in tiles], 1)
    biases[layer] = jnp.concatenate([tile[8 + k : 9 + k] for tile in tiles for k in range(3)], 1)


def start_copies(pieces, packed, layer, sems, shard, replica):
    own, tiles, near, far, x_near, x_far, y_near, y_far, d_first, d_third, d_far = pieces
    copies = [(own, packed.at[layer, shard])]
    for index, step in enumerate((1, 3, 2)):
        owner = packed.at[layer, lax.rem(shard + 4 - step, 4)]
        copies.append((tiles.at[index], owner.at[:, pl.ds(VEC0, LANES)]))
    groups = (
        (0, near.at[0], near.at[1], far),
        (1, x_near.at[0], x_near.at[1], x_far),
        (2, y_near.at[0], y_near.at[1], y_far),
        (3, d_first, d_third, d_far),
    )
    for bits, first, third, second in groups:
        column = pl.multiple_of(lax.bitwise_xor(replica, bits) * QUARTER, LANES)
        for step, piece in ((1, first), (3, third), (2, second)):
            owner = packed.at[layer, lax.rem(shard + 4 - step, 4)]
            copies.append((piece, owner.at[:, pl.ds(column, QUARTER)]))
    return [
        pltpu.make_async_copy(source, target, sems.at[layer, index])
        for index, (source, target) in enumerate(copies)
    ]


def main_kernel(seq, *refs):
    mine, other = refs[0:11], refs[11:22]
    patches, cotangent, live = refs[22:25]
    refs = refs[25:]
    (
        out_one,
        out_two,
        grad_one,
        keep,
        send,
        kept_weights,
        kept_vectors,
    ) = refs[0:7]
    kept_acts = refs[7:13]
    (
        packed,
        down,
        vectors,
        biases,
        rows_in,
        rows_mid,
        up_grad,
        qkv_grad,
        grads,
        sems,
        out_sems,
    ) = refs[13:24]
    acts0, acts1 = refs[24:30], refs[30:36]
    section, shard, replica = positions()
    for copy in start_copies(mine, packed, section, sems, shard, replica):
        copy.start()
    for copy in start_copies(other, packed, 1 - section, sems, shard, replica):
        copy.start()
    width = rows_in.shape[1]
    rows_in[seq - seq % 8 :] = jnp.zeros((SEQ_ROWS - seq + seq % 8, width), F32)
    rows_in[:seq] = patches[section].astype(F32)

    def ready(layer):
        for copy in start_copies(mine, packed, layer, sems, shard, replica):
            copy.wait()
        unfold(packed, down, vectors, biases, layer)
        vec = lambda index: vectors[layer, index : index + 1]
        bias_up = lambda lo, step: biases[layer, :, lo : lo + step]
        return packed_weights(packed, down, layer), vec, bias_up

    weights0, vec0, bias_up0 = ready(0)
    save = [
        pltpu.make_async_copy(packed.at[0], kept_weights.at[0], out_sems.at[0]),
    ]
    for copy in save:
        copy.start()
    kept_vectors[...] = vectors[0]
    x0 = rows_in[...]
    result = layer_forward(x0, seq, weights0, vec0, bias_up0, acts0)
    for index in range(6):
        save.append(pltpu.make_async_copy(acts0[index], kept_acts[index], out_sems.at[3 + index]))
        save[-1].start()
    out_one[...] = result[:seq].astype(BF16)
    live_rows = lax.broadcasted_iota(jnp.int32, (SEQ_ROWS, width), 0) < seq
    rows_mid[...] = jnp.where(live_rows, result.astype(BF16).astype(F32), 0.0)

    weights1, vec1, bias_up1 = ready(1)
    result = layer_forward(rows_mid[...], seq, weights1, vec1, bias_up1, acts1)
    out_two[...] = result[:seq].astype(BF16)

    rows_in[:seq] = cotangent[section].astype(F32) * live[section].astype(F32)
    put = PackedPut(grads, shard, replica)
    grad_x = layer_backward(
        rows_in[...], rows_mid[...], weights1, vec1, acts1, up_grad, qkv_grad, put
    )
    grad_one[...] = grad_x[:seq].astype(BF16)
    copies = [
        pltpu.make_async_copy(grads.at[section], keep, out_sems.at[1]),
        pltpu.make_async_copy(grads.at[1 - section], send, out_sems.at[2]),
    ]
    for copy in copies:
        copy.start()
    for copy in save + copies:
        copy.wait()


def last_kernel(seq, *refs):
    weights, vectors_in, grad_one, patches = refs[0:4]
    saved = refs[4:10]
    grad_out, keep, send = refs[10:13]
    packed, down, rows_in, rows_grad, up_grad, qkv_grad, grads, sems, out_sems = refs[13:22]
    acts = refs[22:28]
    section, shard, replica = positions()
    loads = [pltpu.make_async_copy(weights, packed, sems.at[6])]
    for index in range(6):
        loads.append(pltpu.make_async_copy(saved[index], acts[index], sems.at[index]))
    for load in loads:
        load.start()
    width = rows_in.shape[1]
    for buffer, source in ((rows_in, patches[section]), (rows_grad, grad_one[...])):
        buffer[seq - seq % 8 :] = jnp.zeros((SEQ_ROWS - seq + seq % 8, width), F32)
        buffer[:seq] = source.astype(F32)
    for load in loads:
        load.wait()
    for owner in range(4):
        for fold in range(4):
            at = (owner * 4 + fold) * ROWS
            down[0, at : at + ROWS] = packed[
                0, owner, :, DOWN0 + fold * width : DOWN0 + (fold + 1) * width
            ]
    vec = lambda index: vectors_in[index : index + 1]
    put = PackedPut(grads, shard, replica)
    grad_x = layer_backward(
        rows_grad[...],
        rows_in[...],
        packed_weights(packed, down, 0),
        vec,
        acts,
        up_grad,
        qkv_grad,
        put,
    )
    grad_out[...] = grad_x[:seq]
    copies = [
        pltpu.make_async_copy(grads.at[section], keep, out_sems.at[0]),
        pltpu.make_async_copy(grads.at[1 - section], send, out_sems.at[1]),
    ]
    for copy in copies:
        copy.start()
    for copy in copies:
        copy.wait()


def vmem(count):
    return [pl.BlockSpec(memory_space=pltpu.VMEM)] * count


def anywhere(count):
    return [pl.BlockSpec(memory_space=pl.ANY)] * count


def shape(dims, dtype):
    return jax.ShapeDtypeStruct(dims, dtype)


def act_shapes(width, wide):
    heads = width // HEAD_DIM
    return [
        ((SEQ_ROWS, 3 * width), BF16),
        ((heads, SEQ_ROWS, SEQ_ROWS), BF16),
        ((SEQ_ROWS, width), BF16),
        ((SEQ_ROWS, width), F32),
        ((SEQ_ROWS, wide), BF16),
        ((SEQ_ROWS, wide), BF16),
    ]


def grant(mib):
    return pltpu.CompilerParams(vmem_limit_bytes=mib * MIB)


def run_main(mine, other, patches, cotangent, live, wide):
    seq, width = patches.shape[1:]
    acts = act_shapes(width, wide)
    return pl.pallas_call(
        functools.partial(main_kernel, seq),
        out_shape=[
            shape((seq, width), BF16),
            shape((seq, width), BF16),
            shape((seq, width), BF16),
            shape((4, 4, HALF, PIECE), BF16),
            shape((4, 4, HALF, PIECE), BF16),
            shape((1, 4, ROWS, PACKED), BF16),
            shape((8, width), F32),
        ]
        + [shape(*a) for a in acts],
        in_specs=anywhere(22) + vmem(2) + [pl.BlockSpec(memory_space=pltpu.SMEM)],
        out_specs=vmem(3) + anywhere(3) + vmem(1) + anywhere(6),
        scratch_shapes=[
            pltpu.VMEM((2, 4, ROWS, PACKED), BF16),
            pltpu.VMEM((2, wide, width), BF16),
            pltpu.VMEM((2, 8, width), F32),
            pltpu.VMEM((2, 1, wide), F32),
            pltpu.VMEM((SEQ_ROWS, width), F32),
            pltpu.VMEM((SEQ_ROWS, width), F32),
            pltpu.VMEM((SEQ_ROWS, wide), BF16),
            pltpu.VMEM((SEQ_ROWS, 3 * width), BF16),
            pltpu.VMEM((2, 4, 4, HALF, PIECE), BF16),
            pltpu.SemaphoreType.DMA((2, 16)),
            pltpu.SemaphoreType.DMA((9,)),
        ]
        + [pltpu.VMEM(*a) for a in acts + acts],
        compiler_params=grant(32),
        name="forward_and_layer_one",
    )(*mine, *other, patches, cotangent, live)


def run_last(weights, vectors, grad_one, patches, acts, wide):
    seq, width = patches.shape[1:]
    return pl.pallas_call(
        functools.partial(last_kernel, seq),
        out_shape=[
            shape((seq, width), F32),
            shape((4, 4, HALF, PIECE), BF16),
            shape((4, 4, HALF, PIECE), BF16),
        ],
        in_specs=anywhere(1) + vmem(3) + anywhere(6),
        out_specs=vmem(1) + anywhere(2),
        scratch_shapes=[
            pltpu.VMEM((1, 4, ROWS, PACKED), BF16),
            pltpu.VMEM((1, wide, width), BF16),
            pltpu.VMEM((SEQ_ROWS, width), F32),
            pltpu.VMEM((SEQ_ROWS, width), F32),
            pltpu.VMEM((SEQ_ROWS, wide), BF16),
            pltpu.VMEM((SEQ_ROWS, 3 * width), BF16),
            pltpu.VMEM((2, 4, 4, HALF, PIECE), BF16),
            pltpu.SemaphoreType.DMA((7,)),
            pltpu.SemaphoreType.DMA((2,)),
        ]
        + [pltpu.VMEM(*a) for a in act_shapes(width, wide)],
        compiler_params=grant(20),
        cost_estimate=pl.CostEstimate(flops=8_000_000_000, bytes_accessed=8_000_000, transcendentals=0),
        name="layer_zero_backward",
    )(weights, vectors, grad_one, patches, *acts)


def add(a, b):
    return a.astype(F32) + b.astype(F32)


def small_call(kernel, outs, name, *ins):
    return pl.pallas_call(
        kernel,
        out_shape=[shape(dims, BF16) for dims in outs],
        in_specs=vmem(len(ins)),
        out_specs=vmem(len(outs)),
        compiler_params=grant(12),
        name=name,
    )(*ins)


def pair_sum_kernel(keep, recv, to_x, to_y, own, x_late, y_late):
    for place in range(4):
        own[place] = add(keep[0, place], recv[0, place]).astype(BF16)
    for place in range(2):
        to_x[0, place] = add(keep[1, place], recv[1, place]).astype(BF16)
        to_x[1, place] = add(keep[3, place], recv[3, place]).astype(BF16)
        to_y[0, place] = add(keep[2, 2 + place], recv[2, 2 + place]).astype(BF16)
        to_y[1, place] = add(keep[3, 2 + place], recv[3, 2 + place]).astype(BF16)
        x_late[place] = add(keep[1, 2 + place], recv[1, 2 + place]).astype(BF16)
        y_late[place] = add(keep[2, place], recv[2, place]).astype(BF16)


def relay_kernel(late, got, out):
    for place in range(2):
        out[place] = add(late[place], got[1, place]).astype(BF16)


def plane_sum_kernel(own, got, late, one, two):
    for place, out in enumerate((one, two)):
        out[...] = (add(own[place], got[0, place]) + late[place].astype(F32)).astype(BF16)


def column_sum_kernel(a, b, c, d, out):
    out[...] = (add(a[...], b[...]) + add(c[...], d[...])).astype(BF16)


def unpack_kernel(*refs):
    zero, one = refs[:8], refs[8:16]
    (qkv, out, up, down), rest = refs[16:20], refs[20:29]
    table, sems = refs[29:]
    section, _, replica = positions()

    def copies_of(pieces):
        copies = []
        for bits in range(4):
            place = lax.bitwise_xor(replica, bits)
            for half in range(2):
                where = section if half == 0 else 1 - section
                index = 2 * bits + half
                copies.append(
                    pltpu.make_async_copy(pieces[index], table.at[place, where], sems.at[index])
                )
        return copies

    for layer, pieces in enumerate((zero, one)):

        @pl.when(section == layer)
        def _(pieces=pieces):
            for copy in copies_of(pieces):
                copy.start()
            for copy in copies_of(pieces):
                copy.wait()

    def put(target, row, column, start, count, at):
        while count:
            piece, inside = start // PIECE, start % PIECE
            some = min(count, PIECE - inside)
            for half in range(2):
                target[0, row + half * HALF : row + half * HALF + HALF, at : at + some] = table[
                    piece, half, :, inside : inside + some
                ].astype(F32)
            start, at, count = start + some, at + some, count - some

    put(up, 0, 0, UP0, QKV0 - UP0, 0)
    put(qkv, 0, 0, QKV0, OUT0 - QKV0, 0)
    put(out, 0, 0, OUT0, DOWN0 - OUT0, 0)
    width = out.shape[2]
    for fold in range(4):
        put(down, fold * ROWS, 0, DOWN0 + fold * width, width, 0)
    inside = VEC0 - 3 * PIECE
    tile = table[3, 0, 0:16, inside : inside + LANES].astype(F32)
    for index in range(8):
        rest[index][...] = tile[index : index + 1, :ROWS]
    rest[8][...] = jnp.concatenate([tile[8 + k : 9 + k] for k in range(3)], 1)


def unpack(zero, one, width, wide):
    return pl.pallas_call(
        unpack_kernel,
        out_shape=[
            shape((1, ROWS, 3 * width), F32),
            shape((1, ROWS, width), F32),
            shape((1, ROWS, wide), F32),
            shape((1, 4 * ROWS, width), F32),
        ]
        + [shape((1, ROWS), F32)] * 8
        + [shape((1, 4 * ROWS), F32)],
        in_specs=anywhere(16),
        out_specs=vmem(13),
        scratch_shapes=[
            pltpu.VMEM((4, 2, HALF, PIECE), BF16),
            pltpu.SemaphoreType.DMA((8,)),
        ],
        compiler_params=grant(16),
        name="unpack",
    )(*zero, *one)


def swap(value):
    return lax.ppermute(value, "section", [(0, 1), (1, 0)])


def flip(value, bits):
    return lax.ppermute(value, "replica", [(place, place ^ bits) for place in range(4)])


def shift(value, steps):
    return lax.ppermute(value, "shard", [(place, (place + steps) % 4) for place in range(4)])


def pack_kernel(*refs):
    sources, (own, quarter) = refs[:13], refs[13:15]
    staged, eight, bias_up, sems = refs[15:19]
    _, _, replica = positions()
    width = sources[2].shape[2]
    targets = [
        own.at[:, UP0:QKV0],
        own.at[:, QKV0:OUT0],
        own.at[:, OUT0:DOWN0],
        staged,
    ]
    targets += [eight.at[index : index + 1] for index in range(8)] + [bias_up]
    copies = [
        pltpu.make_async_copy(source.at[0] if index < 4 else source, target, sems.at[index])
        for index, (source, target) in enumerate(zip(sources, targets))
    ]
    for copy in copies:
        copy.start()
    for copy in copies:
        copy.wait()
    for fold in range(4):
        own[:, DOWN0 + fold * width : DOWN0 + (fold + 1) * width] = staged[
            fold * ROWS : (fold + 1) * ROWS
        ]
    padded = jnp.concatenate([eight[...], jnp.zeros((8, LANES - ROWS), F32)], 1)
    up = [bias_up[:, k * LANES : (k + 1) * LANES] for k in range(3)]
    tile = jnp.concatenate([padded] + up + [jnp.zeros((5, LANES), F32)], 0)
    high = tile.astype(BF16)
    low = tile - high.astype(F32)
    own[0:16, VEC0:PACKED] = high
    own[16:32, VEC0:PACKED] = low.astype(BF16)
    own[32:, VEC0:PACKED] = jnp.zeros((ROWS - 32, LANES), BF16)
    quarter[:, QUARTER:] = own[:, VEC0:PACKED]
    for place in range(4):

        @pl.when(replica == place)
        def _(place=place):
            quarter[:, :QUARTER] = own[:, place * QUARTER : (place + 1) * QUARTER]


def pack(*arrays):
    width = arrays[2].shape[2]
    return pl.pallas_call(
        pack_kernel,
        out_shape=[shape(dims, BF16) for dims in ((ROWS, PACKED), (ROWS, PIECE_IN))],
        in_specs=anywhere(13),
        out_specs=vmem(2),
        scratch_shapes=[
            pltpu.VMEM((4 * ROWS, width), BF16),
            pltpu.VMEM((8, ROWS), F32),
            pltpu.VMEM((1, 4 * ROWS), F32),
            pltpu.SemaphoreType.DMA((13,)),
        ],
        compiler_params=grant(60),
        name="pack",
    )(*arrays)


def after(value, *earlier):
    return lax.optimization_barrier((value,) + earlier)[0]


def reduce_plane(keep, send):
    half = (2,) + keep.shape[2:]
    to_x, to_y, own, x_late, y_late = small_call(
        pair_sum_kernel,
        [(2,) + half, (2,) + half, keep.shape[1:], half, half],
        "sum_of_cores",
        keep,
        swap(send),
    )
    return to_x, to_y, own, x_late, y_late


def near_kernel(first, third, near, upper, lower):
    near[0] = first[:, :QUARTER]
    near[1] = third[:, :QUARTER]
    upper[...] = first[:HALF]
    lower[...] = third[HALF:]


def far_kernel(first, third, upper, lower, far, tiles):
    far[:HALF] = upper[:, :QUARTER]
    far[HALF:] = lower[:, :QUARTER]
    tiles[0] = first[:, QUARTER:]
    tiles[1] = third[:, QUARTER:]
    tiles[2, :HALF] = upper[:, QUARTER:]
    tiles[2, HALF:] = lower[:, QUARTER:]


def exchange_plane(to_x, to_y, own, x_late, y_late, got_x, got_y):
    half, piece = x_late.shape, x_late.shape[1:]
    (y_send,) = small_call(relay_kernel, [half], "relay", y_late, got_x)
    (x_send,) = small_call(relay_kernel, [half], "relay", x_late, got_y)
    late_y, late_x = flip(y_send, 2), flip(x_send, 1)
    zero, one = small_call(plane_sum_kernel, [piece] * 2, "sum_of_plane", own[:2], got_x, late_y)
    two, three = small_call(plane_sum_kernel, [piece] * 2, "sum_of_plane", own[2:], got_y, late_x)
    column = small_call(
        column_sum_kernel,
        [piece],
        "sum_of_column",
        zero,
        shift(one, 1),
        shift(two, 2),
        shift(three, 3),
    )[0]
    return column, late_x, late_y


def spread(value):
    pieces = [value] + [flip(value, bits) for bits in (1, 2, 3)]
    return [member for piece in pieces for member in (piece, swap(piece))]


def packed_local(patches, live_slots, cotangent, w_qkv, w_out, w_up, w_down, *small):
    section, _, _ = positions()
    width, wide = w_out.shape[2], w_up.shape[2]
    bias_q, bias_v, bias_out, bias_up, bias_down, gain_one, offset_one, gain_two, offset_two = small
    vectors = (bias_q, bias_v, bias_out, bias_down, gain_one, offset_one, gain_two, offset_two)
    own, quarter = pack(w_up, w_qkv, w_out, w_down, *vectors, bias_up)
    first, third = shift(quarter, 1), shift(quarter, 3)
    half = (HALF, PIECE_IN)
    near, upper, lower = small_call(
        near_kernel, [(2, ROWS, QUARTER), half, half], "near", first, third
    )
    x_near, y_near = flip(near, 1), flip(near, 2)
    far, tiles = small_call(
        far_kernel,
        [(ROWS, QUARTER), (3, ROWS, LANES)],
        "far",
        first,
        third,
        shift(upper, 1),
        shift(lower, 3),
    )
    d_first, d_third = flip(y_near[0], 1), flip(x_near[1], 2)
    far = after(far, x_near, y_near)
    x_far, y_far, d_far = (flip(far, bits) for bits in (1, 2, 3))
    mine = [own, tiles, near, far, x_near, x_far, y_near, y_far, d_first, d_third, d_far]
    other = [swap(member) for member in mine]

    (out_one, out_two, grad_one, keep1, send1, kept, vectors, *acts) = run_main(
        mine, other, patches, cotangent, live_slots, wide
    )
    parts = reduce_plane(keep1, send1)
    got = (flip(parts[0], 1), flip(parts[1], 2))
    last = run_last(after(kept, *parts), vectors, grad_one, patches, acts, wide)
    grad_zero, keep0, send0, *got = lax.optimization_barrier((*last, *got))
    one, *_ = exchange_plane(*parts, *got)
    parts = reduce_plane(keep0, send0)
    zero, *late = exchange_plane(*parts, flip(parts[0], 1), flip(parts[1], 2))
    one = spread(after(one, *late))
    zero = spread(zero)
    grad_qkv, grad_out, grad_up, grad_down, *rest = unpack(zero, one, width, wide)

    first = section == 0
    out_send = jnp.where(first, out_two, out_one)
    out_recv = swap(out_send)
    layer_outputs = jnp.stack(
        [jnp.where(first, out_one, out_recv), jnp.where(first, out_recv, out_two)]
    )[None]
    grad_one32 = grad_one.astype(F32)
    grad_recv = swap(jnp.where(first, grad_one32, grad_zero))
    input_grads = jnp.stack(
        [jnp.where(first, grad_zero, grad_recv), jnp.where(first, grad_recv, grad_one32)]
    )[None]
    (g_q, g_v, g_o, g_d, g_g1, g_o1, g_g2, g_o2, g_up) = rest
    return (
        layer_outputs,
        input_grads,
        grad_qkv,
        grad_out,
        grad_up,
        grad_down,
        g_q,
        g_v,
        g_o,
        g_up,
        g_d,
        g_g1,
        g_o1,
        g_g2,
        g_o2,
    )


class PlainPut:
    def __init__(self, outs, layer):
        self.outs, self.layer = outs, layer

    def w_qkv(self, value):
        self.outs[0][self.layer] = value

    def w_out(self, value):
        self.outs[1][self.layer] = value

    def w_up(self, lo, value):
        self.outs[2][self.layer, :, lo : lo + value.shape[1]] = value

    def w_down(self, lo, value):
        self.outs[3][self.layer, lo : lo + value.shape[0]] = value

    def vectors(self, sums, bias_up):
        self.outs[4][self.layer] = sums
        self.outs[5][self.layer] = bias_up


def plain_kernel(seq, *refs):
    patches, cotangent, live, w_qkv, w_out, w_up, w_down, vectors, biases = refs[:9]
    out_rows, grad_rows = refs[9:11]
    grads = refs[11:17]
    rows_in, rows_mid, up_grad, qkv_grad = refs[17:21]
    acts = (refs[21:27], refs[27:33])
    section = lax.axis_index("section")
    width = rows_in.shape[1]

    def weights_of(layer):
        return (
            lambda: w_qkv[layer],
            lambda: w_out[layer],
            lambda lo, step: w_up[layer, :, lo : lo + step],
            lambda lo, step: w_down[layer, lo : lo + step],
        )

    vec_of = lambda layer: lambda index: vectors[layer, index : index + 1]
    bias_of = lambda layer: lambda lo, step: biases[layer, :, lo : lo + step]
    live_rows = lax.broadcasted_iota(jnp.int32, (SEQ_ROWS, width), 0) < seq
    rows_in[seq - seq % 8 :] = jnp.zeros((SEQ_ROWS - seq + seq % 8, width), F32)
    rows_in[:seq] = patches[section].astype(F32)
    result = layer_forward(rows_in[...], seq, weights_of(0), vec_of(0), bias_of(0), acts[0])
    out_rows[0] = result[:seq].astype(BF16)
    rows_mid[...] = jnp.where(live_rows, result.astype(BF16).astype(F32), 0.0)
    result = layer_forward(rows_mid[...], seq, weights_of(1), vec_of(1), bias_of(1), acts[1])
    out_rows[1] = result[:seq].astype(BF16)
    seed = cotangent[section].astype(F32) * live[section].astype(F32)
    blank = jnp.zeros((SEQ_ROWS - seq, width), F32)
    grad_x = layer_backward(
        jnp.concatenate([seed, blank], 0),
        rows_mid[...],
        weights_of(1),
        vec_of(1),
        acts[1],
        up_grad,
        qkv_grad,
        PlainPut(grads, 1),
    )
    grad_x = grad_x.astype(BF16).astype(F32)
    grad_rows[1] = grad_x[:seq]
    grad_x = layer_backward(
        grad_x,
        rows_in[...],
        weights_of(0),
        vec_of(0),
        acts[0],
        up_grad,
        qkv_grad,
        PlainPut(grads, 0),
    )
    grad_rows[0] = grad_x[:seq]


def plain_local(patches, live_slots, cotangent, w_qkv, w_out, w_up, w_down, *small):
    bias_q, bias_v, bias_out, bias_up, bias_down, gain_one, offset_one, gain_two, offset_two = small
    seq, width = patches.shape[1:]
    wide = w_up.shape[2]

    def whole(value):
        along = lax.all_gather(value, "shard", axis=1, tiled=True)
        return lax.all_gather(along, "section", axis=0, tiled=True)

    small = (bias_q, bias_v, bias_out, bias_down, gain_one, offset_one, gain_two, offset_two)
    vectors = whole(jnp.stack(small, 2)).transpose(0, 2, 1)
    biases = whole(bias_up)[:, None]
    acts = act_shapes(width, wide)
    out_rows, grad_rows, *grads = pl.pallas_call(
        functools.partial(plain_kernel, seq),
        out_shape=[
            shape((2, seq, width), BF16),
            shape((2, seq, width), F32),
            shape((2, width, 3 * width), F32),
            shape((2, width, width), F32),
            shape((2, width, wide), F32),
            shape((2, wide, width), F32),
            shape((2, 8, width), F32),
            shape((2, 1, wide), F32),
        ],
        in_specs=vmem(2) + [pl.BlockSpec(memory_space=pltpu.SMEM)] + vmem(6),
        out_specs=vmem(8),
        scratch_shapes=[
            pltpu.VMEM((SEQ_ROWS, width), F32),
            pltpu.VMEM((SEQ_ROWS, width), F32),
            pltpu.VMEM((SEQ_ROWS, wide), BF16),
            pltpu.VMEM((SEQ_ROWS, 3 * width), BF16),
        ]
        + [pltpu.VMEM(*a) for a in acts + acts],
        compiler_params=grant(56),
        name="both_layers",
    )(patches, cotangent, live_slots, *(whole(w) for w in (w_qkv, w_out, w_up, w_down)), vectors, biases)

    def owned(value):
        mine = lax.psum_scatter(value, "section", scatter_dimension=0, tiled=True)
        mine = lax.psum_scatter(mine.astype(BF16), "shard", scatter_dimension=1, tiled=True)
        return lax.psum(mine, "replica").astype(F32)

    grads = [owned(value) for value in grads[:4]] + [
        owned(grads[4].transpose(0, 2, 1)),
        owned(grads[5][:, 0]),
    ]
    q, v, out, down, g1, o1, g2, o2 = (grads[4][..., index] for index in range(8))

    def by_section(value):
        section = lax.axis_index("section")
        recv = swap(jnp.where(section == 0, value[1], value[0]))
        first = jnp.where(section == 0, value[0], recv)
        return jnp.stack([first, jnp.where(section == 0, recv, value[1])])[None]

    return (
        by_section(out_rows),
        by_section(grad_rows),
        *grads[:4],
        q,
        v,
        out,
        grads[5],
        down,
        g1,
        o1,
        g2,
        o2,
    )


def solution(mesh):
    slots = P(("shard", "replica"), None, None)
    matrix, vector = P("section", "shard", None), P("section", "shard")
    outs = P("section", ("shard", "replica"), None, None)
    packed = mesh.shape["shard"] == 4 and mesh.shape["replica"] == 4
    return jax.shard_map(
        packed_local if packed else plain_local,
        mesh=mesh,
        in_specs=(slots, P(("shard", "replica")), slots) + (matrix,) * 4 + (vector,) * 9,
        out_specs=(outs, outs) + (matrix,) * 4 + (vector,) * 9,
        check_vma=False,
    )
```

```python
import functools

import jax
import jax.numpy as jnp
from jax import lax
from jax.experimental import pallas as pl
from jax.experimental.pallas import tpu as pltpu
from jax.sharding import PartitionSpec as P

HEAD_DIM = 64
EPSILON = 1e-06
ROOT_HALF = 0.7071067811865476
INVERSE_ROOT_TWO_PI = 0.3989422804014327
F32 = jnp.float32
BF16 = jnp.bfloat16
LANES = 128
MIB = 1024 * 1024

BIAS_Q, BIAS_V, BIAS_OUT, BIAS_DOWN, GAIN_ONE, OFFSET_ONE, GAIN_TWO, OFFSET_TWO = range(8)


def dot(a, b):
    return lax.dot_general(a, b, (((1,), (0,)), ((), ())), preferred_element_type=F32)


def dot_back(a, b):
    return lax.dot_general(a, b, (((1,), (1,)), ((), ())), preferred_element_type=F32)


def dot_rows(a, b):
    return lax.dot_general(a, b, (((0,), (0,)), ((), ())), preferred_element_type=F32)


def normalize(values):
    row_mean = jnp.mean(values, -1, keepdims=True)
    centred = values - row_mean
    inverse = lax.rsqrt(jnp.mean(centred * centred, -1, keepdims=True) + EPSILON)
    return centred * inverse, inverse


def norm_backward(grad, unit, inverse):
    centre = jnp.mean(grad, -1, keepdims=True)
    slope = jnp.mean(grad * unit, -1, keepdims=True)
    return inverse * (grad - centre - unit * slope)


def total(values):
    return jnp.sum(values, axis=0, keepdims=True)


def head_masks(rows):
    lane = lax.broadcasted_iota(jnp.int32, (rows, LANES), 1)
    return (lane < HEAD_DIM, lane >= HEAD_DIM)


def pick(mask, value):
    return jnp.where(mask, value.astype(F32), 0.0).astype(BF16)


def layer_forward(x, seq, weights, vec, bias_up, acts):
    rows, width = x.shape
    w_qkv, w_out, w_up, w_down = weights
    qkv_ref, p_ref, attended_ref, hidden_ref, act_ref, slope_ref = acts
    unit, _ = normalize(x)
    normed = (unit * vec(GAIN_ONE) + vec(OFFSET_ONE)).astype(BF16)
    qkv = dot(normed, w_qkv())
    queries = (qkv[:, :width] + vec(BIAS_Q)).astype(BF16).astype(F32) * HEAD_DIM ** (-0.5)
    qkv_ref[:, :width] = queries.astype(BF16)
    qkv_ref[:, width : 2 * width] = qkv[:, width : 2 * width].astype(BF16)
    qkv_ref[:, 2 * width :] = (qkv[:, 2 * width :] + vec(BIAS_V)).astype(BF16)
    masks = head_masks(rows)
    key_live = lax.broadcasted_iota(jnp.int32, (rows, rows), 1) < seq
    for pair in range(width // LANES):
        lo = pair * LANES
        q = qkv_ref[:, lo : lo + LANES]
        k = qkv_ref[:, width + lo : width + lo + LANES]
        v = qkv_ref[:, 2 * width + lo : 2 * width + lo + LANES]
        gathered = None
        for half in range(2):
            scores = dot_back(pick(masks[half], q), k)
            scores = jnp.where(key_live, scores, -1e30)
            scores = jnp.exp(scores - jnp.max(scores, -1, keepdims=True))
            prob = (scores * (1.0 / jnp.sum(scores, -1, keepdims=True))).astype(BF16)
            p_ref[2 * pair + half] = prob
            part = dot(prob, pick(masks[half], v))
            gathered = part if gathered is None else gathered + part
        attended_ref[:, lo : lo + LANES] = gathered.astype(BF16)
    hidden = x + dot(attended_ref[...], w_out()) + vec(BIAS_OUT)
    hidden_ref[...] = hidden
    unit_two, _ = normalize(hidden)
    normed_two = (unit_two * vec(GAIN_TWO) + vec(OFFSET_TWO)).astype(BF16)
    output = hidden + vec(BIAS_DOWN)
    wide = act_ref.shape[1]
    step = 512
    for lo in range(0, wide, step):
        up = dot(normed_two, w_up(lo, step)) + bias_up(lo, step)
        cdf = 0.5 * (1.0 + lax.erf(up * ROOT_HALF))
        density = jnp.exp(-0.5 * up * up) * INVERSE_ROOT_TWO_PI
        act = (up * cdf).astype(BF16)
        act_ref[:, lo : lo + step] = act
        slope_ref[:, lo : lo + step] = (cdf + up * density).astype(BF16)
        output = output + dot(act, w_down(lo, step))
    return output


def layer_backward(grad, x, weights, vec, acts, up_grad_ref, qkv_grad_ref, put):
    rows, width = grad.shape
    w_qkv, w_out, w_up, w_down = weights
    qkv_ref, p_ref, attended_ref, hidden_ref, act_ref, slope_ref = acts
    wide = act_ref.shape[1]
    step = 512
    down_grad = grad.astype(BF16)
    unit_two, inverse_two = normalize(hidden_ref[...])
    normed_two = (unit_two * vec(GAIN_TWO) + vec(OFFSET_TWO)).astype(BF16)
    grad_normed_two = None
    sums_up = []
    for lo in range(0, wide, step):
        put.w_down(lo, dot_rows(act_ref[:, lo : lo + step], down_grad))
        up_grad = dot_back(down_grad, w_down(lo, step)) * slope_ref[:, lo : lo + step].astype(F32)
        up_grad = up_grad.astype(BF16)
        sums_up.append(total(up_grad.astype(F32)))
        put.w_up(lo, dot_rows(normed_two, up_grad))
        part = dot_back(up_grad, w_up(lo, step))
        grad_normed_two = part if grad_normed_two is None else grad_normed_two + part
    grad_hidden = grad + norm_backward(grad_normed_two * vec(GAIN_TWO), unit_two, inverse_two)
    out_grad = grad_hidden.astype(BF16)
    put.w_out(dot_rows(attended_ref[...], out_grad))
    attended_grad = dot_back(out_grad, w_out()).astype(BF16)
    masks = head_masks(rows)
    for pair in range(width // LANES):
        lo = pair * LANES
        q = qkv_ref[:, lo : lo + LANES]
        k = qkv_ref[:, width + lo : width + lo + LANES]
        v = qkv_ref[:, 2 * width + lo : 2 * width + lo + LANES]
        ag = attended_grad[:, lo : lo + LANES]
        q_grad = k_grad = v_grad = None
        for half in range(2):
            mine = pick(masks[half], ag)
            prob = p_ref[2 * pair + half]
            prob32 = prob.astype(F32)
            grad_prob = dot_back(mine, v)
            dv = dot_rows(prob, mine)
            row_term = jnp.sum(grad_prob * prob32, -1, keepdims=True)
            score_grad = (prob32 * (grad_prob - row_term)).astype(BF16)
            dq = dot(score_grad, pick(masks[half], k))
            dk = dot_rows(score_grad, pick(masks[half], q))
            q_grad = dq if q_grad is None else q_grad + dq
            k_grad = dk if k_grad is None else k_grad + dk
            v_grad = dv if v_grad is None else v_grad + dv
        qkv_grad_ref[:, lo : lo + LANES] = (q_grad * HEAD_DIM ** (-0.5)).astype(BF16)
        qkv_grad_ref[:, width + lo : width + lo + LANES] = k_grad.astype(BF16)
        qkv_grad_ref[:, 2 * width + lo : 2 * width + lo + LANES] = v_grad.astype(BF16)
    unit, inverse = normalize(x)
    normed = (unit * vec(GAIN_ONE) + vec(OFFSET_ONE)).astype(BF16)
    put.w_qkv(dot_rows(normed, qkv_grad_ref[...]))
    grad_normed = dot_back(qkv_grad_ref[...], w_qkv())
    grad_x = grad_hidden + norm_backward(grad_normed * vec(GAIN_ONE), unit, inverse)
    sums = jnp.concatenate(
        [
            total(qkv_grad_ref[:, :width].astype(F32)),
            total(qkv_grad_ref[:, 2 * width :].astype(F32)),
            total(grad_hidden),
            total(grad),
            total(grad_normed * unit),
            total(grad_normed),
            total(grad_normed_two * unit_two),
            total(grad_normed_two),
        ],
        0,
    )
    put.vectors(sums, jnp.concatenate(sums_up, 1))
    return grad_x


ROWS = 96
HALF = 48
UP0, QKV0, OUT0, DOWN0, VEC0, PACKED = 0, 1536, 2688, 3072, 4608, 4736
QUARTER = 1152
PIECE_IN = QUARTER + LANES
PIECE = 1280
SEQ_ROWS = 208


def positions():
    return lax.axis_index("section"), lax.axis_index("shard"), lax.axis_index("replica")


class PackedPut:
    def __init__(self, grads, shard, replica):
        self.grads, self.shard, self.replica = grads, shard, replica

    def store(self, owner, column, value, row=0):
        place = lax.rem(owner - self.shard + 4, 4)
        rows, columns = value.shape
        value = value.astype(BF16)
        while columns:
            piece, inside = column // PIECE, column % PIECE
            count = min(columns, PIECE - inside)
            where = lax.bitwise_xor(self.replica, piece)
            for half in range(2):
                lo, hi = max(row, half * HALF), min(row + rows, half * HALF + HALF)
                if lo < hi:
                    self.grads[half, where, place, lo - half * HALF : hi - half * HALF, inside : inside + count] = (
                        value[lo - row : hi - row, :count]
                    )
            value, column, columns = value[:, count:], column + count, columns - count

    def by_rows(self, column, value):
        for owner in range(4):
            self.store(owner, column, value[owner * ROWS : (owner + 1) * ROWS])

    def w_up(self, lo, value):
        self.by_rows(UP0 + lo, value)

    def w_qkv(self, value):
        self.by_rows(QKV0, value)

    def w_out(self, value):
        self.by_rows(OUT0, value)

    def w_down(self, lo, value):
        rows, at = value.shape[0], 0
        while at < rows:
            owner, inside = divmod(lo + at, 4 * ROWS)
            fold, row = divmod(inside, ROWS)
            count = min(rows - at, ROWS - row)
            self.store(owner, DOWN0 + fold * value.shape[1], value[at : at + count], row)
            at += count

    def vectors(self, sums, bias_up):
        place3 = lax.bitwise_xor(self.replica, 3)
        first = VEC0 - 3 * PIECE
        self.grads[:, place3, :, :, first:] = jnp.zeros((2, 4, HALF, PIECE - first), BF16)
        blank = jnp.zeros((8, LANES - ROWS), F32)
        rest = jnp.zeros((5, LANES), F32)
        for owner in range(4):
            up = [
                bias_up[:, owner * 384 + k * LANES : owner * 384 + (k + 1) * LANES] for k in range(3)
            ]
            top = jnp.concatenate([sums[:, owner * ROWS : (owner + 1) * ROWS], blank], 1)
            tile = jnp.concatenate([top] + up + [rest], 0)
            self.store(owner, VEC0, tile)


def packed_weights(packed, down, layer):
    def w_qkv():
        return packed[layer, :, :, QKV0:OUT0].reshape(4 * ROWS, OUT0 - QKV0)

    def w_out():
        return packed[layer, :, :, OUT0:DOWN0].reshape(4 * ROWS, DOWN0 - OUT0)

    def w_up(lo, step):
        return packed[layer, :, :, UP0 + lo : UP0 + lo + step].reshape(4 * ROWS, step)

    def w_down(lo, step):
        return down[layer, lo : lo + step]

    return w_qkv, w_out, w_up, w_down


def unfold(packed, down, vectors, biases, layer):
    width = down.shape[2]
    for owner in range(4):
        for fold in range(4):
            at = (owner * 4 + fold) * ROWS
            down[layer, at : at + ROWS] = packed[
                layer, owner, :, DOWN0 + fold * width : DOWN0 + (fold + 1) * width
            ]
    tiles = [
        packed[layer, owner, 0:16, VEC0:PACKED].astype(F32)
        + packed[layer, owner, 16:32, VEC0:PACKED].astype(F32)
        for owner in range(4)
    ]
    vectors[layer] = jnp.concatenate([tile[0:8, 0:ROWS] for tile in tiles], 1)
    biases[layer] = jnp.concatenate([tile[8 + k : 9 + k] for tile in tiles for k in range(3)], 1)


def start_copies(pieces, packed, layer, sems, shard, replica):
    own, tiles, near, far, x_near, x_far, y_near, y_far, d_first, d_third, d_far = pieces
    copies = [(own, packed.at[layer, shard])]
    for index, step in enumerate((1, 3, 2)):
        owner = packed.at[layer, lax.rem(shard + 4 - step, 4)]
        copies.append((tiles.at[index], owner.at[:, pl.ds(VEC0, LANES)]))
    groups = (
        (0, near.at[0], near.at[1], far),
        (1, x_near.at[0], x_near.at[1], x_far),
        (2, y_near.at[0], y_near.at[1], y_far),
        (3, d_first, d_third, d_far),
    )
    for bits, first, third, second in groups:
        column = pl.multiple_of(lax.bitwise_xor(replica, bits) * QUARTER, LANES)
        for step, piece in ((1, first), (3, third), (2, second)):
            owner = packed.at[layer, lax.rem(shard + 4 - step, 4)]
            copies.append((piece, owner.at[:, pl.ds(column, QUARTER)]))
    return [
        pltpu.make_async_copy(source, target, sems.at[layer, index])
        for index, (source, target) in enumerate(copies)
    ]


def main_kernel(seq, *refs):
    mine, other = refs[0:11], refs[11:22]
    patches, cotangent, live = refs[22:25]
    refs = refs[25:]
    (
        out_mine,
        out_other,
        grad_one,
        keep,
        send,
        kept_weights,
        kept_vectors,
    ) = refs[0:7]
    kept_acts = refs[7:13]
    (
        packed,
        down,
        vectors,
        biases,
        rows_in,
        rows_mid,
        up_grad,
        qkv_grad,
        grads,
        sems,
        out_sems,
    ) = refs[13:24]
    acts0, acts1 = refs[24:30], refs[30:36]
    section, shard, replica = positions()
    for copy in start_copies(mine, packed, section, sems, shard, replica):
        copy.start()
    for copy in start_copies(other, packed, 1 - section, sems, shard, replica):
        copy.start()
    width = rows_in.shape[1]
    rows_in[seq - seq % 8 :] = jnp.zeros((SEQ_ROWS - seq + seq % 8, width), F32)
    rows_in[:seq] = patches[section].astype(F32)

    def ready(layer):
        for copy in start_copies(mine, packed, layer, sems, shard, replica):
            copy.wait()
        unfold(packed, down, vectors, biases, layer)
        vec = lambda index: vectors[layer, index : index + 1]
        bias_up = lambda lo, step: biases[layer, :, lo : lo + step]
        return packed_weights(packed, down, layer), vec, bias_up

    weights0, vec0, bias_up0 = ready(0)
    save = [
        pltpu.make_async_copy(packed.at[0], kept_weights.at[0], out_sems.at[0]),
    ]
    for copy in save:
        copy.start()
    kept_vectors[...] = vectors[0]
    x0 = rows_in[...]
    result = layer_forward(x0, seq, weights0, vec0, bias_up0, acts0)
    for index in range(6):
        save.append(pltpu.make_async_copy(acts0[index], kept_acts[index], out_sems.at[3 + index]))
        save[-1].start()
    live_rows = lax.broadcasted_iota(jnp.int32, (SEQ_ROWS, width), 0) < seq
    rows_mid[...] = jnp.where(live_rows, result.astype(BF16).astype(F32), 0.0)

    @pl.when(section == 0)
    def _():
        out_mine[...] = rows_mid[:seq].astype(BF16)

    @pl.when(section == 1)
    def _():
        out_other[...] = rows_mid[:seq].astype(BF16)

    weights1, vec1, bias_up1 = ready(1)
    result = layer_forward(rows_mid[...], seq, weights1, vec1, bias_up1, acts1)
    rows_in[...] = result

    @pl.when(section == 1)
    def _():
        out_mine[...] = rows_in[:seq].astype(BF16)

    @pl.when(section == 0)
    def _():
        out_other[...] = rows_in[:seq].astype(BF16)

    rows_in[seq - seq % 8 :] = jnp.zeros((SEQ_ROWS - seq + seq % 8, width), F32)
    rows_in[:seq] = cotangent[section].astype(F32) * live[section].astype(F32)
    put = PackedPut(grads, shard, replica)
    grad_x = layer_backward(
        rows_in[...], rows_mid[...], weights1, vec1, acts1, up_grad, qkv_grad, put
    )
    grad_one[...] = grad_x[:seq].astype(BF16)
    copies = [
        pltpu.make_async_copy(grads.at[section], keep, out_sems.at[1]),
        pltpu.make_async_copy(grads.at[1 - section], send, out_sems.at[2]),
    ]
    for copy in copies:
        copy.start()
    for copy in save + copies:
        copy.wait()


def last_kernel(seq, *refs):
    weights, vectors_in, grad_one, patches = refs[0:4]
    saved = refs[4:10]
    grad_mine, grad_other, keep, send = refs[10:14]
    packed, down, rows_in, rows_grad, up_grad, qkv_grad, grads, sems, out_sems = refs[14:23]
    acts = refs[23:29]
    section, shard, replica = positions()
    loads = [pltpu.make_async_copy(weights, packed, sems.at[6])]
    for index in range(6):
        loads.append(pltpu.make_async_copy(saved[index], acts[index], sems.at[index]))
    for load in loads:
        load.start()
    width = rows_in.shape[1]
    for buffer, source in ((rows_in, patches[section]), (rows_grad, grad_one[...])):
        buffer[seq - seq % 8 :] = jnp.zeros((SEQ_ROWS - seq + seq % 8, width), F32)
        buffer[:seq] = source.astype(F32)
    for load in loads:
        load.wait()
    for owner in range(4):
        for fold in range(4):
            at = (owner * 4 + fold) * ROWS
            down[0, at : at + ROWS] = packed[
                0, owner, :, DOWN0 + fold * width : DOWN0 + (fold + 1) * width
            ]
    vec = lambda index: vectors_in[index : index + 1]
    put = PackedPut(grads, shard, replica)
    grad_x = layer_backward(
        rows_grad[...],
        rows_in[...],
        packed_weights(packed, down, 0),
        vec,
        acts,
        up_grad,
        qkv_grad,
        put,
    )
    copies = [
        pltpu.make_async_copy(grads.at[section], keep, out_sems.at[0]),
        pltpu.make_async_copy(grads.at[1 - section], send, out_sems.at[1]),
    ]
    for copy in copies:
        copy.start()
    rows_in[...] = grad_x

    @pl.when(section == 0)
    def _():
        grad_mine[...] = rows_in[:seq]
        grad_other[...] = grad_one[...].astype(F32)

    @pl.when(section == 1)
    def _():
        grad_mine[...] = grad_one[...].astype(F32)
        grad_other[...] = rows_in[:seq]

    for copy in copies:
        copy.wait()


def vmem(count):
    return [pl.BlockSpec(memory_space=pltpu.VMEM)] * count


def anywhere(count):
    return [pl.BlockSpec(memory_space=pl.ANY)] * count


def shape(dims, dtype):
    return jax.ShapeDtypeStruct(dims, dtype)


def act_shapes(width, wide):
    heads = width // HEAD_DIM
    return [
        ((SEQ_ROWS, 3 * width), BF16),
        ((heads, SEQ_ROWS, SEQ_ROWS), BF16),
        ((SEQ_ROWS, width), BF16),
        ((SEQ_ROWS, width), F32),
        ((SEQ_ROWS, wide), BF16),
        ((SEQ_ROWS, wide), BF16),
    ]


def grant(mib):
    return pltpu.CompilerParams(vmem_limit_bytes=mib * MIB)


def run_main(mine, other, patches, cotangent, live, wide):
    seq, width = patches.shape[1:]
    acts = act_shapes(width, wide)
    return pl.pallas_call(
        functools.partial(main_kernel, seq),
        out_shape=[
            shape((seq, width), BF16),
            shape((seq, width), BF16),
            shape((seq, width), BF16),
            shape((4, 4, HALF, PIECE), BF16),
            shape((4, 4, HALF, PIECE), BF16),
            shape((1, 4, ROWS, PACKED), BF16),
            shape((8, width), F32),
        ]
        + [shape(*a) for a in acts],
        in_specs=anywhere(22) + vmem(2) + [pl.BlockSpec(memory_space=pltpu.SMEM)],
        out_specs=vmem(3) + anywhere(3) + vmem(1) + anywhere(6),
        scratch_shapes=[
            pltpu.VMEM((2, 4, ROWS, PACKED), BF16),
            pltpu.VMEM((2, wide, width), BF16),
            pltpu.VMEM((2, 8, width), F32),
            pltpu.VMEM((2, 1, wide), F32),
            pltpu.VMEM((SEQ_ROWS, width), F32),
            pltpu.VMEM((SEQ_ROWS, width), F32),
            pltpu.VMEM((SEQ_ROWS, wide), BF16),
            pltpu.VMEM((SEQ_ROWS, 3 * width), BF16),
            pltpu.VMEM((2, 4, 4, HALF, PIECE), BF16),
            pltpu.SemaphoreType.DMA((2, 16)),
            pltpu.SemaphoreType.DMA((9,)),
        ]
        + [pltpu.VMEM(*a) for a in acts + acts],
        compiler_params=grant(32),
        name="forward_and_layer_one",
    )(*mine, *other, patches, cotangent, live)


def run_last(weights, vectors, grad_one, patches, acts, wide):
    seq, width = patches.shape[1:]
    return pl.pallas_call(
        functools.partial(last_kernel, seq),
        out_shape=[
            shape((seq, width), F32),
            shape((seq, width), F32),
            shape((4, 4, HALF, PIECE), BF16),
            shape((4, 4, HALF, PIECE), BF16),
        ],
        in_specs=anywhere(1) + vmem(3) + anywhere(6),
        out_specs=vmem(2) + anywhere(2),
        scratch_shapes=[
            pltpu.VMEM((1, 4, ROWS, PACKED), BF16),
            pltpu.VMEM((1, wide, width), BF16),
            pltpu.VMEM((SEQ_ROWS, width), F32),
            pltpu.VMEM((SEQ_ROWS, width), F32),
            pltpu.VMEM((SEQ_ROWS, wide), BF16),
            pltpu.VMEM((SEQ_ROWS, 3 * width), BF16),
            pltpu.VMEM((2, 4, 4, HALF, PIECE), BF16),
            pltpu.SemaphoreType.DMA((7,)),
            pltpu.SemaphoreType.DMA((2,)),
        ]
        + [pltpu.VMEM(*a) for a in act_shapes(width, wide)],
        compiler_params=grant(20),
        cost_estimate=pl.CostEstimate(flops=8_000_000_000, bytes_accessed=8_000_000, transcendentals=0),
        name="layer_zero_backward",
    )(weights, vectors, grad_one, patches, *acts)


def add(a, b):
    return a.astype(F32) + b.astype(F32)


def small_call(kernel, outs, name, *ins):
    return pl.pallas_call(
        kernel,
        out_shape=[shape(dims, BF16) for dims in outs],
        in_specs=vmem(len(ins)),
        out_specs=vmem(len(outs)),
        compiler_params=grant(12),
        name=name,
    )(*ins)


def pair_sum_kernel(keep, recv, to_x, to_y, own, x_late, y_late):
    for place in range(4):
        own[place] = add(keep[0, place], recv[0, place]).astype(BF16)
    for place in range(2):
        to_x[0, place] = add(keep[1, place], recv[1, place]).astype(BF16)
        to_x[1, place] = add(keep[3, place], recv[3, place]).astype(BF16)
        to_y[0, place] = add(keep[2, 2 + place], recv[2, 2 + place]).astype(BF16)
        to_y[1, place] = add(keep[3, 2 + place], recv[3, 2 + place]).astype(BF16)
        x_late[place] = add(keep[1, 2 + place], recv[1, 2 + place]).astype(BF16)
        y_late[place] = add(keep[2, place], recv[2, place]).astype(BF16)


def whole_sum_kernel(keep, recv, to_x, to_y, own, opposite):
    for place in range(4):
        own[place] = add(keep[0, place], recv[0, place]).astype(BF16)
        to_x[place] = add(keep[1, place], recv[1, place]).astype(BF16)
        to_y[place] = add(keep[2, place], recv[2, place]).astype(BF16)
        opposite[place] = add(keep[3, place], recv[3, place]).astype(BF16)


def whole_plane_kernel(own, got_x, got_y, opposite, out):
    shard = lax.axis_index("shard")
    for place in range(4):
        owner = lax.rem(shard + place, 4)
        value = add(own[place], got_x[place]) + got_y[place].astype(F32)
        out[owner, 0] = value.astype(BF16)
        out[owner, 1] = opposite[place]


def pair_column_kernel(parts, out):
    for index in range(2):
        value = add(parts[0, index], parts[1, index]) + add(parts[2, index], parts[3, index])
        out[index] = value.astype(BF16)


def join_kernel(*refs):
    pieces, outs = refs[:8], refs[8:]
    for bits in range(4):
        for half in range(2):
            value = add(pieces[2 * bits + half][0], pieces[2 * (3 - bits) + half][1])
            outs[2 * bits + half][...] = value.astype(BF16)


def relay_kernel(late, got, out):
    for place in range(2):
        out[place] = add(late[place], got[1, place]).astype(BF16)


def plane_sum_kernel(own, got_x, got_y, late_y, late_x, out):
    shard = lax.axis_index("shard")
    for first, got, late in ((0, got_x, late_y), (2, got_y, late_x)):
        for place in range(2):
            value = add(own[first + place], got[0, place]) + late[place].astype(F32)
            out[lax.rem(shard + first + place, 4)] = value.astype(BF16)


def column_sum_kernel(parts, out):
    out[...] = (add(parts[0], parts[1]) + add(parts[2], parts[3])).astype(BF16)


def unpack_kernel(*refs):
    zero, one = refs[:8], refs[8:16]
    (qkv, out, up, down), rest = refs[16:20], refs[20:29]
    table, sems = refs[29:]
    section, _, replica = positions()

    def copies_of(pieces, target):
        copies = []
        for bits in range(4):
            place = lax.bitwise_xor(replica, bits)
            for half in range(2):
                where = section if half == 0 else 1 - section
                index = 2 * bits + half
                copies.append(
                    pltpu.make_async_copy(pieces[index], target.at[place, where], sems.at[index])
                )
        return copies

    for layer, pieces in enumerate((zero, one)):

        @pl.when(section == layer)
        def _(pieces=pieces):
            for copy in copies_of(pieces, table):
                copy.start()
            for copy in copies_of(pieces, table):
                copy.wait()

    def put(target, row, column, start, count, at):
        while count:
            piece, inside = start // PIECE, start % PIECE
            some = min(count, PIECE - inside)
            for half in range(2):
                target[0, row + half * HALF : row + half * HALF + HALF, at : at + some] = table[
                    piece, half, :, inside : inside + some
                ].astype(F32)
            start, at, count = start + some, at + some, count - some

    put(up, 0, 0, UP0, QKV0 - UP0, 0)
    put(qkv, 0, 0, QKV0, OUT0 - QKV0, 0)
    put(out, 0, 0, OUT0, DOWN0 - OUT0, 0)
    width = out.shape[2]
    for fold in range(4):
        put(down, fold * ROWS, 0, DOWN0 + fold * width, width, 0)
    inside = VEC0 - 3 * PIECE
    tile = table[3, 0, 0:16, inside : inside + LANES].astype(F32)
    for index in range(8):
        rest[index][...] = tile[index : index + 1, :ROWS]
    rest[8][...] = jnp.concatenate([tile[8 + k : 9 + k] for k in range(3)], 1)


def unpack(zero, one, width, wide):
    return pl.pallas_call(
        unpack_kernel,
        out_shape=[
            shape((1, ROWS, 3 * width), F32),
            shape((1, ROWS, width), F32),
            shape((1, ROWS, wide), F32),
            shape((1, 4 * ROWS, width), F32),
        ]
        + [shape((1, ROWS), F32)] * 8
        + [shape((1, 4 * ROWS), F32)],
        in_specs=anywhere(16),
        out_specs=vmem(13),
        scratch_shapes=[
            pltpu.VMEM((4, 2, HALF, PIECE), BF16),
            pltpu.SemaphoreType.DMA((8,)),
        ],
        compiler_params=grant(16),
        name="unpack",
    )(*zero, *one)


def swap(value):
    return lax.ppermute(value, "section", [(0, 1), (1, 0)])


def flip(value, bits):
    return lax.ppermute(value, "replica", [(place, place ^ bits) for place in range(4)])


def shift(value, steps):
    return lax.ppermute(value, "shard", [(place, (place + steps) % 4) for place in range(4)])


def pack_kernel(*refs):
    sources, (own, quarter) = refs[:13], refs[13:15]
    staged, eight, bias_up, sems = refs[15:19]
    _, _, replica = positions()
    width = sources[2].shape[2]
    targets = [
        own.at[:, UP0:QKV0],
        own.at[:, QKV0:OUT0],
        own.at[:, OUT0:DOWN0],
        staged,
    ]
    targets += [eight.at[index : index + 1] for index in range(8)] + [bias_up]
    copies = [
        pltpu.make_async_copy(source.at[0] if index < 4 else source, target, sems.at[index])
        for index, (source, target) in enumerate(zip(sources, targets))
    ]
    for copy in copies:
        copy.start()
    for copy in copies:
        copy.wait()
    for fold in range(4):
        own[:, DOWN0 + fold * width : DOWN0 + (fold + 1) * width] = staged[
            fold * ROWS : (fold + 1) * ROWS
        ]
    padded = jnp.concatenate([eight[...], jnp.zeros((8, LANES - ROWS), F32)], 1)
    up = [bias_up[:, k * LANES : (k + 1) * LANES] for k in range(3)]
    tile = jnp.concatenate([padded] + up + [jnp.zeros((5, LANES), F32)], 0)
    high = tile.astype(BF16)
    low = tile - high.astype(F32)
    own[0:16, VEC0:PACKED] = high
    own[16:32, VEC0:PACKED] = low.astype(BF16)
    own[32:, VEC0:PACKED] = jnp.zeros((ROWS - 32, LANES), BF16)
    quarter[:, QUARTER:] = own[:, VEC0:PACKED]
    for place in range(4):

        @pl.when(replica == place)
        def _(place=place):
            quarter[:, :QUARTER] = own[:, place * QUARTER : (place + 1) * QUARTER]


def pack(*arrays):
    width = arrays[2].shape[2]
    return pl.pallas_call(
        pack_kernel,
        out_shape=[shape(dims, BF16) for dims in ((ROWS, PACKED), (ROWS, PIECE_IN))],
        in_specs=anywhere(13),
        out_specs=vmem(2),
        scratch_shapes=[
            pltpu.VMEM((4 * ROWS, width), BF16),
            pltpu.VMEM((8, ROWS), F32),
            pltpu.VMEM((1, 4 * ROWS), F32),
            pltpu.SemaphoreType.DMA((13,)),
        ],
        compiler_params=grant(60),
        name="pack",
    )(*arrays)


def after(value, *earlier):
    return lax.optimization_barrier((value,) + earlier)[0]


def reduce_plane(keep, send):
    half = (2,) + keep.shape[2:]
    to_x, to_y, own, x_late, y_late = small_call(
        pair_sum_kernel,
        [(2,) + half, (2,) + half, keep.shape[1:], half, half],
        "sum_of_cores",
        keep,
        swap(send),
    )
    return to_x, to_y, own, x_late, y_late


def near_kernel(first, third, near, upper, lower):
    near[0] = first[:, :QUARTER]
    near[1] = third[:, :QUARTER]
    upper[...] = first[:HALF]
    lower[...] = third[HALF:]


def far_kernel(first, third, upper, lower, far, tiles):
    far[:HALF] = upper[:, :QUARTER]
    far[HALF:] = lower[:, :QUARTER]
    tiles[0] = first[:, QUARTER:]
    tiles[1] = third[:, QUARTER:]
    tiles[2, :HALF] = upper[:, QUARTER:]
    tiles[2, HALF:] = lower[:, QUARTER:]


def relay(parts, got_x, got_y):
    _, _, own, x_late, y_late = parts
    half = x_late.shape
    (y_send,) = small_call(relay_kernel, [half], "relay", y_late, got_x)
    (x_send,) = small_call(relay_kernel, [half], "relay", x_late, got_y)
    return flip(y_send, 2), flip(x_send, 1)


def sum_column(parts):
    return small_call(column_sum_kernel, [parts.shape[1:]], "sum_of_column", parts)[0]


def spread(value):
    return [value] + [flip(value, bits) for bits in (1, 2, 3)]


def both_halves(pieces):
    return [member for piece in pieces for member in (piece, swap(piece))]


def rows_kernel(out_mine, out_other, grad_mine, grad_other, outs, grads):
    section = lax.axis_index("section")
    for slot in range(2):

        @pl.when(section == slot)
        def _(slot=slot):
            outs[:, slot, :] = out_mine[...].astype(F32).astype(BF16)
            outs[:, 1 - slot, :] = out_other[...]
            grads[:, slot, :] = grad_mine[...]
            grads[:, 1 - slot, :] = grad_other[...]


def rows_of_slots(out_mine, out_other, grad_mine, grad_other):
    seq, width = out_mine.shape
    outs, grads = pl.pallas_call(
        rows_kernel,
        out_shape=[shape((seq, 2, width), BF16), shape((seq, 2, width), F32)],
        in_specs=vmem(4),
        out_specs=vmem(2),
        compiler_params=grant(12),
        name="rows_of_slots",
    )(out_mine, out_other, grad_mine, grad_other)
    return outs, grads


def packed_local(patches, live_slots, cotangent, w_qkv, w_out, w_up, w_down, *small):
    width, wide = w_out.shape[2], w_up.shape[2]
    bias_q, bias_v, bias_out, bias_up, bias_down, gain_one, offset_one, gain_two, offset_two = small
    vectors = (bias_q, bias_v, bias_out, bias_down, gain_one, offset_one, gain_two, offset_two)
    own, quarter = pack(w_up, w_qkv, w_out, w_down, *vectors, bias_up)
    first, third = shift(quarter, 1), shift(quarter, 3)
    half = (HALF, PIECE_IN)
    near, upper, lower = small_call(
        near_kernel, [(2, ROWS, QUARTER), half, half], "near", first, third
    )
    x_near, y_near = flip(near, 1), flip(near, 2)
    far, tiles = small_call(
        far_kernel,
        [(ROWS, QUARTER), (3, ROWS, LANES)],
        "far",
        first,
        third,
        shift(upper, 1),
        shift(lower, 3),
    )
    far_now, x_now, y_now = lax.optimization_barrier((far, x_near, y_near))
    x_far, y_far, d_far = (flip(far_now, bits) for bits in (1, 2, 3))
    d_first, d_third = flip(y_now[0], 1), flip(x_now[1], 2)
    mine = [own, tiles, near, far, x_near, x_far, y_near, y_far, d_first, d_third, d_far]
    other = [swap(member) for member in mine]

    (out_mine, out_other, grad_one, keep1, send1, kept, vectors, *acts) = run_main(
        mine, other, patches, cotangent, live_slots, wide
    )
    whole, piece = keep1.shape[1:], keep1.shape[2:]
    to_x, to_y, own1, opposite = small_call(
        whole_sum_kernel, [whole] * 4, "sum_of_cores", keep1, swap(send1)
    )
    got1 = (flip(to_x, 1), flip(to_y, 2))
    kept = after(kept, to_x, to_y, own1, opposite)
    last = run_last(kept, vectors, grad_one, patches, acts, wide)
    grad_mine, grad_other, keep0, send0, *got1 = lax.optimization_barrier((*last, *got1))
    (sums1,) = small_call(
        whole_plane_kernel, [(4, 2) + piece], "sum_of_plane", own1, *got1, opposite
    )
    column1 = lax.all_to_all(sums1, "shard", 0, 0, tiled=True)
    parts0 = reduce_plane(after(keep0, sums1), send0)
    got0 = (flip(parts0[0], 1), flip(parts0[1], 2))
    rows = rows_of_slots(out_mine, swap(out_other), grad_mine, swap(grad_other))
    *got0, outs, grads = lax.optimization_barrier((*got0, *rows))
    layer_outputs, input_grads = outs.transpose(1, 0, 2)[None], grads.transpose(1, 0, 2)[None]
    late0 = relay(parts0, *got0)
    (sums0,) = small_call(
        plane_sum_kernel, [parts0[2].shape], "sum_of_plane", parts0[2], *got0, *late0
    )
    column0 = lax.all_to_all(sums0, "shard", 0, 0, tiled=True)
    (one,) = small_call(
        pair_column_kernel, [(2,) + piece], "sum_of_column", after(column1, sums0)
    )
    one = spread(one)
    column0 = after(column0, *one[1:])
    zero = spread(sum_column(column0))
    one = small_call(join_kernel, [piece] * 8, "join", *both_halves(one))
    grad_qkv, grad_out, grad_up, grad_down, *rest = unpack(
        both_halves(zero), one, width, wide
    )

    (g_q, g_v, g_o, g_d, g_g1, g_o1, g_g2, g_o2, g_up) = rest
    return (
        layer_outputs,
        input_grads,
        grad_qkv,
        grad_out,
        grad_up,
        grad_down,
        g_q,
        g_v,
        g_o,
        g_up,
        g_d,
        g_g1,
        g_o1,
        g_g2,
        g_o2,
    )


class PlainPut:
    def __init__(self, outs, layer):
        self.outs, self.layer = outs, layer

    def w_qkv(self, value):
        self.outs[0][self.layer] = value

    def w_out(self, value):
        self.outs[1][self.layer] = value

    def w_up(self, lo, value):
        self.outs[2][self.layer, :, lo : lo + value.shape[1]] = value

    def w_down(self, lo, value):
        self.outs[3][self.layer, lo : lo + value.shape[0]] = value

    def vectors(self, sums, bias_up):
        self.outs[4][self.layer] = sums
        self.outs[5][self.layer] = bias_up


def plain_kernel(seq, *refs):
    patches, cotangent, live, w_qkv, w_out, w_up, w_down, vectors, biases = refs[:9]
    out_rows, grad_rows = refs[9:11]
    grads = refs[11:17]
    rows_in, rows_mid, up_grad, qkv_grad = refs[17:21]
    acts = (refs[21:27], refs[27:33])
    section = lax.axis_index("section")
    width = rows_in.shape[1]

    def weights_of(layer):
        return (
            lambda: w_qkv[layer],
            lambda: w_out[layer],
            lambda lo, step: w_up[layer, :, lo : lo + step],
            lambda lo, step: w_down[layer, lo : lo + step],
        )

    vec_of = lambda layer: lambda index: vectors[layer, index : index + 1]
    bias_of = lambda layer: lambda lo, step: biases[layer, :, lo : lo + step]
    live_rows = lax.broadcasted_iota(jnp.int32, (SEQ_ROWS, width), 0) < seq
    rows_in[seq - seq % 8 :] = jnp.zeros((SEQ_ROWS - seq + seq % 8, width), F32)
    rows_in[:seq] = patches[section].astype(F32)
    result = layer_forward(rows_in[...], seq, weights_of(0), vec_of(0), bias_of(0), acts[0])
    out_rows[0] = result[:seq].astype(BF16)
    rows_mid[...] = jnp.where(live_rows, result.astype(BF16).astype(F32), 0.0)
    result = layer_forward(rows_mid[...], seq, weights_of(1), vec_of(1), bias_of(1), acts[1])
    out_rows[1] = result[:seq].astype(BF16)
    seed = cotangent[section].astype(F32) * live[section].astype(F32)
    blank = jnp.zeros((SEQ_ROWS - seq, width), F32)
    grad_x = layer_backward(
        jnp.concatenate([seed, blank], 0),
        rows_mid[...],
        weights_of(1),
        vec_of(1),
        acts[1],
        up_grad,
        qkv_grad,
        PlainPut(grads, 1),
    )
    grad_x = grad_x.astype(BF16).astype(F32)
    grad_rows[1] = grad_x[:seq]
    grad_x = layer_backward(
        grad_x,
        rows_in[...],
        weights_of(0),
        vec_of(0),
        acts[0],
        up_grad,
        qkv_grad,
        PlainPut(grads, 0),
    )
    grad_rows[0] = grad_x[:seq]


def plain_local(patches, live_slots, cotangent, w_qkv, w_out, w_up, w_down, *small):
    bias_q, bias_v, bias_out, bias_up, bias_down, gain_one, offset_one, gain_two, offset_two = small
    seq, width = patches.shape[1:]
    wide = w_up.shape[2]

    def whole(value):
        along = lax.all_gather(value, "shard", axis=1, tiled=True)
        return lax.all_gather(along, "section", axis=0, tiled=True)

    small = (bias_q, bias_v, bias_out, bias_down, gain_one, offset_one, gain_two, offset_two)
    vectors = whole(jnp.stack(small, 2)).transpose(0, 2, 1)
    biases = whole(bias_up)[:, None]
    acts = act_shapes(width, wide)
    out_rows, grad_rows, *grads = pl.pallas_call(
        functools.partial(plain_kernel, seq),
        out_shape=[
            shape((2, seq, width), BF16),
            shape((2, seq, width), F32),
            shape((2, width, 3 * width), F32),
            shape((2, width, width), F32),
            shape((2, width, wide), F32),
            shape((2, wide, width), F32),
            shape((2, 8, width), F32),
            shape((2, 1, wide), F32),
        ],
        in_specs=vmem(2) + [pl.BlockSpec(memory_space=pltpu.SMEM)] + vmem(6),
        out_specs=vmem(8),
        scratch_shapes=[
            pltpu.VMEM((SEQ_ROWS, width), F32),
            pltpu.VMEM((SEQ_ROWS, width), F32),
            pltpu.VMEM((SEQ_ROWS, wide), BF16),
            pltpu.VMEM((SEQ_ROWS, 3 * width), BF16),
        ]
        + [pltpu.VMEM(*a) for a in acts + acts],
        compiler_params=grant(56),
        name="both_layers",
    )(patches, cotangent, live_slots, *(whole(w) for w in (w_qkv, w_out, w_up, w_down)), vectors, biases)

    def owned(value):
        mine = lax.psum_scatter(value, "section", scatter_dimension=0, tiled=True)
        mine = lax.psum_scatter(mine.astype(BF16), "shard", scatter_dimension=1, tiled=True)
        return lax.psum(mine, "replica").astype(F32)

    grads = [owned(value) for value in grads[:4]] + [
        owned(grads[4].transpose(0, 2, 1)),
        owned(grads[5][:, 0]),
    ]
    q, v, out, down, g1, o1, g2, o2 = (grads[4][..., index] for index in range(8))

    def by_section(value):
        section = lax.axis_index("section")
        recv = swap(jnp.where(section == 0, value[1], value[0]))
        first = jnp.where(section == 0, value[0], recv)
        return jnp.stack([first, jnp.where(section == 0, recv, value[1])])[None]

    return (
        by_section(out_rows),
        by_section(grad_rows),
        *grads[:4],
        q,
        v,
        out,
        grads[5],
        down,
        g1,
        o1,
        g2,
        o2,
    )


def solution(mesh):
    slots = P(("shard", "replica"), None, None)
    matrix, vector = P("section", "shard", None), P("section", "shard")
    outs = P("section", ("shard", "replica"), None, None)
    packed = mesh.shape["shard"] == 4 and mesh.shape["replica"] == 4
    return jax.shard_map(
        packed_local if packed else plain_local,
        mesh=mesh,
        in_specs=(slots, P(("shard", "replica")), slots) + (matrix,) * 4 + (vector,) * 9,
        out_specs=(outs, outs) + (matrix,) * 4 + (vector,) * 9,
        check_vma=False,
    )
```

```python
import functools

import jax
import jax.numpy as jnp
from jax import lax
from jax.experimental import pallas as pl
from jax.experimental.pallas import tpu as pltpu
from jax.sharding import PartitionSpec as P

HEAD_DIM = 64
EPSILON = 1e-06
ROOT_HALF = 0.7071067811865476
INVERSE_ROOT_TWO_PI = 0.3989422804014327
F32 = jnp.float32
BF16 = jnp.bfloat16
LANES = 128
MIB = 1024 * 1024

BIAS_Q, BIAS_V, BIAS_OUT, BIAS_DOWN, GAIN_ONE, OFFSET_ONE, GAIN_TWO, OFFSET_TWO = range(8)


def dot(a, b):
    return lax.dot_general(a, b, (((1,), (0,)), ((), ())), preferred_element_type=F32)


def dot_back(a, b):
    return lax.dot_general(a, b, (((1,), (1,)), ((), ())), preferred_element_type=F32)


def dot_rows(a, b):
    return lax.dot_general(a, b, (((0,), (0,)), ((), ())), preferred_element_type=F32)


def normalize(values):
    row_mean = jnp.mean(values, -1, keepdims=True)
    centred = values - row_mean
    inverse = lax.rsqrt(jnp.mean(centred * centred, -1, keepdims=True) + EPSILON)
    return centred * inverse, inverse


def norm_backward(grad, unit, inverse):
    centre = jnp.mean(grad, -1, keepdims=True)
    slope = jnp.mean(grad * unit, -1, keepdims=True)
    return inverse * (grad - centre - unit * slope)


def total(values):
    return jnp.sum(values, axis=0, keepdims=True)


def head_masks(rows):
    lane = lax.broadcasted_iota(jnp.int32, (rows, LANES), 1)
    return (lane < HEAD_DIM, lane >= HEAD_DIM)


def pick(mask, value):
    return jnp.where(mask, value.astype(F32), 0.0).astype(BF16)


def layer_forward(x, seq, weights, vec, bias_up, acts):
    rows, width = x.shape
    w_qkv, w_out, w_up, w_down = weights
    qkv_ref, p_ref, attended_ref, hidden_ref, act_ref, slope_ref = acts
    unit, _ = normalize(x)
    normed = (unit * vec(GAIN_ONE) + vec(OFFSET_ONE)).astype(BF16)
    qkv = dot(normed, w_qkv())
    queries = (qkv[:, :width] + vec(BIAS_Q)).astype(BF16).astype(F32) * HEAD_DIM ** (-0.5)
    qkv_ref[:, :width] = queries.astype(BF16)
    qkv_ref[:, width : 2 * width] = qkv[:, width : 2 * width].astype(BF16)
    qkv_ref[:, 2 * width :] = (qkv[:, 2 * width :] + vec(BIAS_V)).astype(BF16)
    masks = head_masks(rows)
    key_live = lax.broadcasted_iota(jnp.int32, (rows, rows), 1) < seq
    for pair in range(width // LANES):
        lo = pair * LANES
        q = qkv_ref[:, lo : lo + LANES]
        k = qkv_ref[:, width + lo : width + lo + LANES]
        v = qkv_ref[:, 2 * width + lo : 2 * width + lo + LANES]
        gathered = None
        for half in range(2):
            scores = dot_back(pick(masks[half], q), k)
            scores = jnp.where(key_live, scores, -1e30)
            scores = jnp.exp(scores - jnp.max(scores, -1, keepdims=True))
            prob = (scores * (1.0 / jnp.sum(scores, -1, keepdims=True))).astype(BF16)
            p_ref[2 * pair + half] = prob
            part = dot(prob, pick(masks[half], v))
            gathered = part if gathered is None else gathered + part
        attended_ref[:, lo : lo + LANES] = gathered.astype(BF16)
    hidden = x + dot(attended_ref[...], w_out()) + vec(BIAS_OUT)
    hidden_ref[...] = hidden
    unit_two, _ = normalize(hidden)
    normed_two = (unit_two * vec(GAIN_TWO) + vec(OFFSET_TWO)).astype(BF16)
    output = hidden + vec(BIAS_DOWN)
    wide = act_ref.shape[1]
    step = 512
    for lo in range(0, wide, step):
        up = dot(normed_two, w_up(lo, step)) + bias_up(lo, step)
        cdf = 0.5 * (1.0 + lax.erf(up * ROOT_HALF))
        density = jnp.exp(-0.5 * up * up) * INVERSE_ROOT_TWO_PI
        act = (up * cdf).astype(BF16)
        act_ref[:, lo : lo + step] = act
        slope_ref[:, lo : lo + step] = (cdf + up * density).astype(BF16)
        output = output + dot(act, w_down(lo, step))
    return output


def layer_backward(grad, x, weights, vec, acts, up_grad_ref, qkv_grad_ref, put):
    rows, width = grad.shape
    w_qkv, w_out, w_up, w_down = weights
    qkv_ref, p_ref, attended_ref, hidden_ref, act_ref, slope_ref = acts
    wide = act_ref.shape[1]
    step = 512
    down_grad = grad.astype(BF16)
    unit_two, inverse_two = normalize(hidden_ref[...])
    normed_two = (unit_two * vec(GAIN_TWO) + vec(OFFSET_TWO)).astype(BF16)
    grad_normed_two = None
    sums_up = []
    for lo in range(0, wide, step):
        put.w_down(lo, dot_rows(act_ref[:, lo : lo + step], down_grad))
        up_grad = dot_back(down_grad, w_down(lo, step)) * slope_ref[:, lo : lo + step].astype(F32)
        up_grad = up_grad.astype(BF16)
        sums_up.append(total(up_grad.astype(F32)))
        put.w_up(lo, dot_rows(normed_two, up_grad))
        part = dot_back(up_grad, w_up(lo, step))
        grad_normed_two = part if grad_normed_two is None else grad_normed_two + part
    grad_hidden = grad + norm_backward(grad_normed_two * vec(GAIN_TWO), unit_two, inverse_two)
    out_grad = grad_hidden.astype(BF16)
    put.w_out(dot_rows(attended_ref[...], out_grad))
    attended_grad = dot_back(out_grad, w_out()).astype(BF16)
    masks = head_masks(rows)
    for pair in range(width // LANES):
        lo = pair * LANES
        q = qkv_ref[:, lo : lo + LANES]
        k = qkv_ref[:, width + lo : width + lo + LANES]
        v = qkv_ref[:, 2 * width + lo : 2 * width + lo + LANES]
        ag = attended_grad[:, lo : lo + LANES]
        q_grad = k_grad = v_grad = None
        for half in range(2):
            mine = pick(masks[half], ag)
            prob = p_ref[2 * pair + half]
            prob32 = prob.astype(F32)
            grad_prob = dot_back(mine, v)
            dv = dot_rows(prob, mine)
            row_term = jnp.sum(grad_prob * prob32, -1, keepdims=True)
            score_grad = (prob32 * (grad_prob - row_term)).astype(BF16)
            dq = dot(score_grad, pick(masks[half], k))
            dk = dot_rows(score_grad, pick(masks[half], q))
            q_grad = dq if q_grad is None else q_grad + dq
            k_grad = dk if k_grad is None else k_grad + dk
            v_grad = dv if v_grad is None else v_grad + dv
        qkv_grad_ref[:, lo : lo + LANES] = (q_grad * HEAD_DIM ** (-0.5)).astype(BF16)
        qkv_grad_ref[:, width + lo : width + lo + LANES] = k_grad.astype(BF16)
        qkv_grad_ref[:, 2 * width + lo : 2 * width + lo + LANES] = v_grad.astype(BF16)
    unit, inverse = normalize(x)
    normed = (unit * vec(GAIN_ONE) + vec(OFFSET_ONE)).astype(BF16)
    put.w_qkv(dot_rows(normed, qkv_grad_ref[...]))
    grad_normed = dot_back(qkv_grad_ref[...], w_qkv())
    grad_x = grad_hidden + norm_backward(grad_normed * vec(GAIN_ONE), unit, inverse)
    sums = jnp.concatenate(
        [
            total(qkv_grad_ref[:, :width].astype(F32)),
            total(qkv_grad_ref[:, 2 * width :].astype(F32)),
            total(grad_hidden),
            total(grad),
            total(grad_normed * unit),
            total(grad_normed),
            total(grad_normed_two * unit_two),
            total(grad_normed_two),
        ],
        0,
    )
    put.vectors(sums, jnp.concatenate(sums_up, 1))
    return grad_x


ROWS = 96
HALF = 48
UP0, QKV0, OUT0, DOWN0, VEC0, PACKED = 0, 1536, 2688, 3072, 4608, 4736
QUARTER = 1152
PIECE_IN = QUARTER + LANES
PIECE = 1280
SEQ_ROWS = 208


def positions():
    return lax.axis_index("section"), lax.axis_index("shard"), lax.axis_index("replica")


class PackedPut:
    def __init__(self, grads, shard, replica):
        self.grads, self.shard, self.replica = grads, shard, replica

    def store(self, owner, column, value, row=0):
        place = lax.rem(owner - self.shard + 4, 4)
        rows, columns = value.shape
        value = value.astype(BF16)
        while columns:
            piece, inside = column // PIECE, column % PIECE
            count = min(columns, PIECE - inside)
            where = lax.bitwise_xor(self.replica, piece)
            for half in range(2):
                lo, hi = max(row, half * HALF), min(row + rows, half * HALF + HALF)
                if lo < hi:
                    self.grads[half, where, place, lo - half * HALF : hi - half * HALF, inside : inside + count] = (
                        value[lo - row : hi - row, :count]
                    )
            value, column, columns = value[:, count:], column + count, columns - count

    def by_rows(self, column, value):
        for owner in range(4):
            self.store(owner, column, value[owner * ROWS : (owner + 1) * ROWS])

    def w_up(self, lo, value):
        self.by_rows(UP0 + lo, value)

    def w_qkv(self, value):
        self.by_rows(QKV0, value)

    def w_out(self, value):
        self.by_rows(OUT0, value)

    def w_down(self, lo, value):
        rows, at = value.shape[0], 0
        while at < rows:
            owner, inside = divmod(lo + at, 4 * ROWS)
            fold, row = divmod(inside, ROWS)
            count = min(rows - at, ROWS - row)
            self.store(owner, DOWN0 + fold * value.shape[1], value[at : at + count], row)
            at += count

    def vectors(self, sums, bias_up):
        place3 = lax.bitwise_xor(self.replica, 3)
        first = VEC0 - 3 * PIECE
        self.grads[:, place3, :, :, first:] = jnp.zeros((2, 4, HALF, PIECE - first), BF16)
        blank = jnp.zeros((8, LANES - ROWS), F32)
        rest = jnp.zeros((5, LANES), F32)
        for owner in range(4):
            up = [
                bias_up[:, owner * 384 + k * LANES : owner * 384 + (k + 1) * LANES] for k in range(3)
            ]
            top = jnp.concatenate([sums[:, owner * ROWS : (owner + 1) * ROWS], blank], 1)
            tile = jnp.concatenate([top] + up + [rest], 0)
            self.store(owner, VEC0, tile)


def packed_weights(packed, down, layer):
    def w_qkv():
        return packed[layer, :, :, QKV0:OUT0].reshape(4 * ROWS, OUT0 - QKV0)

    def w_out():
        return packed[layer, :, :, OUT0:DOWN0].reshape(4 * ROWS, DOWN0 - OUT0)

    def w_up(lo, step):
        return packed[layer, :, :, UP0 + lo : UP0 + lo + step].reshape(4 * ROWS, step)

    def w_down(lo, step):
        return down[layer, lo : lo + step]

    return w_qkv, w_out, w_up, w_down


def unfold(packed, down, vectors, biases, layer):
    width = down.shape[2]
    for owner in range(4):
        for fold in range(4):
            at = (owner * 4 + fold) * ROWS
            down[layer, at : at + ROWS] = packed[
                layer, owner, :, DOWN0 + fold * width : DOWN0 + (fold + 1) * width
            ]
    tiles = [
        packed[layer, owner, 0:16, VEC0:PACKED].astype(F32)
        + packed[layer, owner, 16:32, VEC0:PACKED].astype(F32)
        for owner in range(4)
    ]
    vectors[layer] = jnp.concatenate([tile[0:8, 0:ROWS] for tile in tiles], 1)
    biases[layer] = jnp.concatenate([tile[8 + k : 9 + k] for tile in tiles for k in range(3)], 1)


def start_copies(pieces, packed, layer, sems, shard, replica):
    own, tiles, near, far, x_near, x_far, y_near, y_far, d_first, d_third, d_far = pieces
    copies = [(own, packed.at[layer, shard])]
    for index, step in enumerate((1, 3, 2)):
        owner = packed.at[layer, lax.rem(shard + 4 - step, 4)]
        copies.append((tiles.at[index], owner.at[:, pl.ds(VEC0, LANES)]))
    groups = (
        (0, near.at[0], near.at[1], far),
        (1, x_near.at[0], x_near.at[1], x_far),
        (2, y_near.at[0], y_near.at[1], y_far),
        (3, d_first, d_third, d_far),
    )
    for bits, first, third, second in groups:
        column = pl.multiple_of(lax.bitwise_xor(replica, bits) * QUARTER, LANES)
        for step, piece in ((1, first), (3, third), (2, second)):
            owner = packed.at[layer, lax.rem(shard + 4 - step, 4)]
            copies.append((piece, owner.at[:, pl.ds(column, QUARTER)]))
    return [
        pltpu.make_async_copy(source, target, sems.at[layer, index])
        for index, (source, target) in enumerate(copies)
    ]


def main_kernel(seq, *refs):
    mine, other = refs[0:11], refs[11:22]
    patches, cotangent, live = refs[22:25]
    refs = refs[25:]
    (
        out_mine,
        out_other,
        grad_one,
        keep,
        send_near,
        send_rest,
        kept_weights,
        kept_vectors,
    ) = refs[0:8]
    kept_acts = refs[8:14]
    (
        packed,
        down,
        vectors,
        biases,
        rows_in,
        rows_mid,
        up_grad,
        qkv_grad,
        grads,
        sems,
        out_sems,
    ) = refs[14:25]
    acts0, acts1 = refs[25:31], refs[31:37]
    section, shard, replica = positions()
    for copy in start_copies(mine, packed, section, sems, shard, replica):
        copy.start()
    for copy in start_copies(other, packed, 1 - section, sems, shard, replica):
        copy.start()
    width = rows_in.shape[1]
    rows_in[seq - seq % 8 :] = jnp.zeros((SEQ_ROWS - seq + seq % 8, width), F32)
    rows_in[:seq] = patches[section].astype(F32)

    def ready(layer):
        for copy in start_copies(mine, packed, layer, sems, shard, replica):
            copy.wait()
        unfold(packed, down, vectors, biases, layer)
        vec = lambda index: vectors[layer, index : index + 1]
        bias_up = lambda lo, step: biases[layer, :, lo : lo + step]
        return packed_weights(packed, down, layer), vec, bias_up

    weights0, vec0, bias_up0 = ready(0)
    save = [
        pltpu.make_async_copy(packed.at[0], kept_weights.at[0], out_sems.at[0]),
    ]
    for copy in save:
        copy.start()
    kept_vectors[...] = vectors[0]
    x0 = rows_in[...]
    result = layer_forward(x0, seq, weights0, vec0, bias_up0, acts0)
    for index in range(6):
        save.append(pltpu.make_async_copy(acts0[index], kept_acts[index], out_sems.at[3 + index]))
        save[-1].start()
    live_rows = lax.broadcasted_iota(jnp.int32, (SEQ_ROWS, width), 0) < seq
    rows_mid[...] = jnp.where(live_rows, result.astype(BF16).astype(F32), 0.0)

    @pl.when(section == 0)
    def _():
        out_mine[...] = rows_mid[:seq].astype(BF16)

    @pl.when(section == 1)
    def _():
        out_other[...] = rows_mid[:seq].astype(BF16)

    weights1, vec1, bias_up1 = ready(1)
    result = layer_forward(rows_mid[...], seq, weights1, vec1, bias_up1, acts1)
    rows_in[...] = result

    @pl.when(section == 1)
    def _():
        out_mine[...] = rows_in[:seq].astype(BF16)

    @pl.when(section == 0)
    def _():
        out_other[...] = rows_in[:seq].astype(BF16)

    rows_in[seq - seq % 8 :] = jnp.zeros((SEQ_ROWS - seq + seq % 8, width), F32)
    rows_in[:seq] = cotangent[section].astype(F32) * live[section].astype(F32)
    put = PackedPut(grads, shard, replica)
    grad_x = layer_backward(
        rows_in[...], rows_mid[...], weights1, vec1, acts1, up_grad, qkv_grad, put
    )
    grad_one[...] = grad_x[:seq].astype(BF16)
    copies = [
        pltpu.make_async_copy(grads.at[1 - section, 1:3], send_near, out_sems.at[1]),
        pltpu.make_async_copy(grads.at[section], keep, out_sems.at[2]),
        pltpu.make_async_copy(grads.at[1 - section, 0], send_rest.at[0], out_sems.at[9]),
        pltpu.make_async_copy(grads.at[1 - section, 3], send_rest.at[1], out_sems.at[10]),
    ]
    for copy in copies:
        copy.start()
    for copy in save + copies:
        copy.wait()


def last_kernel(seq, *refs):
    weights, vectors_in, grad_one, patches = refs[0:4]
    saved = refs[4:10]
    grad_mine, grad_other, keep, send = refs[10:14]
    packed, down, rows_in, rows_grad, up_grad, qkv_grad, grads, sems, out_sems = refs[14:23]
    acts = refs[23:29]
    section, shard, replica = positions()
    loads = [pltpu.make_async_copy(weights, packed, sems.at[6])]
    for index in range(6):
        loads.append(pltpu.make_async_copy(saved[index], acts[index], sems.at[index]))
    for load in loads:
        load.start()
    width = rows_in.shape[1]
    for buffer, source in ((rows_in, patches[section]), (rows_grad, grad_one[...])):
        buffer[seq - seq % 8 :] = jnp.zeros((SEQ_ROWS - seq + seq % 8, width), F32)
        buffer[:seq] = source.astype(F32)
    for load in loads:
        load.wait()
    for owner in range(4):
        for fold in range(4):
            at = (owner * 4 + fold) * ROWS
            down[0, at : at + ROWS] = packed[
                0, owner, :, DOWN0 + fold * width : DOWN0 + (fold + 1) * width
            ]
    vec = lambda index: vectors_in[index : index + 1]
    put = PackedPut(grads, shard, replica)
    grad_x = layer_backward(
        rows_grad[...],
        rows_in[...],
        packed_weights(packed, down, 0),
        vec,
        acts,
        up_grad,
        qkv_grad,
        put,
    )
    copies = [
        pltpu.make_async_copy(grads.at[section], keep, out_sems.at[0]),
        pltpu.make_async_copy(grads.at[1 - section], send, out_sems.at[1]),
    ]
    for copy in copies:
        copy.start()
    rows_in[...] = grad_x

    @pl.when(section == 0)
    def _():
        grad_mine[...] = rows_in[:seq]
        grad_other[...] = grad_one[...].astype(F32)

    @pl.when(section == 1)
    def _():
        grad_mine[...] = grad_one[...].astype(F32)
        grad_other[...] = rows_in[:seq]

    for copy in copies:
        copy.wait()


def vmem(count):
    return [pl.BlockSpec(memory_space=pltpu.VMEM)] * count


def anywhere(count):
    return [pl.BlockSpec(memory_space=pl.ANY)] * count


def shape(dims, dtype):
    return jax.ShapeDtypeStruct(dims, dtype)


def act_shapes(width, wide):
    heads = width // HEAD_DIM
    return [
        ((SEQ_ROWS, 3 * width), BF16),
        ((heads, SEQ_ROWS, SEQ_ROWS), BF16),
        ((SEQ_ROWS, width), BF16),
        ((SEQ_ROWS, width), F32),
        ((SEQ_ROWS, wide), BF16),
        ((SEQ_ROWS, wide), BF16),
    ]


def grant(mib):
    return pltpu.CompilerParams(vmem_limit_bytes=mib * MIB)


def run_main(mine, other, patches, cotangent, live, wide):
    seq, width = patches.shape[1:]
    acts = act_shapes(width, wide)
    return pl.pallas_call(
        functools.partial(main_kernel, seq),
        out_shape=[
            shape((seq, width), BF16),
            shape((seq, width), BF16),
            shape((seq, width), BF16),
            shape((4, 4, HALF, PIECE), BF16),
            shape((2, 4, HALF, PIECE), BF16),
            shape((2, 4, HALF, PIECE), BF16),
            shape((1, 4, ROWS, PACKED), BF16),
            shape((8, width), F32),
        ]
        + [shape(*a) for a in acts],
        in_specs=anywhere(22) + vmem(2) + [pl.BlockSpec(memory_space=pltpu.SMEM)],
        out_specs=vmem(6) + anywhere(1) + vmem(1) + anywhere(6),
        scratch_shapes=[
            pltpu.VMEM((2, 4, ROWS, PACKED), BF16),
            pltpu.VMEM((2, wide, width), BF16),
            pltpu.VMEM((2, 8, width), F32),
            pltpu.VMEM((2, 1, wide), F32),
            pltpu.VMEM((SEQ_ROWS, width), F32),
            pltpu.VMEM((SEQ_ROWS, width), F32),
            pltpu.VMEM((SEQ_ROWS, wide), BF16),
            pltpu.VMEM((SEQ_ROWS, 3 * width), BF16),
            pltpu.VMEM((2, 4, 4, HALF, PIECE), BF16),
            pltpu.SemaphoreType.DMA((2, 16)),
            pltpu.SemaphoreType.DMA((11,)),
        ]
        + [pltpu.VMEM(*a) for a in acts + acts],
        compiler_params=grant(32),
        name="forward_and_layer_one",
    )(*mine, *other, patches, cotangent, live)


def run_last(weights, vectors, grad_one, patches, acts, wide):
    seq, width = patches.shape[1:]
    return pl.pallas_call(
        functools.partial(last_kernel, seq),
        out_shape=[
            shape((seq, width), F32),
            shape((seq, width), F32),
            shape((4, 4, HALF, PIECE), BF16),
            shape((4, 4, HALF, PIECE), BF16),
        ],
        in_specs=anywhere(1) + vmem(3) + anywhere(6),
        out_specs=vmem(2) + anywhere(2),
        scratch_shapes=[
            pltpu.VMEM((1, 4, ROWS, PACKED), BF16),
            pltpu.VMEM((1, wide, width), BF16),
            pltpu.VMEM((SEQ_ROWS, width), F32),
            pltpu.VMEM((SEQ_ROWS, width), F32),
            pltpu.VMEM((SEQ_ROWS, wide), BF16),
            pltpu.VMEM((SEQ_ROWS, 3 * width), BF16),
            pltpu.VMEM((2, 4, 4, HALF, PIECE), BF16),
            pltpu.SemaphoreType.DMA((7,)),
            pltpu.SemaphoreType.DMA((2,)),
        ]
        + [pltpu.VMEM(*a) for a in act_shapes(width, wide)],
        compiler_params=grant(20),
        cost_estimate=pl.CostEstimate(flops=8_000_000_000, bytes_accessed=8_000_000, transcendentals=0),
        name="layer_zero_backward",
    )(weights, vectors, grad_one, patches, *acts)


def add(a, b):
    return a.astype(F32) + b.astype(F32)


def small_call(kernel, outs, name, *ins):
    return pl.pallas_call(
        kernel,
        out_shape=[shape(dims, BF16) for dims in outs],
        in_specs=vmem(len(ins)),
        out_specs=vmem(len(outs)),
        compiler_params=grant(12),
        name=name,
    )(*ins)


def pair_sum_kernel(keep, recv, to_x, to_y, own, x_late, y_late):
    for place in range(4):
        own[place] = add(keep[0, place], recv[0, place]).astype(BF16)
    for place in range(2):
        to_x[0, place] = add(keep[1, place], recv[1, place]).astype(BF16)
        to_x[1, place] = add(keep[3, place], recv[3, place]).astype(BF16)
        to_y[0, place] = add(keep[2, 2 + place], recv[2, 2 + place]).astype(BF16)
        to_y[1, place] = add(keep[3, 2 + place], recv[3, 2 + place]).astype(BF16)
        x_late[place] = add(keep[1, 2 + place], recv[1, 2 + place]).astype(BF16)
        y_late[place] = add(keep[2, place], recv[2, place]).astype(BF16)


def near_sum_kernel(keep, recv, to_x, to_y):
    for place in range(4):
        to_x[place] = add(keep[1, place], recv[0, place]).astype(BF16)
        to_y[place] = add(keep[2, place], recv[1, place]).astype(BF16)


def whole_plane_kernel(keep, recv, got_x, got_y, out):
    shard = lax.axis_index("shard")
    for place in range(4):
        owner = lax.rem(shard + place, 4)
        value = add(keep[0, place], recv[0, place]) + add(got_x[place], got_y[place])
        out[owner, 0] = value.astype(BF16)
        out[owner, 1] = add(keep[3, place], recv[1, place]).astype(BF16)


def pair_column_kernel(parts, out):
    for index in range(2):
        value = add(parts[0, index], parts[1, index]) + add(parts[2, index], parts[3, index])
        out[index] = value.astype(BF16)


def join_kernel(*refs):
    pieces, outs = refs[:8], refs[8:]
    for bits in range(4):
        for half in range(2):
            value = add(pieces[2 * bits + half][0], pieces[2 * (3 - bits) + half][1])
            outs[2 * bits + half][...] = value.astype(BF16)


def relay_kernel(late, got, out):
    for place in range(2):
        out[place] = add(late[place], got[1, place]).astype(BF16)


def plane_sum_kernel(own, got_x, got_y, late_y, late_x, out):
    shard = lax.axis_index("shard")
    for first, got, late in ((0, got_x, late_y), (2, got_y, late_x)):
        for place in range(2):
            value = add(own[first + place], got[0, place]) + late[place].astype(F32)
            out[lax.rem(shard + first + place, 4)] = value.astype(BF16)


def column_sum_kernel(parts, out):
    out[...] = (add(parts[0], parts[1]) + add(parts[2], parts[3])).astype(BF16)


def unpack_kernel(*refs):
    zero, one = refs[:8], refs[8:16]
    (qkv, out, up, down), rest = refs[16:20], refs[20:29]
    table, sems = refs[29:]
    section, _, replica = positions()

    def copies_of(pieces, target):
        copies = []
        for bits in range(4):
            place = lax.bitwise_xor(replica, bits)
            for half in range(2):
                where = section if half == 0 else 1 - section
                index = 2 * bits + half
                copies.append(
                    pltpu.make_async_copy(pieces[index], target.at[place, where], sems.at[index])
                )
        return copies

    for layer, pieces in enumerate((zero, one)):

        @pl.when(section == layer)
        def _(pieces=pieces):
            for copy in copies_of(pieces, table):
                copy.start()
            for copy in copies_of(pieces, table):
                copy.wait()

    def put(target, row, column, start, count, at):
        while count:
            piece, inside = start // PIECE, start % PIECE
            some = min(count, PIECE - inside)
            for half in range(2):
                target[0, row + half * HALF : row + half * HALF + HALF, at : at + some] = table[
                    piece, half, :, inside : inside + some
                ].astype(F32)
            start, at, count = start + some, at + some, count - some

    put(up, 0, 0, UP0, QKV0 - UP0, 0)
    put(qkv, 0, 0, QKV0, OUT0 - QKV0, 0)
    put(out, 0, 0, OUT0, DOWN0 - OUT0, 0)
    width = out.shape[2]
    for fold in range(4):
        put(down, fold * ROWS, 0, DOWN0 + fold * width, width, 0)
    inside = VEC0 - 3 * PIECE
    tile = table[3, 0, 0:16, inside : inside + LANES].astype(F32)
    for index in range(8):
        rest[index][...] = tile[index : index + 1, :ROWS]
    rest[8][...] = jnp.concatenate([tile[8 + k : 9 + k] for k in range(3)], 1)


def unpack(zero, one, width, wide):
    return pl.pallas_call(
        unpack_kernel,
        out_shape=[
            shape((1, ROWS, 3 * width), F32),
            shape((1, ROWS, width), F32),
            shape((1, ROWS, wide), F32),
            shape((1, 4 * ROWS, width), F32),
        ]
        + [shape((1, ROWS), F32)] * 8
        + [shape((1, 4 * ROWS), F32)],
        in_specs=anywhere(16),
        out_specs=vmem(13),
        scratch_shapes=[
            pltpu.VMEM((4, 2, HALF, PIECE), BF16),
            pltpu.SemaphoreType.DMA((8,)),
        ],
        compiler_params=grant(16),
        name="unpack",
    )(*zero, *one)


def swap(value):
    return lax.ppermute(value, "section", [(0, 1), (1, 0)])


def flip(value, bits):
    return lax.ppermute(value, "replica", [(place, place ^ bits) for place in range(4)])


def shift(value, steps):
    return lax.ppermute(value, "shard", [(place, (place + steps) % 4) for place in range(4)])


def pack_kernel(*refs):
    sources, (own, quarter) = refs[:13], refs[13:15]
    staged, eight, bias_up, sems = refs[15:19]
    _, _, replica = positions()
    width = sources[2].shape[2]
    targets = [
        own.at[:, UP0:QKV0],
        own.at[:, QKV0:OUT0],
        own.at[:, OUT0:DOWN0],
        staged,
    ]
    targets += [eight.at[index : index + 1] for index in range(8)] + [bias_up]
    copies = [
        pltpu.make_async_copy(source.at[0] if index < 4 else source, target, sems.at[index])
        for index, (source, target) in enumerate(zip(sources, targets))
    ]
    for copy in copies:
        copy.start()
    for copy in copies:
        copy.wait()
    for fold in range(4):
        own[:, DOWN0 + fold * width : DOWN0 + (fold + 1) * width] = staged[
            fold * ROWS : (fold + 1) * ROWS
        ]
    padded = jnp.concatenate([eight[...], jnp.zeros((8, LANES - ROWS), F32)], 1)
    up = [bias_up[:, k * LANES : (k + 1) * LANES] for k in range(3)]
    tile = jnp.concatenate([padded] + up + [jnp.zeros((5, LANES), F32)], 0)
    high = tile.astype(BF16)
    low = tile - high.astype(F32)
    own[0:16, VEC0:PACKED] = high
    own[16:32, VEC0:PACKED] = low.astype(BF16)
    own[32:, VEC0:PACKED] = jnp.zeros((ROWS - 32, LANES), BF16)
    quarter[:, QUARTER:] = own[:, VEC0:PACKED]
    for place in range(4):

        @pl.when(replica == place)
        def _(place=place):
            quarter[:, :QUARTER] = own[:, place * QUARTER : (place + 1) * QUARTER]


def pack(*arrays):
    width = arrays[2].shape[2]
    return pl.pallas_call(
        pack_kernel,
        out_shape=[shape(dims, BF16) for dims in ((ROWS, PACKED), (ROWS, PIECE_IN))],
        in_specs=anywhere(13),
        out_specs=vmem(2),
        scratch_shapes=[
            pltpu.VMEM((4 * ROWS, width), BF16),
            pltpu.VMEM((8, ROWS), F32),
            pltpu.VMEM((1, 4 * ROWS), F32),
            pltpu.SemaphoreType.DMA((13,)),
        ],
        compiler_params=grant(60),
        name="pack",
    )(*arrays)


def after(value, *earlier):
    return lax.optimization_barrier((value,) + earlier)[0]


def reduce_plane(keep, send):
    half = (2,) + keep.shape[2:]
    to_x, to_y, own, x_late, y_late = small_call(
        pair_sum_kernel,
        [(2,) + half, (2,) + half, keep.shape[1:], half, half],
        "sum_of_cores",
        keep,
        swap(send),
    )
    return to_x, to_y, own, x_late, y_late


def near_kernel(first, third, near, upper, lower):
    near[0] = first[:, :QUARTER]
    near[1] = third[:, :QUARTER]
    upper[...] = first[:HALF]
    lower[...] = third[HALF:]


def far_kernel(first, third, upper, lower, far, tiles):
    far[:HALF] = upper[:, :QUARTER]
    far[HALF:] = lower[:, :QUARTER]
    tiles[0] = first[:, QUARTER:]
    tiles[1] = third[:, QUARTER:]
    tiles[2, :HALF] = upper[:, QUARTER:]
    tiles[2, HALF:] = lower[:, QUARTER:]


def relay(parts, got_x, got_y):
    _, _, own, x_late, y_late = parts
    half = x_late.shape
    (y_send,) = small_call(relay_kernel, [half], "relay", y_late, got_x)
    (x_send,) = small_call(relay_kernel, [half], "relay", x_late, got_y)
    return flip(y_send, 2), flip(x_send, 1)


def sum_column(parts):
    return small_call(column_sum_kernel, [parts.shape[1:]], "sum_of_column", parts)[0]


def spread(value):
    return [value] + [flip(value, bits) for bits in (1, 2, 3)]


def both_halves(pieces):
    return [member for piece in pieces for member in (piece, swap(piece))]


def rows_kernel(out_mine, out_other, grad_mine, grad_other, outs, grads):
    section = lax.axis_index("section")
    for slot in range(2):

        @pl.when(section == slot)
        def _(slot=slot):
            outs[:, slot, :] = out_mine[...].astype(F32).astype(BF16)
            outs[:, 1 - slot, :] = out_other[...]
            grads[:, slot, :] = grad_mine[...]
            grads[:, 1 - slot, :] = grad_other[...]


def rows_of_slots(out_mine, out_other, grad_mine, grad_other):
    seq, width = out_mine.shape
    outs, grads = pl.pallas_call(
        rows_kernel,
        out_shape=[shape((seq, 2, width), BF16), shape((seq, 2, width), F32)],
        in_specs=vmem(4),
        out_specs=vmem(2),
        compiler_params=grant(12),
        name="rows_of_slots",
    )(out_mine, out_other, grad_mine, grad_other)
    return outs, grads


def packed_local(patches, live_slots, cotangent, w_qkv, w_out, w_up, w_down, *small):
    width, wide = w_out.shape[2], w_up.shape[2]
    bias_q, bias_v, bias_out, bias_up, bias_down, gain_one, offset_one, gain_two, offset_two = small
    vectors = (bias_q, bias_v, bias_out, bias_down, gain_one, offset_one, gain_two, offset_two)
    own, quarter = pack(w_up, w_qkv, w_out, w_down, *vectors, bias_up)
    first, third = shift(quarter, 1), shift(quarter, 3)
    half = (HALF, PIECE_IN)
    near, upper, lower = small_call(
        near_kernel, [(2, ROWS, QUARTER), half, half], "near", first, third
    )
    x_near, y_near = flip(near, 1), flip(near, 2)
    far, tiles = small_call(
        far_kernel,
        [(ROWS, QUARTER), (3, ROWS, LANES)],
        "far",
        first,
        third,
        shift(upper, 1),
        shift(lower, 3),
    )
    far_now, x_now, y_now = lax.optimization_barrier((far, x_near, y_near))
    x_far, y_far, d_far = (flip(far_now, bits) for bits in (1, 2, 3))
    d_first, d_third = flip(y_now[0], 1), flip(x_now[1], 2)
    mine = [own, tiles, near, far, x_near, x_far, y_near, y_far, d_first, d_third, d_far]
    other = [swap(member) for member in mine]

    (out_mine, out_other, grad_one, keep1, near1, rest1, kept, vectors, *acts) = run_main(
        mine, other, patches, cotangent, live_slots, wide
    )
    whole, piece = keep1.shape[1:], keep1.shape[2:]
    to_x, to_y = small_call(near_sum_kernel, [whole] * 2, "sum_of_cores", keep1, swap(near1))
    got1 = (flip(to_x, 1), flip(to_y, 2))
    kept = after(kept, to_x, to_y)
    last = run_last(kept, vectors, grad_one, patches, acts, wide)
    grad_mine, grad_other, keep0, send0, recv1, *got1 = lax.optimization_barrier(
        (*last, swap(rest1), *got1)
    )
    (sums1,) = small_call(
        whole_plane_kernel, [(4, 2) + piece], "sum_of_plane", keep1, recv1, *got1
    )
    column1 = lax.all_to_all(sums1, "shard", 0, 0, tiled=True)
    parts0 = reduce_plane(after(keep0, sums1), send0)
    got0 = (flip(parts0[0], 1), flip(parts0[1], 2))
    rows = rows_of_slots(out_mine, swap(out_other), grad_mine, swap(grad_other))
    *got0, outs, grads = lax.optimization_barrier((*got0, *rows))
    layer_outputs, input_grads = outs.transpose(1, 0, 2)[None], grads.transpose(1, 0, 2)[None]
    late0 = relay(parts0, *got0)
    (sums0,) = small_call(
        plane_sum_kernel, [parts0[2].shape], "sum_of_plane", parts0[2], *got0, *late0
    )
    column0 = lax.all_to_all(sums0, "shard", 0, 0, tiled=True)
    (one,) = small_call(
        pair_column_kernel, [(2,) + piece], "sum_of_column", after(column1, sums0)
    )
    one = spread(one)
    column0 = after(column0, *one[1:])
    zero = spread(sum_column(column0))
    one = small_call(join_kernel, [piece] * 8, "join", *both_halves(one))
    grad_qkv, grad_out, grad_up, grad_down, *rest = unpack(
        both_halves(zero), one, width, wide
    )

    (g_q, g_v, g_o, g_d, g_g1, g_o1, g_g2, g_o2, g_up) = rest
    return (
        layer_outputs,
        input_grads,
        grad_qkv,
        grad_out,
        grad_up,
        grad_down,
        g_q,
        g_v,
        g_o,
        g_up,
        g_d,
        g_g1,
        g_o1,
        g_g2,
        g_o2,
    )


class PlainPut:
    def __init__(self, outs, layer):
        self.outs, self.layer = outs, layer

    def w_qkv(self, value):
        self.outs[0][self.layer] = value

    def w_out(self, value):
        self.outs[1][self.layer] = value

    def w_up(self, lo, value):
        self.outs[2][self.layer, :, lo : lo + value.shape[1]] = value

    def w_down(self, lo, value):
        self.outs[3][self.layer, lo : lo + value.shape[0]] = value

    def vectors(self, sums, bias_up):
        self.outs[4][self.layer] = sums
        self.outs[5][self.layer] = bias_up


def plain_kernel(seq, *refs):
    patches, cotangent, live, w_qkv, w_out, w_up, w_down, vectors, biases = refs[:9]
    out_rows, grad_rows = refs[9:11]
    grads = refs[11:17]
    rows_in, rows_mid, up_grad, qkv_grad = refs[17:21]
    acts = (refs[21:27], refs[27:33])
    section = lax.axis_index("section")
    width = rows_in.shape[1]

    def weights_of(layer):
        return (
            lambda: w_qkv[layer],
            lambda: w_out[layer],
            lambda lo, step: w_up[layer, :, lo : lo + step],
            lambda lo, step: w_down[layer, lo : lo + step],
        )

    vec_of = lambda layer: lambda index: vectors[layer, index : index + 1]
    bias_of = lambda layer: lambda lo, step: biases[layer, :, lo : lo + step]
    live_rows = lax.broadcasted_iota(jnp.int32, (SEQ_ROWS, width), 0) < seq
    rows_in[seq - seq % 8 :] = jnp.zeros((SEQ_ROWS - seq + seq % 8, width), F32)
    rows_in[:seq] = patches[section].astype(F32)
    result = layer_forward(rows_in[...], seq, weights_of(0), vec_of(0), bias_of(0), acts[0])
    out_rows[0] = result[:seq].astype(BF16)
    rows_mid[...] = jnp.where(live_rows, result.astype(BF16).astype(F32), 0.0)
    result = layer_forward(rows_mid[...], seq, weights_of(1), vec_of(1), bias_of(1), acts[1])
    out_rows[1] = result[:seq].astype(BF16)
    seed = cotangent[section].astype(F32) * live[section].astype(F32)
    blank = jnp.zeros((SEQ_ROWS - seq, width), F32)
    grad_x = layer_backward(
        jnp.concatenate([seed, blank], 0),
        rows_mid[...],
        weights_of(1),
        vec_of(1),
        acts[1],
        up_grad,
        qkv_grad,
        PlainPut(grads, 1),
    )
    grad_x = grad_x.astype(BF16).astype(F32)
    grad_rows[1] = grad_x[:seq]
    grad_x = layer_backward(
        grad_x,
        rows_in[...],
        weights_of(0),
        vec_of(0),
        acts[0],
        up_grad,
        qkv_grad,
        PlainPut(grads, 0),
    )
    grad_rows[0] = grad_x[:seq]


def plain_local(patches, live_slots, cotangent, w_qkv, w_out, w_up, w_down, *small):
    bias_q, bias_v, bias_out, bias_up, bias_down, gain_one, offset_one, gain_two, offset_two = small
    seq, width = patches.shape[1:]
    wide = w_up.shape[2]

    def whole(value):
        along = lax.all_gather(value, "shard", axis=1, tiled=True)
        return lax.all_gather(along, "section", axis=0, tiled=True)

    small = (bias_q, bias_v, bias_out, bias_down, gain_one, offset_one, gain_two, offset_two)
    vectors = whole(jnp.stack(small, 2)).transpose(0, 2, 1)
    biases = whole(bias_up)[:, None]
    acts = act_shapes(width, wide)
    out_rows, grad_rows, *grads = pl.pallas_call(
        functools.partial(plain_kernel, seq),
        out_shape=[
            shape((2, seq, width), BF16),
            shape((2, seq, width), F32),
            shape((2, width, 3 * width), F32),
            shape((2, width, width), F32),
            shape((2, width, wide), F32),
            shape((2, wide, width), F32),
            shape((2, 8, width), F32),
            shape((2, 1, wide), F32),
        ],
        in_specs=vmem(2) + [pl.BlockSpec(memory_space=pltpu.SMEM)] + vmem(6),
        out_specs=vmem(8),
        scratch_shapes=[
            pltpu.VMEM((SEQ_ROWS, width), F32),
            pltpu.VMEM((SEQ_ROWS, width), F32),
            pltpu.VMEM((SEQ_ROWS, wide), BF16),
            pltpu.VMEM((SEQ_ROWS, 3 * width), BF16),
        ]
        + [pltpu.VMEM(*a) for a in acts + acts],
        compiler_params=grant(56),
        name="both_layers",
    )(patches, cotangent, live_slots, *(whole(w) for w in (w_qkv, w_out, w_up, w_down)), vectors, biases)

    def owned(value):
        mine = lax.psum_scatter(value, "section", scatter_dimension=0, tiled=True)
        mine = lax.psum_scatter(mine.astype(BF16), "shard", scatter_dimension=1, tiled=True)
        return lax.psum(mine, "replica").astype(F32)

    grads = [owned(value) for value in grads[:4]] + [
        owned(grads[4].transpose(0, 2, 1)),
        owned(grads[5][:, 0]),
    ]
    q, v, out, down, g1, o1, g2, o2 = (grads[4][..., index] for index in range(8))

    def by_section(value):
        section = lax.axis_index("section")
        recv = swap(jnp.where(section == 0, value[1], value[0]))
        first = jnp.where(section == 0, value[0], recv)
        return jnp.stack([first, jnp.where(section == 0, recv, value[1])])[None]

    return (
        by_section(out_rows),
        by_section(grad_rows),
        *grads[:4],
        q,
        v,
        out,
        grads[5],
        down,
        g1,
        o1,
        g2,
        o2,
    )


def solution(mesh):
    slots = P(("shard", "replica"), None, None)
    matrix, vector = P("section", "shard", None), P("section", "shard")
    outs = P("section", ("shard", "replica"), None, None)
    packed = mesh.shape["shard"] == 4 and mesh.shape["replica"] == 4
    return jax.shard_map(
        packed_local if packed else plain_local,
        mesh=mesh,
        in_specs=(slots, P(("shard", "replica")), slots) + (matrix,) * 4 + (vector,) * 9,
        out_specs=(outs, outs) + (matrix,) * 4 + (vector,) * 9,
        check_vma=False,
    )
```

```python
import functools

import jax
import jax.numpy as jnp
from jax import lax
from jax.experimental import pallas as pl
from jax.experimental.pallas import tpu as pltpu
from jax.sharding import PartitionSpec as P

HEAD_DIM = 64
EPSILON = 1e-06
ROOT_HALF = 0.7071067811865476
INVERSE_ROOT_TWO_PI = 0.3989422804014327
F32 = jnp.float32
BF16 = jnp.bfloat16
LANES = 128
MIB = 1024 * 1024

BIAS_Q, BIAS_V, BIAS_OUT, BIAS_DOWN, GAIN_ONE, OFFSET_ONE, GAIN_TWO, OFFSET_TWO = range(8)


def dot(a, b):
    return lax.dot_general(a, b, (((1,), (0,)), ((), ())), preferred_element_type=F32)


def dot_back(a, b):
    return lax.dot_general(a, b, (((1,), (1,)), ((), ())), preferred_element_type=F32)


def dot_rows(a, b):
    return lax.dot_general(a, b, (((0,), (0,)), ((), ())), preferred_element_type=F32)


def normalize(values):
    row_mean = jnp.mean(values, -1, keepdims=True)
    centred = values - row_mean
    inverse = lax.rsqrt(jnp.mean(centred * centred, -1, keepdims=True) + EPSILON)
    return centred * inverse, inverse


def norm_backward(grad, unit, inverse):
    centre = jnp.mean(grad, -1, keepdims=True)
    slope = jnp.mean(grad * unit, -1, keepdims=True)
    return inverse * (grad - centre - unit * slope)


def total(values):
    return jnp.sum(values, axis=0, keepdims=True)


def head_masks(rows):
    lane = lax.broadcasted_iota(jnp.int32, (rows, LANES), 1)
    return (lane < HEAD_DIM, lane >= HEAD_DIM)


def pick(mask, value):
    return jnp.where(mask, value.astype(F32), 0.0).astype(BF16)


def layer_forward(x, seq, weights, vec, bias_up, acts):
    rows, width = x.shape
    w_qkv, w_out, w_up, w_down = weights
    qkv_ref, p_ref, attended_ref, hidden_ref, act_ref, slope_ref = acts
    unit, _ = normalize(x)
    normed = (unit * vec(GAIN_ONE) + vec(OFFSET_ONE)).astype(BF16)
    qkv = dot(normed, w_qkv())
    queries = (qkv[:, :width] + vec(BIAS_Q)).astype(BF16).astype(F32) * HEAD_DIM ** (-0.5)
    qkv_ref[:, :width] = queries.astype(BF16)
    qkv_ref[:, width : 2 * width] = qkv[:, width : 2 * width].astype(BF16)
    qkv_ref[:, 2 * width :] = (qkv[:, 2 * width :] + vec(BIAS_V)).astype(BF16)
    masks = head_masks(rows)
    key_live = lax.broadcasted_iota(jnp.int32, (rows, rows), 1) < seq
    for pair in range(width // LANES):
        lo = pair * LANES
        q = qkv_ref[:, lo : lo + LANES]
        k = qkv_ref[:, width + lo : width + lo + LANES]
        v = qkv_ref[:, 2 * width + lo : 2 * width + lo + LANES]
        gathered = None
        for half in range(2):
            scores = dot_back(pick(masks[half], q), k)
            scores = jnp.where(key_live, scores, -1e30)
            scores = jnp.exp(scores - jnp.max(scores, -1, keepdims=True))
            prob = (scores * (1.0 / jnp.sum(scores, -1, keepdims=True))).astype(BF16)
            p_ref[2 * pair + half] = prob
            part = dot(prob, pick(masks[half], v))
            gathered = part if gathered is None else gathered + part
        attended_ref[:, lo : lo + LANES] = gathered.astype(BF16)
    hidden = x + dot(attended_ref[...], w_out()) + vec(BIAS_OUT)
    hidden_ref[...] = hidden
    unit_two, _ = normalize(hidden)
    normed_two = (unit_two * vec(GAIN_TWO) + vec(OFFSET_TWO)).astype(BF16)
    output = hidden + vec(BIAS_DOWN)
    wide = act_ref.shape[1]
    step = 512
    for lo in range(0, wide, step):
        up = dot(normed_two, w_up(lo, step)) + bias_up(lo, step)
        cdf = 0.5 * (1.0 + lax.erf(up * ROOT_HALF))
        density = jnp.exp(-0.5 * up * up) * INVERSE_ROOT_TWO_PI
        act = (up * cdf).astype(BF16)
        act_ref[:, lo : lo + step] = act
        slope_ref[:, lo : lo + step] = (cdf + up * density).astype(BF16)
        output = output + dot(act, w_down(lo, step))
    return output


def layer_backward(grad, x, weights, vec, acts, up_grad_ref, qkv_grad_ref, put):
    rows, width = grad.shape
    w_qkv, w_out, w_up, w_down = weights
    qkv_ref, p_ref, attended_ref, hidden_ref, act_ref, slope_ref = acts
    wide = act_ref.shape[1]
    step = 512
    down_grad = grad.astype(BF16)
    unit_two, inverse_two = normalize(hidden_ref[...])
    normed_two = (unit_two * vec(GAIN_TWO) + vec(OFFSET_TWO)).astype(BF16)
    grad_normed_two = None
    sums_up = []
    for lo in range(0, wide, step):
        put.w_down(lo, dot_rows(act_ref[:, lo : lo + step], down_grad))
        up_grad = dot_back(down_grad, w_down(lo, step)) * slope_ref[:, lo : lo + step].astype(F32)
        up_grad = up_grad.astype(BF16)
        sums_up.append(total(up_grad.astype(F32)))
        put.w_up(lo, dot_rows(normed_two, up_grad))
        part = dot_back(up_grad, w_up(lo, step))
        grad_normed_two = part if grad_normed_two is None else grad_normed_two + part
    grad_hidden = grad + norm_backward(grad_normed_two * vec(GAIN_TWO), unit_two, inverse_two)
    out_grad = grad_hidden.astype(BF16)
    put.w_out(dot_rows(attended_ref[...], out_grad))
    attended_grad = dot_back(out_grad, w_out()).astype(BF16)
    masks = head_masks(rows)
    for pair in range(width // LANES):
        lo = pair * LANES
        q = qkv_ref[:, lo : lo + LANES]
        k = qkv_ref[:, width + lo : width + lo + LANES]
        v = qkv_ref[:, 2 * width + lo : 2 * width + lo + LANES]
        ag = attended_grad[:, lo : lo + LANES]
        q_grad = k_grad = v_grad = None
        for half in range(2):
            mine = pick(masks[half], ag)
            prob = p_ref[2 * pair + half]
            prob32 = prob.astype(F32)
            grad_prob = dot_back(mine, v)
            dv = dot_rows(prob, mine)
            row_term = jnp.sum(grad_prob * prob32, -1, keepdims=True)
            score_grad = (prob32 * (grad_prob - row_term)).astype(BF16)
            dq = dot(score_grad, pick(masks[half], k))
            dk = dot_rows(score_grad, pick(masks[half], q))
            q_grad = dq if q_grad is None else q_grad + dq
            k_grad = dk if k_grad is None else k_grad + dk
            v_grad = dv if v_grad is None else v_grad + dv
        qkv_grad_ref[:, lo : lo + LANES] = (q_grad * HEAD_DIM ** (-0.5)).astype(BF16)
        qkv_grad_ref[:, width + lo : width + lo + LANES] = k_grad.astype(BF16)
        qkv_grad_ref[:, 2 * width + lo : 2 * width + lo + LANES] = v_grad.astype(BF16)
    unit, inverse = normalize(x)
    normed = (unit * vec(GAIN_ONE) + vec(OFFSET_ONE)).astype(BF16)
    put.w_qkv(dot_rows(normed, qkv_grad_ref[...]))
    grad_normed = dot_back(qkv_grad_ref[...], w_qkv())
    grad_x = grad_hidden + norm_backward(grad_normed * vec(GAIN_ONE), unit, inverse)
    sums = jnp.concatenate(
        [
            total(qkv_grad_ref[:, :width].astype(F32)),
            total(qkv_grad_ref[:, 2 * width :].astype(F32)),
            total(grad_hidden),
            total(grad),
            total(grad_normed * unit),
            total(grad_normed),
            total(grad_normed_two * unit_two),
            total(grad_normed_two),
        ],
        0,
    )
    put.vectors(sums, jnp.concatenate(sums_up, 1))
    return grad_x


ROWS = 96
HALF = 48
UP0, QKV0, OUT0, DOWN0, VEC0, PACKED = 0, 1536, 2688, 3072, 4608, 4736
QUARTER = 1152
PIECE_IN = QUARTER + LANES
PIECE = 1280
SEQ_ROWS = 208


def positions():
    return lax.axis_index("section"), lax.axis_index("shard"), lax.axis_index("replica")


class PackedPut:
    def __init__(self, grads, shard, replica):
        self.grads, self.shard, self.replica = grads, shard, replica

    def store(self, owner, column, value, row=0):
        place = lax.rem(owner - self.shard + 4, 4)
        rows, columns = value.shape
        value = value.astype(BF16)
        while columns:
            piece, inside = column // PIECE, column % PIECE
            count = min(columns, PIECE - inside)
            where = lax.bitwise_xor(self.replica, piece)
            for half in range(2):
                lo, hi = max(row, half * HALF), min(row + rows, half * HALF + HALF)
                if lo < hi:
                    self.grads[half, where, place, lo - half * HALF : hi - half * HALF, inside : inside + count] = (
                        value[lo - row : hi - row, :count]
                    )
            value, column, columns = value[:, count:], column + count, columns - count

    def by_rows(self, column, value):
        for owner in range(4):
            self.store(owner, column, value[owner * ROWS : (owner + 1) * ROWS])

    def w_up(self, lo, value):
        self.by_rows(UP0 + lo, value)

    def w_qkv(self, value):
        self.by_rows(QKV0, value)

    def w_out(self, value):
        self.by_rows(OUT0, value)

    def w_down(self, lo, value):
        rows, at = value.shape[0], 0
        while at < rows:
            owner, inside = divmod(lo + at, 4 * ROWS)
            fold, row = divmod(inside, ROWS)
            count = min(rows - at, ROWS - row)
            self.store(owner, DOWN0 + fold * value.shape[1], value[at : at + count], row)
            at += count

    def vectors(self, sums, bias_up):
        place3 = lax.bitwise_xor(self.replica, 3)
        first = VEC0 - 3 * PIECE
        self.grads[:, place3, :, :, first:] = jnp.zeros((2, 4, HALF, PIECE - first), BF16)
        blank = jnp.zeros((8, LANES - ROWS), F32)
        rest = jnp.zeros((5, LANES), F32)
        for owner in range(4):
            up = [
                bias_up[:, owner * 384 + k * LANES : owner * 384 + (k + 1) * LANES] for k in range(3)
            ]
            top = jnp.concatenate([sums[:, owner * ROWS : (owner + 1) * ROWS], blank], 1)
            tile = jnp.concatenate([top] + up + [rest], 0)
            self.store(owner, VEC0, tile)


def packed_weights(packed, down, layer):
    def w_qkv():
        return packed[layer, :, :, QKV0:OUT0].reshape(4 * ROWS, OUT0 - QKV0)

    def w_out():
        return packed[layer, :, :, OUT0:DOWN0].reshape(4 * ROWS, DOWN0 - OUT0)

    def w_up(lo, step):
        return packed[layer, :, :, UP0 + lo : UP0 + lo + step].reshape(4 * ROWS, step)

    def w_down(lo, step):
        return down[layer, lo : lo + step]

    return w_qkv, w_out, w_up, w_down


def unfold(packed, down, vectors, biases, layer):
    width = down.shape[2]
    for owner in range(4):
        for fold in range(4):
            at = (owner * 4 + fold) * ROWS
            down[layer, at : at + ROWS] = packed[
                layer, owner, :, DOWN0 + fold * width : DOWN0 + (fold + 1) * width
            ]
    tiles = [
        packed[layer, owner, 0:16, VEC0:PACKED].astype(F32)
        + packed[layer, owner, 16:32, VEC0:PACKED].astype(F32)
        for owner in range(4)
    ]
    vectors[layer] = jnp.concatenate([tile[0:8, 0:ROWS] for tile in tiles], 1)
    biases[layer] = jnp.concatenate([tile[8 + k : 9 + k] for tile in tiles for k in range(3)], 1)


def start_copies(pieces, packed, layer, sems, shard, replica):
    own, tiles, near, far, x_near, x_far, y_near, y_far, d_first, d_third, d_far = pieces
    copies = [(own, packed.at[layer, shard])]
    for index, step in enumerate((1, 3, 2)):
        owner = packed.at[layer, lax.rem(shard + 4 - step, 4)]
        copies.append((tiles.at[index], owner.at[:, pl.ds(VEC0, LANES)]))
    groups = (
        (0, near.at[0], near.at[1], far),
        (1, x_near.at[0], x_near.at[1], x_far),
        (2, y_near.at[0], y_near.at[1], y_far),
        (3, d_first, d_third, d_far),
    )
    for bits, first, third, second in groups:
        column = pl.multiple_of(lax.bitwise_xor(replica, bits) * QUARTER, LANES)
        for step, piece in ((1, first), (3, third), (2, second)):
            owner = packed.at[layer, lax.rem(shard + 4 - step, 4)]
            copies.append((piece, owner.at[:, pl.ds(column, QUARTER)]))
    return [
        pltpu.make_async_copy(source, target, sems.at[layer, index])
        for index, (source, target) in enumerate(copies)
    ]


def main_kernel(seq, *refs):
    mine, other = refs[0:11], refs[11:22]
    patches, cotangent, live = refs[22:25]
    refs = refs[25:]
    (
        out_mine,
        out_other,
        grad_one,
        keep,
        send_near,
        send_rest,
        kept_weights,
        kept_vectors,
    ) = refs[0:8]
    kept_acts = refs[8:14]
    (
        packed,
        down,
        vectors,
        biases,
        rows_in,
        rows_mid,
        up_grad,
        qkv_grad,
        grads,
        sems,
        out_sems,
    ) = refs[14:25]
    acts0, acts1 = refs[25:31], refs[31:37]
    section, shard, replica = positions()
    for copy in start_copies(mine, packed, section, sems, shard, replica):
        copy.start()
    for copy in start_copies(other, packed, 1 - section, sems, shard, replica):
        copy.start()
    width = rows_in.shape[1]
    rows_in[seq - seq % 8 :] = jnp.zeros((SEQ_ROWS - seq + seq % 8, width), F32)
    rows_in[:seq] = patches[section].astype(F32)

    def ready(layer):
        for copy in start_copies(mine, packed, layer, sems, shard, replica):
            copy.wait()
        unfold(packed, down, vectors, biases, layer)
        vec = lambda index: vectors[layer, index : index + 1]
        bias_up = lambda lo, step: biases[layer, :, lo : lo + step]
        return packed_weights(packed, down, layer), vec, bias_up

    weights0, vec0, bias_up0 = ready(0)
    save = [
        pltpu.make_async_copy(packed.at[0], kept_weights.at[0], out_sems.at[0]),
    ]
    for copy in save:
        copy.start()
    kept_vectors[...] = vectors[0]
    x0 = rows_in[...]
    result = layer_forward(x0, seq, weights0, vec0, bias_up0, acts0)
    for index in range(6):
        save.append(pltpu.make_async_copy(acts0[index], kept_acts[index], out_sems.at[3 + index]))
        save[-1].start()
    live_rows = lax.broadcasted_iota(jnp.int32, (SEQ_ROWS, width), 0) < seq
    rows_mid[...] = jnp.where(live_rows, result.astype(BF16).astype(F32), 0.0)

    @pl.when(section == 0)
    def _():
        out_mine[...] = rows_mid[:seq].astype(BF16)

    @pl.when(section == 1)
    def _():
        out_other[...] = rows_mid[:seq].astype(BF16)

    weights1, vec1, bias_up1 = ready(1)
    result = layer_forward(rows_mid[...], seq, weights1, vec1, bias_up1, acts1)
    rows_in[...] = result

    @pl.when(section == 1)
    def _():
        out_mine[...] = rows_in[:seq].astype(BF16)

    @pl.when(section == 0)
    def _():
        out_other[...] = rows_in[:seq].astype(BF16)

    rows_in[seq - seq % 8 :] = jnp.zeros((SEQ_ROWS - seq + seq % 8, width), F32)
    rows_in[:seq] = cotangent[section].astype(F32) * live[section].astype(F32)
    put = PackedPut(grads, shard, replica)
    grad_x = layer_backward(
        rows_in[...], rows_mid[...], weights1, vec1, acts1, up_grad, qkv_grad, put
    )
    grad_one[...] = grad_x[:seq].astype(BF16)
    copies = [
        pltpu.make_async_copy(grads.at[1 - section, 1:3], send_near, out_sems.at[1]),
        pltpu.make_async_copy(grads.at[section], keep, out_sems.at[2]),
        pltpu.make_async_copy(grads.at[1 - section, 0], send_rest.at[0], out_sems.at[9]),
        pltpu.make_async_copy(grads.at[1 - section, 3], send_rest.at[1], out_sems.at[10]),
    ]
    for copy in copies:
        copy.start()
    for copy in save + copies:
        copy.wait()


def last_kernel(seq, *refs):
    weights, vectors_in, grad_one, patches = refs[0:4]
    saved = refs[4:10]
    grad_mine, grad_other, keep, send = refs[10:14]
    packed, down, rows_in, rows_grad, up_grad, qkv_grad, grads, sems, out_sems = refs[14:23]
    acts = refs[23:29]
    section, shard, replica = positions()
    loads = [pltpu.make_async_copy(weights, packed, sems.at[6])]
    for index in range(6):
        loads.append(pltpu.make_async_copy(saved[index], acts[index], sems.at[index]))
    for load in loads:
        load.start()
    width = rows_in.shape[1]
    for buffer, source in ((rows_in, patches[section]), (rows_grad, grad_one[...])):
        buffer[seq - seq % 8 :] = jnp.zeros((SEQ_ROWS - seq + seq % 8, width), F32)
        buffer[:seq] = source.astype(F32)
    for load in loads:
        load.wait()
    for owner in range(4):
        for fold in range(4):
            at = (owner * 4 + fold) * ROWS
            down[0, at : at + ROWS] = packed[
                0, owner, :, DOWN0 + fold * width : DOWN0 + (fold + 1) * width
            ]
    vec = lambda index: vectors_in[index : index + 1]
    put = PackedPut(grads, shard, replica)
    grad_x = layer_backward(
        rows_grad[...],
        rows_in[...],
        packed_weights(packed, down, 0),
        vec,
        acts,
        up_grad,
        qkv_grad,
        put,
    )
    copies = [
        pltpu.make_async_copy(grads.at[section], keep, out_sems.at[0]),
        pltpu.make_async_copy(grads.at[1 - section], send, out_sems.at[1]),
    ]
    for copy in copies:
        copy.start()
    rows_in[...] = grad_x

    @pl.when(section == 0)
    def _():
        grad_mine[...] = rows_in[:seq]
        grad_other[...] = grad_one[...].astype(F32)

    @pl.when(section == 1)
    def _():
        grad_mine[...] = grad_one[...].astype(F32)
        grad_other[...] = rows_in[:seq]

    for copy in copies:
        copy.wait()


def vmem(count):
    return [pl.BlockSpec(memory_space=pltpu.VMEM)] * count


def anywhere(count):
    return [pl.BlockSpec(memory_space=pl.ANY)] * count


def shape(dims, dtype):
    return jax.ShapeDtypeStruct(dims, dtype)


def act_shapes(width, wide):
    heads = width // HEAD_DIM
    return [
        ((SEQ_ROWS, 3 * width), BF16),
        ((heads, SEQ_ROWS, SEQ_ROWS), BF16),
        ((SEQ_ROWS, width), BF16),
        ((SEQ_ROWS, width), F32),
        ((SEQ_ROWS, wide), BF16),
        ((SEQ_ROWS, wide), BF16),
    ]


def grant(mib):
    return pltpu.CompilerParams(vmem_limit_bytes=mib * MIB)


def run_main(mine, other, patches, cotangent, live, wide):
    seq, width = patches.shape[1:]
    acts = act_shapes(width, wide)
    return pl.pallas_call(
        functools.partial(main_kernel, seq),
        out_shape=[
            shape((seq, width), BF16),
            shape((seq, width), BF16),
            shape((seq, width), BF16),
            shape((4, 4, HALF, PIECE), BF16),
            shape((2, 4, HALF, PIECE), BF16),
            shape((2, 4, HALF, PIECE), BF16),
            shape((1, 4, ROWS, PACKED), BF16),
            shape((8, width), F32),
        ]
        + [shape(*a) for a in acts],
        in_specs=anywhere(22) + vmem(2) + [pl.BlockSpec(memory_space=pltpu.SMEM)],
        out_specs=vmem(6) + anywhere(1) + vmem(1) + anywhere(6),
        scratch_shapes=[
            pltpu.VMEM((2, 4, ROWS, PACKED), BF16),
            pltpu.VMEM((2, wide, width), BF16),
            pltpu.VMEM((2, 8, width), F32),
            pltpu.VMEM((2, 1, wide), F32),
            pltpu.VMEM((SEQ_ROWS, width), F32),
            pltpu.VMEM((SEQ_ROWS, width), F32),
            pltpu.VMEM((SEQ_ROWS, wide), BF16),
            pltpu.VMEM((SEQ_ROWS, 3 * width), BF16),
            pltpu.VMEM((2, 4, 4, HALF, PIECE), BF16),
            pltpu.SemaphoreType.DMA((2, 16)),
            pltpu.SemaphoreType.DMA((11,)),
        ]
        + [pltpu.VMEM(*a) for a in acts + acts],
        compiler_params=grant(32),
        name="forward_and_layer_one",
    )(*mine, *other, patches, cotangent, live)


def run_last(weights, vectors, grad_one, patches, acts, wide):
    seq, width = patches.shape[1:]
    return pl.pallas_call(
        functools.partial(last_kernel, seq),
        out_shape=[
            shape((seq, width), F32),
            shape((seq, width), F32),
            shape((4, 4, HALF, PIECE), BF16),
            shape((4, 4, HALF, PIECE), BF16),
        ],
        in_specs=anywhere(1) + vmem(3) + anywhere(6),
        out_specs=vmem(4),
        scratch_shapes=[
            pltpu.VMEM((1, 4, ROWS, PACKED), BF16),
            pltpu.VMEM((1, wide, width), BF16),
            pltpu.VMEM((SEQ_ROWS, width), F32),
            pltpu.VMEM((SEQ_ROWS, width), F32),
            pltpu.VMEM((SEQ_ROWS, wide), BF16),
            pltpu.VMEM((SEQ_ROWS, 3 * width), BF16),
            pltpu.VMEM((2, 4, 4, HALF, PIECE), BF16),
            pltpu.SemaphoreType.DMA((7,)),
            pltpu.SemaphoreType.DMA((2,)),
        ]
        + [pltpu.VMEM(*a) for a in act_shapes(width, wide)],
        compiler_params=grant(20),
        cost_estimate=pl.CostEstimate(flops=8_000_000_000, bytes_accessed=8_000_000, transcendentals=0),
        name="layer_zero_backward",
    )(weights, vectors, grad_one, patches, *acts)


def add(a, b):
    return a.astype(F32) + b.astype(F32)


def small_call(kernel, outs, name, *ins):
    return pl.pallas_call(
        kernel,
        out_shape=[shape(dims, BF16) for dims in outs],
        in_specs=vmem(len(ins)),
        out_specs=vmem(len(outs)),
        compiler_params=grant(12),
        name=name,
    )(*ins)


def pair_sum_kernel(keep, recv, to_x, to_y, own, x_late, y_late):
    for place in range(4):
        own[place] = add(keep[0, place], recv[0, place]).astype(BF16)
    for place in range(2):
        to_x[0, place] = add(keep[1, place], recv[1, place]).astype(BF16)
        to_x[1, place] = add(keep[3, place], recv[3, place]).astype(BF16)
        to_y[0, place] = add(keep[2, 2 + place], recv[2, 2 + place]).astype(BF16)
        to_y[1, place] = add(keep[3, 2 + place], recv[3, 2 + place]).astype(BF16)
        x_late[place] = add(keep[1, 2 + place], recv[1, 2 + place]).astype(BF16)
        y_late[place] = add(keep[2, place], recv[2, place]).astype(BF16)


def near_sum_kernel(keep, recv, to_x, to_y):
    for place in range(4):
        to_x[place] = add(keep[1, place], recv[0, place]).astype(BF16)
        to_y[place] = add(keep[2, place], recv[1, place]).astype(BF16)


def whole_plane_kernel(keep, recv, got_x, got_y, out):
    shard = lax.axis_index("shard")
    for place in range(4):
        owner = lax.rem(shard + place, 4)
        value = add(keep[0, place], recv[0, place]) + add(got_x[place], got_y[place])
        out[owner, 0] = value.astype(BF16)
        out[owner, 1] = add(keep[3, place], recv[1, place]).astype(BF16)


def pair_column_kernel(parts, out):
    for index in range(2):
        value = add(parts[0, index], parts[1, index]) + add(parts[2, index], parts[3, index])
        out[index] = value.astype(BF16)


def join_kernel(*refs):
    pieces, outs = refs[:8], refs[8:]
    for bits in range(4):
        for half in range(2):
            value = add(pieces[2 * bits + half][0], pieces[2 * (3 - bits) + half][1])
            outs[2 * bits + half][...] = value.astype(BF16)


def relay_kernel(late, got, out):
    for place in range(2):
        out[place] = add(late[place], got[1, place]).astype(BF16)


def plane_sum_kernel(own, got_x, got_y, late_y, late_x, out):
    shard = lax.axis_index("shard")
    for first, got, late in ((0, got_x, late_y), (2, got_y, late_x)):
        for place in range(2):
            value = add(own[first + place], got[0, place]) + late[place].astype(F32)
            out[lax.rem(shard + first + place, 4)] = value.astype(BF16)


def column_sum_kernel(parts, out):
    out[...] = (add(parts[0], parts[1]) + add(parts[2], parts[3])).astype(BF16)


def unpack_kernel(*refs):
    zero, one = refs[:8], refs[8:16]
    (qkv, out, up, down), rest = refs[16:20], refs[20:29]
    table, sems = refs[29:]
    section, _, replica = positions()

    def copies_of(pieces, target):
        copies = []
        for bits in range(4):
            place = lax.bitwise_xor(replica, bits)
            for half in range(2):
                where = section if half == 0 else 1 - section
                index = 2 * bits + half
                copies.append(
                    pltpu.make_async_copy(pieces[index], target.at[place, where], sems.at[index])
                )
        return copies

    for layer, pieces in enumerate((zero, one)):

        @pl.when(section == layer)
        def _(pieces=pieces):
            for copy in copies_of(pieces, table):
                copy.start()
            for copy in copies_of(pieces, table):
                copy.wait()

    def put(target, row, column, start, count, at):
        while count:
            piece, inside = start // PIECE, start % PIECE
            some = min(count, PIECE - inside)
            for half in range(2):
                target[0, row + half * HALF : row + half * HALF + HALF, at : at + some] = table[
                    piece, half, :, inside : inside + some
                ].astype(F32)
            start, at, count = start + some, at + some, count - some

    put(up, 0, 0, UP0, QKV0 - UP0, 0)
    put(qkv, 0, 0, QKV0, OUT0 - QKV0, 0)
    put(out, 0, 0, OUT0, DOWN0 - OUT0, 0)
    width = out.shape[2]
    for fold in range(4):
        put(down, fold * ROWS, 0, DOWN0 + fold * width, width, 0)
    inside = VEC0 - 3 * PIECE
    tile = table[3, 0, 0:16, inside : inside + LANES].astype(F32)
    for index in range(8):
        rest[index][...] = tile[index : index + 1, :ROWS]
    rest[8][...] = jnp.concatenate([tile[8 + k : 9 + k] for k in range(3)], 1)


def unpack(zero, one, width, wide):
    return pl.pallas_call(
        unpack_kernel,
        out_shape=[
            shape((1, ROWS, 3 * width), F32),
            shape((1, ROWS, width), F32),
            shape((1, ROWS, wide), F32),
            shape((1, 4 * ROWS, width), F32),
        ]
        + [shape((1, ROWS), F32)] * 8
        + [shape((1, 4 * ROWS), F32)],
        in_specs=anywhere(16),
        out_specs=vmem(13),
        scratch_shapes=[
            pltpu.VMEM((4, 2, HALF, PIECE), BF16),
            pltpu.SemaphoreType.DMA((8,)),
        ],
        compiler_params=grant(16),
        name="unpack",
    )(*zero, *one)


def swap(value):
    return lax.ppermute(value, "section", [(0, 1), (1, 0)])


def flip(value, bits):
    return lax.ppermute(value, "replica", [(place, place ^ bits) for place in range(4)])


def shift(value, steps):
    return lax.ppermute(value, "shard", [(place, (place + steps) % 4) for place in range(4)])


def pack_kernel(*refs):
    sources, (own, quarter) = refs[:13], refs[13:15]
    staged, eight, bias_up, sems = refs[15:19]
    _, _, replica = positions()
    width = sources[2].shape[2]
    targets = [
        own.at[:, UP0:QKV0],
        own.at[:, QKV0:OUT0],
        own.at[:, OUT0:DOWN0],
        staged,
    ]
    targets += [eight.at[index : index + 1] for index in range(8)] + [bias_up]
    copies = [
        pltpu.make_async_copy(source.at[0] if index < 4 else source, target, sems.at[index])
        for index, (source, target) in enumerate(zip(sources, targets))
    ]
    for copy in copies:
        copy.start()
    for copy in copies:
        copy.wait()
    for fold in range(4):
        own[:, DOWN0 + fold * width : DOWN0 + (fold + 1) * width] = staged[
            fold * ROWS : (fold + 1) * ROWS
        ]
    padded = jnp.concatenate([eight[...], jnp.zeros((8, LANES - ROWS), F32)], 1)
    up = [bias_up[:, k * LANES : (k + 1) * LANES] for k in range(3)]
    tile = jnp.concatenate([padded] + up + [jnp.zeros((5, LANES), F32)], 0)
    high = tile.astype(BF16)
    low = tile - high.astype(F32)
    own[0:16, VEC0:PACKED] = high
    own[16:32, VEC0:PACKED] = low.astype(BF16)
    own[32:, VEC0:PACKED] = jnp.zeros((ROWS - 32, LANES), BF16)
    quarter[:, QUARTER:] = own[:, VEC0:PACKED]
    for place in range(4):

        @pl.when(replica == place)
        def _(place=place):
            quarter[:, :QUARTER] = own[:, place * QUARTER : (place + 1) * QUARTER]


def pack(*arrays):
    width = arrays[2].shape[2]
    return pl.pallas_call(
        pack_kernel,
        out_shape=[shape(dims, BF16) for dims in ((ROWS, PACKED), (ROWS, PIECE_IN))],
        in_specs=anywhere(13),
        out_specs=vmem(2),
        scratch_shapes=[
            pltpu.VMEM((4 * ROWS, width), BF16),
            pltpu.VMEM((8, ROWS), F32),
            pltpu.VMEM((1, 4 * ROWS), F32),
            pltpu.SemaphoreType.DMA((13,)),
        ],
        compiler_params=grant(60),
        name="pack",
    )(*arrays)


def after(value, *earlier):
    return lax.optimization_barrier((value,) + earlier)[0]


def reduce_plane(keep, send):
    half = (2,) + keep.shape[2:]
    to_x, to_y, own, x_late, y_late = small_call(
        pair_sum_kernel,
        [(2,) + half, (2,) + half, keep.shape[1:], half, half],
        "sum_of_cores",
        keep,
        swap(send),
    )
    return to_x, to_y, own, x_late, y_late


def near_kernel(first, third, near, upper, lower):
    near[0] = first[:, :QUARTER]
    near[1] = third[:, :QUARTER]
    upper[...] = first[:HALF]
    lower[...] = third[HALF:]


def far_kernel(first, third, upper, lower, far, tiles):
    far[:HALF] = upper[:, :QUARTER]
    far[HALF:] = lower[:, :QUARTER]
    tiles[0] = first[:, QUARTER:]
    tiles[1] = third[:, QUARTER:]
    tiles[2, :HALF] = upper[:, QUARTER:]
    tiles[2, HALF:] = lower[:, QUARTER:]


def relay(parts, got_x, got_y):
    _, _, own, x_late, y_late = parts
    half = x_late.shape
    (y_send,) = small_call(relay_kernel, [half], "relay", y_late, got_x)
    (x_send,) = small_call(relay_kernel, [half], "relay", x_late, got_y)
    return flip(y_send, 2), flip(x_send, 1)


def sum_column(parts):
    return small_call(column_sum_kernel, [parts.shape[1:]], "sum_of_column", parts)[0]


def spread(value):
    return [value] + [flip(value, bits) for bits in (1, 2, 3)]


def both_halves(pieces):
    return [member for piece in pieces for member in (piece, swap(piece))]


def rows_kernel(out_mine, out_other, grad_mine, grad_other, outs, grads):
    section = lax.axis_index("section")
    for slot in range(2):

        @pl.when(section == slot)
        def _(slot=slot):
            outs[:, slot, :] = out_mine[...].astype(F32).astype(BF16)
            outs[:, 1 - slot, :] = out_other[...]
            grads[:, slot, :] = grad_mine[...]
            grads[:, 1 - slot, :] = grad_other[...]


def rows_of_slots(out_mine, out_other, grad_mine, grad_other):
    seq, width = out_mine.shape
    outs, grads = pl.pallas_call(
        rows_kernel,
        out_shape=[shape((seq, 2, width), BF16), shape((seq, 2, width), F32)],
        in_specs=vmem(4),
        out_specs=vmem(2),
        compiler_params=grant(12),
        name="rows_of_slots",
    )(out_mine, out_other, grad_mine, grad_other)
    return outs, grads


def packed_local(patches, live_slots, cotangent, w_qkv, w_out, w_up, w_down, *small):
    width, wide = w_out.shape[2], w_up.shape[2]
    bias_q, bias_v, bias_out, bias_up, bias_down, gain_one, offset_one, gain_two, offset_two = small
    vectors = (bias_q, bias_v, bias_out, bias_down, gain_one, offset_one, gain_two, offset_two)
    own, quarter = pack(w_up, w_qkv, w_out, w_down, *vectors, bias_up)
    first, third = shift(quarter, 1), shift(quarter, 3)
    half = (HALF, PIECE_IN)
    near, upper, lower = small_call(
        near_kernel, [(2, ROWS, QUARTER), half, half], "near", first, third
    )
    x_near, y_near = flip(near, 1), flip(near, 2)
    far, tiles = small_call(
        far_kernel,
        [(ROWS, QUARTER), (3, ROWS, LANES)],
        "far",
        first,
        third,
        shift(upper, 1),
        shift(lower, 3),
    )
    far_now, x_now, y_now = lax.optimization_barrier((far, x_near, y_near))
    x_far, y_far, d_far = (flip(far_now, bits) for bits in (1, 2, 3))
    d_first, d_third = flip(y_now[0], 1), flip(x_now[1], 2)
    mine = [own, tiles, near, far, x_near, x_far, y_near, y_far, d_first, d_third, d_far]
    other = [swap(member) for member in mine]

    (out_mine, out_other, grad_one, keep1, near1, rest1, kept, vectors, *acts) = run_main(
        mine, other, patches, cotangent, live_slots, wide
    )
    whole, piece = keep1.shape[1:], keep1.shape[2:]
    to_x, to_y = small_call(near_sum_kernel, [whole] * 2, "sum_of_cores", keep1, swap(near1))
    got1 = (flip(to_x, 1), flip(to_y, 2))
    kept = after(kept, to_x, to_y)
    last = run_last(kept, vectors, grad_one, patches, acts, wide)
    grad_mine, grad_other, keep0, send0, recv1, *got1 = lax.optimization_barrier(
        (*last, swap(rest1), *got1)
    )
    (sums1,) = small_call(
        whole_plane_kernel, [(4, 2) + piece], "sum_of_plane", keep1, recv1, *got1
    )
    column1 = lax.all_to_all(sums1, "shard", 0, 0, tiled=True)
    parts0 = reduce_plane(after(keep0, sums1), send0)
    got0 = (flip(parts0[0], 1), flip(parts0[1], 2))
    rows = rows_of_slots(out_mine, swap(out_other), grad_mine, swap(grad_other))
    *got0, outs, grads = lax.optimization_barrier((*got0, *rows))
    layer_outputs, input_grads = outs.transpose(1, 0, 2)[None], grads.transpose(1, 0, 2)[None]
    late0 = relay(parts0, *got0)
    (sums0,) = small_call(
        plane_sum_kernel, [parts0[2].shape], "sum_of_plane", parts0[2], *got0, *late0
    )
    column0 = lax.all_to_all(sums0, "shard", 0, 0, tiled=True)
    (one,) = small_call(
        pair_column_kernel, [(2,) + piece], "sum_of_column", after(column1, sums0)
    )
    one = spread(one)
    column0 = after(column0, *one[1:])
    zero = spread(sum_column(column0))
    one = small_call(join_kernel, [piece] * 8, "join", *both_halves(one))
    grad_qkv, grad_out, grad_up, grad_down, *rest = unpack(
        both_halves(zero), one, width, wide
    )

    (g_q, g_v, g_o, g_d, g_g1, g_o1, g_g2, g_o2, g_up) = rest
    return (
        layer_outputs,
        input_grads,
        grad_qkv,
        grad_out,
        grad_up,
        grad_down,
        g_q,
        g_v,
        g_o,
        g_up,
        g_d,
        g_g1,
        g_o1,
        g_g2,
        g_o2,
    )


class PlainPut:
    def __init__(self, outs, layer):
        self.outs, self.layer = outs, layer

    def w_qkv(self, value):
        self.outs[0][self.layer] = value

    def w_out(self, value):
        self.outs[1][self.layer] = value

    def w_up(self, lo, value):
        self.outs[2][self.layer, :, lo : lo + value.shape[1]] = value

    def w_down(self, lo, value):
        self.outs[3][self.layer, lo : lo + value.shape[0]] = value

    def vectors(self, sums, bias_up):
        self.outs[4][self.layer] = sums
        self.outs[5][self.layer] = bias_up


def plain_kernel(seq, *refs):
    patches, cotangent, live, w_qkv, w_out, w_up, w_down, vectors, biases = refs[:9]
    out_rows, grad_rows = refs[9:11]
    grads = refs[11:17]
    rows_in, rows_mid, up_grad, qkv_grad = refs[17:21]
    acts = (refs[21:27], refs[27:33])
    section = lax.axis_index("section")
    width = rows_in.shape[1]

    def weights_of(layer):
        return (
            lambda: w_qkv[layer],
            lambda: w_out[layer],
            lambda lo, step: w_up[layer, :, lo : lo + step],
            lambda lo, step: w_down[layer, lo : lo + step],
        )

    vec_of = lambda layer: lambda index: vectors[layer, index : index + 1]
    bias_of = lambda layer: lambda lo, step: biases[layer, :, lo : lo + step]
    live_rows = lax.broadcasted_iota(jnp.int32, (SEQ_ROWS, width), 0) < seq
    rows_in[seq - seq % 8 :] = jnp.zeros((SEQ_ROWS - seq + seq % 8, width), F32)
    rows_in[:seq] = patches[section].astype(F32)
    result = layer_forward(rows_in[...], seq, weights_of(0), vec_of(0), bias_of(0), acts[0])
    out_rows[0] = result[:seq].astype(BF16)
    rows_mid[...] = jnp.where(live_rows, result.astype(BF16).astype(F32), 0.0)
    result = layer_forward(rows_mid[...], seq, weights_of(1), vec_of(1), bias_of(1), acts[1])
    out_rows[1] = result[:seq].astype(BF16)
    seed = cotangent[section].astype(F32) * live[section].astype(F32)
    blank = jnp.zeros((SEQ_ROWS - seq, width), F32)
    grad_x = layer_backward(
        jnp.concatenate([seed, blank], 0),
        rows_mid[...],
        weights_of(1),
        vec_of(1),
        acts[1],
        up_grad,
        qkv_grad,
        PlainPut(grads, 1),
    )
    grad_x = grad_x.astype(BF16).astype(F32)
    grad_rows[1] = grad_x[:seq]
    grad_x = layer_backward(
        grad_x,
        rows_in[...],
        weights_of(0),
        vec_of(0),
        acts[0],
        up_grad,
        qkv_grad,
        PlainPut(grads, 0),
    )
    grad_rows[0] = grad_x[:seq]


def plain_local(patches, live_slots, cotangent, w_qkv, w_out, w_up, w_down, *small):
    bias_q, bias_v, bias_out, bias_up, bias_down, gain_one, offset_one, gain_two, offset_two = small
    seq, width = patches.shape[1:]
    wide = w_up.shape[2]

    def whole(value):
        along = lax.all_gather(value, "shard", axis=1, tiled=True)
        return lax.all_gather(along, "section", axis=0, tiled=True)

    small = (bias_q, bias_v, bias_out, bias_down, gain_one, offset_one, gain_two, offset_two)
    vectors = whole(jnp.stack(small, 2)).transpose(0, 2, 1)
    biases = whole(bias_up)[:, None]
    acts = act_shapes(width, wide)
    out_rows, grad_rows, *grads = pl.pallas_call(
        functools.partial(plain_kernel, seq),
        out_shape=[
            shape((2, seq, width), BF16),
            shape((2, seq, width), F32),
            shape((2, width, 3 * width), F32),
            shape((2, width, width), F32),
            shape((2, width, wide), F32),
            shape((2, wide, width), F32),
            shape((2, 8, width), F32),
            shape((2, 1, wide), F32),
        ],
        in_specs=vmem(2) + [pl.BlockSpec(memory_space=pltpu.SMEM)] + vmem(6),
        out_specs=vmem(8),
        scratch_shapes=[
            pltpu.VMEM((SEQ_ROWS, width), F32),
            pltpu.VMEM((SEQ_ROWS, width), F32),
            pltpu.VMEM((SEQ_ROWS, wide), BF16),
            pltpu.VMEM((SEQ_ROWS, 3 * width), BF16),
        ]
        + [pltpu.VMEM(*a) for a in acts + acts],
        compiler_params=grant(56),
        name="both_layers",
    )(patches, cotangent, live_slots, *(whole(w) for w in (w_qkv, w_out, w_up, w_down)), vectors, biases)

    def owned(value):
        mine = lax.psum_scatter(value, "section", scatter_dimension=0, tiled=True)
        mine = lax.psum_scatter(mine.astype(BF16), "shard", scatter_dimension=1, tiled=True)
        return lax.psum(mine, "replica").astype(F32)

    grads = [owned(value) for value in grads[:4]] + [
        owned(grads[4].transpose(0, 2, 1)),
        owned(grads[5][:, 0]),
    ]
    q, v, out, down, g1, o1, g2, o2 = (grads[4][..., index] for index in range(8))

    def by_section(value):
        section = lax.axis_index("section")
        recv = swap(jnp.where(section == 0, value[1], value[0]))
        first = jnp.where(section == 0, value[0], recv)
        return jnp.stack([first, jnp.where(section == 0, recv, value[1])])[None]

    return (
        by_section(out_rows),
        by_section(grad_rows),
        *grads[:4],
        q,
        v,
        out,
        grads[5],
        down,
        g1,
        o1,
        g2,
        o2,
    )


def solution(mesh):
    slots = P(("shard", "replica"), None, None)
    matrix, vector = P("section", "shard", None), P("section", "shard")
    outs = P("section", ("shard", "replica"), None, None)
    packed = mesh.shape["shard"] == 4 and mesh.shape["replica"] == 4
    return jax.shard_map(
        packed_local if packed else plain_local,
        mesh=mesh,
        in_specs=(slots, P(("shard", "replica")), slots) + (matrix,) * 4 + (vector,) * 9,
        out_specs=(outs, outs) + (matrix,) * 4 + (vector,) * 9,
        check_vma=False,
    )
```
